32 devices in a mesh: dp: 8 (over z, y), seq: 4 (over x, core).
Axes of the slice: x: 2, y: 2, z: 4, core: 2. Of those that a mesh axis runs over, the one named last changes fastest.
Arguments:
- tokens: bfloat16 [16, 512, 768], P('dp', 'seq'), may hold values from -6 to 6
- segment_ids: int32 [16, 512], P('dp'), may hold values from 0 to 7, never falling along the last dimension, each value on 1 to 128 neighbouring positions
- padding: int32 [16, 512], P('dp'), may hold values 0 or 1
- w_qkv: bfloat16 [768, 2304], replicated, may hold values from -0.21875 to 0.21875
- b_query: float32 [768], replicated, may hold values from -3 to 3
- b_value: float32 [768], replicated, may hold values from -3 to 3
- w_out: bfloat16 [768, 768], replicated, may hold values from -0.625 to 0.625
- b_out: float32 [768], replicated, may hold values from -3 to 3
- ln1_gain: float32 [768], replicated, may hold values from 0.1 to 1.9
- ln1_bias: float32 [768], replicated, may hold values from -3 to 3
- w_in: bfloat16 [768, 3072], replicated, may hold values from -0.21875 to 0.21875
- b_in: float32 [3072], replicated, may hold values from -3 to 3
- w_back: bfloat16 [3072, 768], replicated, may hold values from -0.109375 to 0.109375
- b_back: float32 [768], replicated, may hold values from -3 to 3
- ln2_gain: float32 [768], replicated, may hold values from 0.1 to 1.9
- ln2_bias: float32 [768], replicated, may hold values from -3 to 3
- out_grad: bfloat16 [16, 512, 768], P('dp', 'seq'), may hold values from -6 to 6
Outputs:
- layer_output: bfloat16 [16, 512, 768], P('dp', 'seq')
- input_grad: bfloat16 [16, 512, 768], P('dp', 'seq')
- grad_w_qkv: float32 [768, 2304], P('dp', 'seq')
- grad_b_query: float32 [768], replicated
- grad_b_value: float32 [768], replicated
- grad_w_out: float32 [768, 768], P('dp', 'seq')
- grad_b_out: float32 [768], replicated
- grad_ln1_gain: float32 [768], replicated
- grad_ln1_bias: float32 [768], replicated
- grad_w_in: float32 [768, 3072], P('dp', 'seq')
- grad_b_in: float32 [3072], replicated
- grad_w_back: float32 [3072, 768], P('dp', 'seq')
- grad_b_back: float32 [768], replicated
- grad_ln2_gain: float32 [768], replicated
- grad_ln2_bias: float32 [768], replicated
The draws below stay inside these ranges and needn't reach their ends.
Inputs may be any that keep to these rules, and one draw needn't show every extreme that they name: `segment_ids`: along a row the ids never fall, and each id covers 1 to 128 consecutive tokens.
All inputs are finite; a program needn't handle non-finite values. No bound on the sum of `padding` on one device may be relied on, other than what follows from the above.
Results may differ from the reference program's by a relative error of at most 0.015.
Values may be sent and summed in bfloat16 or wider, within the bound.
No kernel may reach another device: no remote copies, remote signals or barrier semaphores. Data moves between devices by JAX's collectives and lax.ppermute only.
A program may use at most 128 MiB of HBM per device.

```python
import math
import jax
import jax.numpy as jnp
import numpy as np
from jax import lax

D = 768
HEADS = 12
HDIM = 64
FF = 3072
LEN = 512
PAIRS = 8
PAIR_MOST = 128
SEQ_DEV = 2
SEQS = 16


def with_ends(values, rng, low, top_value):
    longest = values.shape.index(max(values.shape))
    spots = []
    for shift in (0, 1):
        where = [jax.random.randint(jax.random.fold_in(rng, axis), (), 0, length) for axis, length in enumerate(values.shape)]
        where[longest] = (where[longest] + shift) % values.shape[longest]
        spots.append(tuple(where))
    return values.at[spots[0]].set(low).at[spots[1]].set(top_value)


def block_levels(stream_key, dims, split, smallest, largest):
    def one(axis_at, shards_of):
        heights = jax.random.uniform(jax.random.fold_in(jax.random.fold_in(stream_key, 6), axis_at), (shards_of,), jnp.float32, smallest / len(split), largest / len(split))
        return jnp.repeat(jnp.exp(heights), dims[axis_at] // shards_of).reshape((-1,) + (1,) * (len(dims) - axis_at - 1))

    factor_of = one(*split[0])
    for cut in split[1:]:
        factor_of = factor_of * one(*cut)
    return factor_of


def length_profile(amount, total, bound, lean):
    weights = [(1 << 20) // math.isqrt(rank ** lean) + 1 for rank in range(2, amount + 1)]
    rest, counts = total - bound - (amount - 1), [1] * (amount - 1)
    while rest > 0:
        movable = [i for i in range(amount - 1) if counts[i] < bound]
        mass, remaining = sum([weights[i] for i in movable]), rest
        for i in movable:
            extra = min(bound - counts[i], max(1, remaining * weights[i] // mass), rest)
            counts[i] = counts[i] + extra
            rest = rest - extra
    return np.array([bound] + counts)


def uneven_parts(key, number_of, total, most, skew):
    if number_of == 2:
        one = jax.random.randint(key, (), max(1, total - most), min(most, total - 1) + 1)
        return jnp.stack([one, total - one])
    sizes = jnp.asarray(length_profile(number_of, total, most, skew), jnp.int32)
    twos = (number_of - 1) // 2
    giver, sink = sizes[1:1 + 2 * twos:2], sizes[2:2 + 2 * twos:2]
    margin = jnp.minimum(giver - 1, most - sink)
    shifted = jax.random.randint(jax.random.fold_in(key, 1), (twos,), 0, 1 << 20) % (margin + 1)
    sizes = sizes.at[1:1 + 2 * twos:2].set(giver - shifted).at[2:2 + 2 * twos:2].set(sink + shifted)
    return sizes[jax.random.permutation(jax.random.fold_in(key, 2), number_of)]


def normal_values(stream_key, dims, width, bound, cuts=(), held_as=jnp.bfloat16):
    level = block_levels(stream_key, dims, cuts, -0.22, 0.18) if cuts else 1.0
    drawn = jax.random.normal(stream_key, dims, jnp.float32) * width * level
    return jnp.minimum(jnp.maximum(drawn, -bound), bound).astype(held_as)


def setup_inputs(seed: int = 0) -> dict:
    key_list = jax.random.split(jax.random.key(seed), 18)
    return {
        "tokens": normal_values(key_list[0], (SEQS, LEN, D), 1.0, 6.0, ((0, 8), (1, 4))),
        "segment_ids": jax.vmap(lambda own: jnp.searchsorted(jnp.cumsum(uneven_parts(own, PAIRS, LEN, PAIR_MOST, 0)), jnp.arange(LEN), side="right"))(jax.random.split(key_list[1], SEQS)).reshape((SEQS, LEN)).astype(jnp.int32),
        "padding": with_ends((jax.random.randint(key_list[2], (SEQS, LEN), 0, 8) < 1).astype(jnp.int32), jax.random.fold_in(key_list[2], 1), 0, 1),
        "w_qkv": normal_values(key_list[3], (D, 3 * D), D ** -0.5, 0.21875),
        "b_query": normal_values(key_list[4], (D,), 0.5, 3.0, (), jnp.float32),
        "b_value": normal_values(key_list[5], (D,), 0.5, 3.0, (), jnp.float32),
        "w_out": normal_values(key_list[6], (D, D), (D // 8) ** -0.5, 0.625),
        "b_out": normal_values(key_list[7], (D,), 0.5, 3.0, (), jnp.float32),
        "ln1_gain": jnp.clip(1.0 + 0.18 * jax.random.normal(key_list[8], (D,), jnp.float32), 0.1, 1.9),
        "ln1_bias": normal_values(key_list[9], (D,), 0.5, 3.0, (), jnp.float32),
        "w_in": normal_values(key_list[10], (D, FF), D ** -0.5, 0.21875),
        "b_in": normal_values(key_list[11], (FF,), 0.5, 3.0, (), jnp.float32),
        "w_back": normal_values(key_list[12], (FF, D), FF ** -0.5, 0.109375),
        "b_back": normal_values(key_list[13], (D,), 0.5, 3.0, (), jnp.float32),
        "ln2_gain": jnp.clip(1.0 + 0.18 * jax.random.normal(key_list[14], (D,), jnp.float32), 0.1, 1.9),
        "ln2_bias": normal_values(key_list[15], (D,), 0.5, 3.0, (), jnp.float32),
        "out_grad": normal_values(key_list[16], (SEQS, LEN, D), 1.0, 6.0, ((0, 8), (1, 4))),
    }


highest = lax.Precision.HIGHEST
ln_eps = 1e-12

@jax.custom_vjp
def low(v):
    return lax.optimization_barrier(v.astype(jnp.bfloat16)).astype(jnp.float32)

@jax.custom_vjp
def low_back(v):
    return v

def low_keep(v):
    return (low(v), None)

def low_pass(kept, grad):
    return (grad,)

def back_keep(v):
    return (v, None)

def back_low(kept, grad):
    return (low(grad),)
low.defvjp(low_keep, low_pass)
low_back.defvjp(back_keep, back_low)

def matmul(left, right):
    return jnp.dot(left, right, precision=highest, preferred_element_type=jnp.float32)

def layer_norm(values, gain_vec, shift_vec):
    center = values - lax.optimization_barrier(jnp.mean(values, axis=-1, keepdims=True))
    spread = lax.optimization_barrier(jnp.mean(center * center, axis=-1, keepdims=True))
    return center * lax.rsqrt(spread + ln_eps) * gain_vec + shift_vec

def attend_one(block_in):
    queries, key_rows, value_rows, seg_row, pad_row = block_in
    scores = jnp.einsum('qhd,khd->hqk', queries, key_rows, precision=highest) * HDIM ** (-0.5)
    scores = low_back(scores)
    places = jnp.arange(LEN)
    allowed = (seg_row[:, None] == seg_row[None, :]) & ((pad_row[None, :] == 0) | (places[:, None] == places[None, :]))
    scores = jnp.where(allowed[None, :, :], scores, -1000000000.0)
    row_top = lax.optimization_barrier(jnp.max(scores, axis=-1, keepdims=True))
    log_total = row_top + jnp.log(lax.optimization_barrier(jnp.sum(jnp.exp(scores - row_top), axis=-1, keepdims=True)))
    prob_rows = low(jnp.exp(scores - log_total))
    return jnp.einsum('hqk,khd->qhd', prob_rows, value_rows, precision=highest)

def layer(params, tokens, seg_ids, pad_flags):
    w_qkv, b_query, b_value, w_out, b_out, ln1_gain, ln1_bias, w_in, b_in, w_back, b_back, ln2_gain, ln2_bias = params
    seq_count = tokens.shape[0]
    bias_all = jnp.concatenate([b_query, jnp.zeros_like(b_query), b_value])
    projected = low(low_back(matmul(tokens, w_qkv) + bias_all))
    projected = projected.reshape(seq_count, LEN, 3, HEADS, HDIM)
    context = lax.map(jax.checkpoint(attend_one), (projected[:, :, 0], projected[:, :, 1], projected[:, :, 2], seg_ids, pad_flags))
    context = low(low_back(context.reshape(seq_count, LEN, D)))
    branch = low_back(matmul(context, w_out) + b_out)
    first_out = layer_norm(tokens + branch, ln1_gain, ln1_bias)
    before = low_back(matmul(low(first_out), w_in) + b_in)
    hidden = low(jax.nn.gelu(before, approximate=False))
    feed_out = low_back(matmul(hidden, w_back) + b_back)
    return layer_norm(first_out + feed_out, ln2_gain, ln2_bias)

def reference(tokens, segment_ids, padding, w_qkv, b_query, b_value, w_out, b_out, ln1_gain, ln1_bias, w_in, b_in, w_back, b_back, ln2_gain, ln2_bias, out_grad):
    params = tuple((entry_arg.astype(jnp.float32) for entry_arg in (w_qkv, b_query, b_value, w_out, b_out, ln1_gain, ln1_bias, w_in, b_in, w_back, b_back, ln2_gain, ln2_bias)))
    group_count = SEQS // SEQ_DEV
    inputs = tokens.astype(jnp.float32).reshape(group_count, SEQ_DEV, LEN, D)
    cotangent = out_grad.astype(jnp.float32).reshape(group_count, SEQ_DEV, LEN, D)
    seg_groups = segment_ids.astype(jnp.int32).reshape(group_count, SEQ_DEV, LEN)
    pad_groups = padding.astype(jnp.int32).reshape(group_count, SEQ_DEV, LEN)

    def group_step(totals, group_data):
        group_in, group_cot, group_seg, group_pad = group_data

        def forward(weight_set, values):
            return layer(weight_set, values, group_seg, group_pad)
        result, pull_back = jax.vjp(forward, params, group_in)
        weight_grads, grad_in = pull_back(group_cot)
        totals = jax.tree.map(jnp.add, totals, weight_grads)
        return (totals, (result.astype(jnp.bfloat16), grad_in.astype(jnp.bfloat16)))
    zero_init = jax.tree.map(jnp.zeros_like, params)
    totals, (outputs, grads_in) = lax.scan(group_step, zero_init, (inputs, cotangent, seg_groups, pad_groups))
    return (outputs.reshape(SEQS, LEN, D), grads_in.reshape(SEQS, LEN, D), totals[0], totals[1], totals[2], totals[3], totals[4], totals[5], totals[6], totals[7], totals[8], totals[9], totals[10], totals[11], totals[12])
```

```python
import jax
import jax.numpy as jnp
from jax import lax
from jax.sharding import PartitionSpec as P

HEADS = 12
HDIM = 64
LN_EPS = 1e-12
BOTH = ("dp", "seq")
BF = jnp.bfloat16
F32 = jnp.float32


def dot(a, b, ca=1, cb=0):
    return lax.dot_general(a, b, (((ca,), (cb,)), ((), ())), preferred_element_type=F32)


def norm_forward(values, gain_vec, shift_vec):
    center = values - jnp.mean(values, axis=-1, keepdims=True)
    inverse = lax.rsqrt(jnp.mean(center * center, axis=-1, keepdims=True) + LN_EPS)
    normed = center * inverse
    return normed * gain_vec + shift_vec, normed, inverse


def norm_backward(upstream, normed, inverse, gain_vec):
    scaled = upstream * gain_vec
    centred = (
        scaled
        - jnp.mean(scaled, axis=-1, keepdims=True)
        - normed * jnp.mean(scaled * normed, axis=-1, keepdims=True)
    )
    return centred * inverse, jnp.sum(upstream * normed, axis=0), jnp.sum(upstream, axis=0)


def flip(value, bit):
    count = lax.axis_size("dp") * lax.axis_size("seq")
    return lax.ppermute(value, BOTH, [(i, i ^ (1 << bit)) for i in range(count)])


def weight_grad(left, right, order, peer_left=None):
    seq, dp = lax.axis_size("seq"), lax.axis_size("dp")
    s, d = lax.axis_index("seq"), lax.axis_index("dp")
    core = s % 2
    tokens, cols = right.shape
    width = cols // seq
    right = right.reshape(tokens, seq // 2, 2, width)
    mine = lax.dynamic_index_in_dim(right, core, 2, keepdims=False)
    sent = lax.dynamic_index_in_dim(right, 1 - core, 2, keepdims=False)
    if peer_left is None:
        peer_left = flip(left, 0)
    both_left = jnp.concatenate([left, peer_left], axis=0)
    both_right = jnp.concatenate([mine, flip(sent, 0)], axis=0)
    part = jnp.einsum("tk,txw->xkw", both_left, both_right, preferred_element_type=F32)
    rows = left.shape[1] // dp
    dp_bits = dp.bit_length() - 1
    part = part.astype(BF).reshape((2,) * (1 + dp_bits) + (rows, width))
    dims = ["x"] + list(range(dp_bits))[::-1]
    for step, o in enumerate(order):
        axis = dims.index(o)
        bit = (s // 2) if o == "x" else (d >> o) & 1
        away = lax.dynamic_index_in_dim(part, 1 - bit, axis, keepdims=False)
        keep = lax.dynamic_index_in_dim(part, bit, axis, keepdims=False)
        got = flip(away, 1 if o == "x" else 2 + o)
        part = keep.astype(F32) + got.astype(F32)
        if step < len(order) - 1:
            part = part.astype(BF)
        dims.pop(axis)
    return part


def all_sum(value):
    count = lax.axis_size("dp") * lax.axis_size("seq")
    for bit in range(count.bit_length() - 1):
        value = value + flip(value, bit)
    return value


def local(
    tokens,
    segment_ids,
    padding,
    w_qkv,
    b_query,
    b_value,
    w_out,
    b_out,
    ln1_gain,
    ln1_bias,
    w_in,
    b_in,
    w_back,
    b_back,
    ln2_gain,
    ln2_bias,
    out_grad,
):
    seqs, loc, width = tokens.shape
    groups, dp = lax.axis_size("seq"), lax.axis_size("dp")
    dp_bits = dp.bit_length() - 1
    s = lax.axis_index("seq")
    up = [(i, i + 1) for i in range(groups - 1)]
    down = [(i + 1, i) for i in range(groups - 1)]

    def around(value):
        before = lax.ppermute(value, "seq", up)
        after = lax.ppermute(value, "seq", down)
        return jnp.concatenate([before, value, after], axis=1)

    rows = seqs * loc
    flat = tokens.reshape(rows, width)
    near = around(tokens)
    bias_all = jnp.concatenate([b_query, jnp.zeros_like(b_query), b_value])
    proj = (dot(near.reshape(3 * rows, width), w_qkv) + bias_all).astype(BF)
    proj = proj.reshape(seqs, 3 * loc, 3, HEADS, HDIM)
    queries, keys, values = proj[:, :, 0], proj[:, :, 1], proj[:, :, 2]
    own = slice(loc, 2 * loc)

    def window(v, low, high):
        v = jnp.concatenate(
            [jnp.full((seqs, loc), low, v.dtype), v, jnp.full((seqs, loc), high, v.dtype)], axis=1
        )
        return lax.dynamic_slice_in_dim(v, s * loc, 3 * loc, axis=1)

    seg = window(segment_ids, -1, -2)
    pad = window(padding, 1, 1)
    same = seg[:, own, None] == seg[:, None, :]
    diag = (lax.iota(jnp.int32, loc)[:, None] + loc) == lax.iota(jnp.int32, 3 * loc)[None, :]
    allowed = same & ((pad[:, None, :] == 0) | diag)
    allowed_t = same & ((pad[:, own, None] == 0) | diag)
    scale = HDIM**-0.5

    scores = jnp.einsum("bqhd,bkhd->bhqk", queries[:, own], keys, preferred_element_type=F32) * scale
    scores = jnp.where(allowed[:, None], scores, -1e9)
    top = jnp.max(scores, axis=-1, keepdims=True)
    log_total = top + jnp.log(jnp.sum(jnp.exp(scores - top), axis=-1, keepdims=True))
    probs = jnp.exp(scores - log_total)
    context = jnp.einsum(
        "bhqk,bkhd->bqhd", probs.astype(BF), values, preferred_element_type=F32
    ).astype(BF)
    context_flat = context.reshape(rows, width)

    branch = dot(context_flat, w_out) + b_out
    first, normed_one, inverse_one = norm_forward(flat.astype(F32) + branch, ln1_gain, ln1_bias)
    first_low = first.astype(BF)
    before = dot(first_low, w_in) + b_in
    cdf = 0.5 * (1.0 + lax.erf(before * (0.5**0.5)))
    hidden = (before * cdf).astype(BF)
    slope = cdf + before * jnp.exp(-0.5 * before * before) * ((2 * jnp.pi) ** -0.5)
    feed = dot(hidden, w_back) + b_back
    result, normed_two, inverse_two = norm_forward(first + feed, ln2_gain, ln2_bias)
    upstream = out_grad.reshape(rows, width).astype(F32)
    grad_two, gain_two, shift_two = norm_backward(upstream, normed_two, inverse_two, ln2_gain)
    feed_grad = grad_two.astype(BF)
    b_back_grad = jnp.sum(feed_grad.astype(F32), axis=0)
    g_back = weight_grad(hidden, feed_grad, ["x"] + list(range(dp_bits)))
    before_grad = (dot(feed_grad, w_back, 1, 1) * slope).astype(BF)
    b_in_grad = jnp.sum(before_grad.astype(F32), axis=0)
    g_in = weight_grad(first_low, before_grad, [0, "x"] + list(range(1, dp_bits)))
    first_grad = grad_two + dot(before_grad, w_in, 1, 1)
    grad_one, gain_one, shift_one = norm_backward(first_grad, normed_one, inverse_one, ln1_gain)
    branch_grad = grad_one.astype(BF)
    b_out_grad = jnp.sum(branch_grad.astype(F32), axis=0)
    g_out = weight_grad(context_flat, branch_grad, ["x"] + list(range(dp_bits)))
    context_grad = dot(branch_grad, w_out, 1, 1).astype(BF).reshape(seqs, loc, HEADS, HDIM)

    delta = jnp.sum(context_grad.astype(F32) * context.astype(F32), axis=-1)
    up_grad = around(context_grad)
    row_info = around(jnp.stack([log_total[..., 0].transpose(0, 2, 1), delta], axis=-1))
    log_all = row_info[..., 0].transpose(0, 2, 1)
    delta_all = row_info[..., 1].transpose(0, 2, 1)

    prob_grad = jnp.einsum("bqhd,bkhd->bhqk", context_grad, values, preferred_element_type=F32)
    score_grad = (probs * (prob_grad - delta.transpose(0, 2, 1)[..., None])).astype(BF)
    query_grad = jnp.einsum("bhqk,bkhd->bqhd", score_grad, keys, preferred_element_type=F32) * scale

    scores_t = jnp.einsum("bkhd,bqhd->bhkq", keys[:, own], queries, preferred_element_type=F32) * scale
    scores_t = jnp.where(allowed_t[:, None], scores_t, -1e9)
    probs_t = jnp.where(allowed_t[:, None], jnp.exp(scores_t - log_all[:, :, None, :]), 0.0)
    value_grad = jnp.einsum("bhkq,bqhd->bkhd", probs_t.astype(BF), up_grad, preferred_element_type=F32)
    prob_grad_t = jnp.einsum("bkhd,bqhd->bhkq", values[:, own], up_grad, preferred_element_type=F32)
    score_grad_t = (probs_t * (prob_grad_t - delta_all[:, :, None, :])).astype(BF)
    key_grad = jnp.einsum("bhkq,bqhd->bkhd", score_grad_t, queries, preferred_element_type=F32) * scale
    qkv_grad = jnp.stack([query_grad, key_grad, value_grad], axis=2).astype(BF)
    qkv_grad = qkv_grad.reshape(rows, 3 * width)
    peer = lax.dynamic_index_in_dim(near.reshape(seqs, 3, loc, width), 2 - 2 * (s % 2), 1, keepdims=False)
    g_qkv = weight_grad(flat, qkv_grad, [1, "x"] + [i for i in range(dp_bits) if i != 1], peer.reshape(rows, width))
    b_q_grad = jnp.sum(qkv_grad[:, :width].astype(F32), axis=0)
    b_v_grad = jnp.sum(qkv_grad[:, 2 * width :].astype(F32), axis=0)
    input_grad = grad_one + dot(qkv_grad, w_qkv, 1, 1)

    early = [b_out_grad, gain_one, shift_one, b_in_grad, b_back_grad, gain_two, shift_two]
    late = [b_q_grad, b_v_grad]

    def summed(items):
        total = all_sum(jnp.concatenate(items))
        out, at = [], 0
        for item in items:
            out.append(total[at : at + item.shape[0]])
            at += item.shape[0]
        return out

    e = summed(early)
    l = summed(late)
    shape = (seqs, loc, width)
    return (
        result.reshape(shape).astype(BF),
        input_grad.reshape(shape).astype(BF),
        g_qkv,
        l[0],
        l[1],
        g_out,
        e[0],
        e[1],
        e[2],
        g_in,
        e[3],
        g_back,
        e[4],
        e[5],
        e[6],
    )


def solution(mesh):
    row = P("dp", "seq", None)
    in_specs = (row, P("dp", None), P("dp", None)) + (P(),) * 13 + (row,)
    block = P("dp", "seq")
    out_specs = (row, row, block, P(), P(), block, P(), P(), P(), block, P(), block, P(), P(), P())
    return jax.shard_map(local, mesh=mesh, in_specs=in_specs, out_specs=out_specs, check_vma=False)
```

```python
import functools

import jax
import jax.numpy as jnp
from jax import lax
from jax.experimental import pallas as pl
from jax.experimental.pallas import tpu as pltpu
from jax.sharding import PartitionSpec as P

HEADS = 12
HDIM = 64
PAIR = 2 * HDIM
LN_EPS = 1e-12
FAR = -1e9
SUM_ROWS = 16
BOTH = ("dp", "seq")
BF = jnp.bfloat16
F32 = jnp.float32
HBM = pl.BlockSpec(memory_space=pltpu.HBM)
VMEM = pl.BlockSpec(memory_space=pltpu.VMEM)
SMEM = pl.BlockSpec(memory_space=pltpu.SMEM)


def dot(a, b, ca=1, cb=0):
    return lax.dot_general(a, b, (((ca,), (cb,)), ((), ())), preferred_element_type=F32)


def mean_of(v):
    return jnp.mean(v, axis=-1, keepdims=True)


def norm_parts(values):
    center = values - mean_of(values)
    inverse = lax.rsqrt(mean_of(center * center) + LN_EPS)
    return center * inverse, inverse


def norm_pull(upstream, normed, inverse, gain):
    scaled = upstream * gain
    return (scaled - mean_of(scaled) - normed * mean_of(scaled * normed)) * inverse


def col_sum(v):
    return jnp.sum(v, axis=0, keepdims=True)


def mask_of(me, groups, ids_ref, row, loc):
    own = pl.ds(pl.multiple_of(me * loc, loc), loc)
    seg_ref, pad_ref = ids_ref.at[0], ids_ref.at[1]
    seg_t = jnp.broadcast_to(seg_ref[row : row + 1, own].astype(F32), (loc, loc)).T
    pad_t = jnp.broadcast_to(pad_ref[row : row + 1, own].astype(F32), (loc, loc)).T
    eye = lax.broadcasted_iota(jnp.int32, (loc, loc), 0) == lax.broadcasted_iota(
        jnp.int32, (loc, loc), 1
    )
    keys, queries = [], []
    for block in range(3):
        at = me + block - 1
        out_of = jnp.where((at < 0) | (at >= groups), FAR, 0.0).astype(F32)
        at = jnp.clip(at, 0, groups - 1)
        span = pl.ds(pl.multiple_of(at * loc, loc), loc)
        seg_b = seg_ref[row : row + 1, span].astype(F32)
        pad_b = pad_ref[row : row + 1, span].astype(F32)
        same = seg_t == seg_b
        seen, seen_t = pad_b == 0.0, pad_t == 0.0
        if block == 1:
            seen, seen_t = seen | eye, seen_t | eye
        keys.append(jnp.where(same & seen, 0.0, FAR) + out_of)
        queries.append(jnp.where(same & seen_t, 0.0, FAR) + out_of)
    return jnp.concatenate(keys, axis=1), jnp.concatenate(queries, axis=1)


def split_pair(v, low):
    zero = jnp.zeros_like(v)
    return jnp.concatenate([jnp.where(low, v, zero), jnp.where(low, zero, v)], axis=0)


def join_pair(v, low):
    half = v.shape[0] // 2
    return jnp.where(low, v[:half], v[half:])


def own_kernel(
    groups, me_ref, ids_ref, tok_ref, vec_ref, wqkv, qkv_ref, mask_ref, mask_t_ref
):
    me = me_ref[0]
    rows, width = tok_ref.shape
    loc = rows // 2
    for row in range(2):
        mask_ref[row], mask_t_ref[row] = mask_of(me, groups, ids_ref, row, loc)
    vec = vec_ref[...].reshape(1, -1)
    biases = (vec[:, :width], 0.0, vec[:, width : 2 * width])
    for part in range(3):
        cols = slice(part * width, (part + 1) * width)
        qkv_ref[:, cols] = (dot(tok_ref[...], wqkv[:, cols]) + biases[part]).astype(BF)


def forward_kernel(
    groups,
    me_ref,
    tok_prev,
    tok_next,
    tok_own,
    own_ref,
    mask_ref,
    vec_ref,
    vec2_ref,
    b_in_ref,
    wqkv,
    og_hbm,
    wout_hbm,
    win_hbm,
    wback_hbm,
    qkv_ref,
    acts_ref,
    feed_ref,
    slope_ref,
    lse_ref,
    normed_ref,
    inv_ref,
    gtwo_ref,
    out_ref,
    keep_ref,
    small_ref,
    wout,
    win,
    wback,
    ctx_ref,
    og_ref,
    sems,
):
    me = me_ref[0]
    rows, width = tok_own.shape
    loc = rows // 2
    ff = win.shape[1]
    pairs = ((wout_hbm, wout), (win_hbm, win), (wback_hbm, wback), (og_hbm, og_ref))
    copies = [pltpu.make_async_copy(a, b, sems.at[i]) for i, (a, b) in enumerate(pairs)]
    for copy in copies:
        copy.start()
    vec, vec2 = vec_ref[...].reshape(1, -1), vec2_ref[...].reshape(1, -1)
    b_query, b_value, b_out, gain1 = (vec[:, i * width : (i + 1) * width] for i in range(4))
    shift1, b_back, gain2, shift2 = (vec2[:, i * width : (i + 1) * width] for i in range(4))
    b_in = b_in_ref[...].reshape(1, -1)
    b_qkv = (b_query, 0.0, b_value)
    for part in range(3):
        cols = slice(part * width, (part + 1) * width)
        for block, tok in enumerate((tok_prev, tok_next)):
            qkv_ref[block, :, cols] = (dot(tok[...], wqkv[:, cols]) + b_qkv[part]).astype(BF)
    blocks = (qkv_ref.at[0], own_ref, qkv_ref.at[1])
    low = lax.broadcasted_iota(jnp.int32, (loc, PAIR), 1) < HDIM
    lanes = lax.broadcasted_iota(jnp.int32, (loc, 128), 1)

    def attend(p, totals):
        spans = [pl.ds(pl.multiple_of(p * PAIR + part * width, PAIR), PAIR) for part in range(3)]
        result = []
        for row in range(2):
            at = slice(row * loc, (row + 1) * loc)
            q2 = split_pair(own_ref[at, spans[0]], low) * jnp.asarray(HDIM**-0.5, BF)
            k3 = jnp.concatenate([b[at, spans[1]] for b in blocks], axis=0)
            v3 = jnp.concatenate([b[at, spans[2]] for b in blocks], axis=0)
            mask = mask_ref[row]
            scores = dot(q2, k3, 1, 1) + jnp.concatenate([mask, mask], axis=0)
            top = jnp.max(scores, axis=-1, keepdims=True)
            powers = jnp.exp(scores - top)
            total = jnp.sum(powers, axis=-1, keepdims=True)
            probs = (powers * (1.0 / total)).astype(BF)
            ctx_ref[at, pl.ds(pl.multiple_of(p * PAIR, PAIR), PAIR)] = join_pair(
                dot(probs, v3), low
            ).astype(BF)
            lse = top + jnp.log(total)
            old = totals[row]
            old = jnp.where(lanes == 2 * p, lse[:loc], old)
            result.append(jnp.where(lanes == 2 * p + 1, lse[loc:], old))
        return tuple(result)

    zero = jnp.zeros((loc, 128), F32)
    totals = lax.fori_loop(0, HEADS // 2, attend, (zero, zero))
    lse_ref[:loc, :] = totals[0]
    lse_ref[loc:, :] = totals[1]
    context = ctx_ref[...]
    acts_ref[:, ff + width : ff + 2 * width] = context
    copies[0].wait()
    branch = dot(context, wout[...]) + b_out
    normed, inverse = norm_parts(tok_own[...].astype(F32) + branch)
    normed_ref[...] = normed
    inv_ref[...] = inverse
    first = normed * gain1 + shift1
    first_low = first.astype(BF)
    acts_ref[:, ff : ff + width] = first_low
    copies[1].wait()
    copies[2].wait()
    feed = first + b_back
    for c in range(ff // width):
        cols = slice(c * width, (c + 1) * width)
        before = dot(first_low, win[:, cols]) + b_in[:, cols]
        cdf = 0.5 + 0.5 * lax.erf(before * (0.5**0.5))
        hidden = (before * cdf).astype(BF)
        acts_ref[:, cols] = hidden
        bell = jnp.exp(-0.5 * before * before) * (0.3989422804014327)
        slope_ref[:, cols] = (cdf + before * bell).astype(BF)
        feed = feed + dot(hidden, wback[cols, :])
    normed2, inverse2 = norm_parts(feed)
    out_ref[...] = (normed2 * gain2 + shift2).astype(BF)
    copies[3].wait()
    upstream = og_ref[...].astype(F32)
    grad_two = norm_pull(upstream, normed2, inverse2, gain2)
    gtwo_ref[...] = grad_two
    feed_grad = grad_two.astype(BF)
    feed_ref[...] = feed_grad
    small_ref[0:1, :] = col_sum(feed_grad.astype(F32))
    small_ref[1:2, :] = col_sum(upstream * normed2)
    small_ref[2:3, :] = col_sum(upstream)
    base = ff + 2 * width
    block = width // groups
    for s in range(groups):
        rel = s ^ me
        piece = feed_grad[:, s * block : (s + 1) * block]
        for i in range(groups // 2):

            @pl.when(rel == 2 * i)
            def _():
                keep_ref[:, i * block : (i + 1) * block] = piece

            @pl.when(rel == 2 * i + 1)
            def _():
                acts_ref[:, base + i * block : base + (i + 1) * block] = piece


def backward_kernel(
    groups,
    me_ref,
    feed_ref,
    slope_ref,
    gtwo_ref,
    normed_ref,
    inv_ref,
    acts_ref,
    lse_ref,
    vec_ref,
    wback_hbm,
    win_hbm,
    wout_hbm,
    keep_ref,
    send_ref,
    msg_ref,
    gone_ref,
    small_ref,
    wback,
    win,
    wout,
    sems,
):
    me = me_ref[0]
    rows, width = feed_ref.shape
    ff = win.shape[1]
    block = ff // groups
    spans = [pl.ds(pl.multiple_of((i ^ me) * block, block), block) for i in range(groups)]
    copies = []
    for i, span in enumerate(spans):
        copies += [
            pltpu.make_async_copy(wback_hbm.at[span], wback.at[span], sems.at[2 * i]),
            pltpu.make_async_copy(win_hbm.at[:, span], win.at[:, span], sems.at[2 * i + 1]),
        ]
    copies += [
        pltpu.make_async_copy(wout_hbm, wout, sems.at[2 * groups]),
    ]
    for copy in copies:
        copy.start()
    feed_grad = feed_ref[...]
    first_grad = gtwo_ref[...]
    for i, span in enumerate(spans):
        s = i ^ me
        copies[2 * i].wait()
        copies[2 * i + 1].wait()
        hidden_grad = dot(feed_grad, wback[span, :], 1, 1)
        before_grad = (hidden_grad * slope_ref[:, span].astype(F32)).astype(BF)
        small_ref[pl.ds(s, 1), :] = col_sum(before_grad.astype(F32))
        target = send_ref if i % 2 else keep_ref
        target[:, (i // 2) * block : (i // 2 + 1) * block] = before_grad
        first_grad = first_grad + dot(before_grad, win[:, span], 1, 1)
    copies[-1].wait()
    normed = normed_ref[...]
    grad_one = norm_pull(first_grad, normed, inv_ref[...], vec_ref[3 * width :].reshape(1, -1))
    gone_ref[...] = grad_one
    branch_grad = grad_one.astype(BF)
    small_ref[4:5, :] = col_sum(branch_grad.astype(F32))
    small_ref[5:6, :] = col_sum(first_grad * normed)
    small_ref[6:7, :] = col_sum(first_grad)
    context_grad = dot(branch_grad, wout[...], 1, 1).astype(BF)
    msg_ref[:, :width] = context_grad
    product = context_grad.astype(F32) * acts_ref[:, ff + width : ff + 2 * width].astype(F32)
    lanes = lax.broadcasted_iota(jnp.int32, (rows, 128), 1)
    low = lanes < HDIM
    delta = jnp.zeros((rows, 128), F32)
    for p in range(HEADS // 2):
        tile = product[:, p * PAIR : (p + 1) * PAIR]
        both = jnp.sum(tile, axis=-1, keepdims=True)
        even = jnp.sum(jnp.where(low, tile, 0.0), axis=-1, keepdims=True)
        delta = jnp.where(lanes == 2 * p, even, delta)
        delta = jnp.where(lanes == 2 * p + 1, both - even, delta)
    packed = jnp.zeros((rows, 128), F32)
    shift = 0
    for value in (lse_ref[...], delta):
        for _ in range(3):
            term = value.astype(BF).astype(F32)
            packed = packed + (pltpu.roll(term, shift, 1) if shift else term)
            value = value - term
            shift += 16
    msg_ref[:, width:] = packed.astype(BF)
    base = 2 * block
    small = width // groups
    for s in range(groups):
        rel = s ^ me
        piece = branch_grad[:, s * small : (s + 1) * small]
        for i in range(groups // 2):

            @pl.when(rel == 2 * i)
            def _():
                keep_ref[:, base + i * small : base + (i + 1) * small] = piece

            @pl.when(rel == 2 * i + 1)
            def _():
                send_ref[:, base + i * small : base + (i + 1) * small] = piece


def attend_back_kernel(
    groups,
    me_ref,
    mask_ref,
    mask_t_ref,
    near_ref,
    own_ref,
    msg_prev,
    msg_own,
    msg_next,
    small1_ref,
    small2_ref,
    all_ref,
    keep_ref,
    send_ref,
    send2_ref,
    sums_ref,
    info_t_ref,
):
    me = me_ref[0]
    rows = msg_own.shape[0]
    width = own_ref.shape[1] // 3
    loc = rows // 2
    msgs = (msg_prev, msg_own, msg_next)
    blocks = (near_ref.at[0], own_ref, near_ref.at[1])
    own_info = []
    for row in range(2):
        at = slice(row * loc, (row + 1) * loc)
        for b in range(3):
            raw = msgs[b][at, width:].astype(F32)
            info = raw + pltpu.roll(raw, 112, 1) + pltpu.roll(raw, 96, 1)
            if b == 1:
                own_info.append(info)
            info_t_ref[row, b] = info.T
    low = lax.broadcasted_iota(jnp.int32, (loc, PAIR), 1) < HDIM
    lanes = lax.broadcasted_iota(jnp.int32, (loc, 128), 1)
    scale = jnp.asarray(HDIM**-0.5, BF)

    def column(info, lane):
        return jnp.sum(jnp.where(lanes == lane, info, 0.0), axis=-1, keepdims=True)

    def heads(p, carry):
        spans = [pl.ds(pl.multiple_of(p * PAIR + part * width, PAIR), PAIR) for part in range(3)]
        for row in range(2):
            at = slice(row * loc, (row + 1) * loc)
            info = own_info[row]
            lse2 = jnp.concatenate([column(info, 2 * p), column(info, 2 * p + 1)], axis=0)
            delta2 = jnp.concatenate([column(info, 48 + 2 * p), column(info, 49 + 2 * p)], axis=0)
            q3 = jnp.concatenate([b[at, spans[0]] for b in blocks], axis=0)
            k3 = jnp.concatenate([b[at, spans[1]] for b in blocks], axis=0)
            v3 = jnp.concatenate([b[at, spans[2]] for b in blocks], axis=0)
            u3 = jnp.concatenate([m[at, spans[0]] for m in msgs], axis=0)
            mask = mask_ref[row]
            scores = dot(split_pair(q3[loc : 2 * loc], low) * scale, k3, 1, 1)
            probs = jnp.exp(scores + jnp.concatenate([mask, mask], axis=0) - lse2)
            prob_grad = dot(split_pair(u3[loc : 2 * loc], low), v3, 1, 1)
            score_grad = (probs * (prob_grad - delta2)).astype(BF)
            query_grad = join_pair(dot(score_grad, k3), low) * HDIM**-0.5
            all_ref[at, spans[0]] = query_grad.astype(BF)

            def line(which):
                halves = []
                for h in range(2):
                    parts = [info_t_ref[row, b, pl.ds(which + 2 * p + h, 1), :] for b in range(3)]
                    halves.append(
                        jnp.broadcast_to(jnp.concatenate(parts, axis=1), (loc, 3 * loc))
                    )
                return jnp.concatenate(halves, axis=0)

            mask_t = mask_t_ref[row]
            scores_t = dot(split_pair(k3[loc : 2 * loc], low) * scale, q3, 1, 1)
            probs_t = jnp.exp(scores_t + jnp.concatenate([mask_t, mask_t], axis=0) - line(0))
            value_grad = join_pair(dot(probs_t.astype(BF), u3), low)
            prob_grad_t = dot(split_pair(v3[loc : 2 * loc], low), u3, 1, 1)
            score_grad_t = (probs_t * (prob_grad_t - line(48))).astype(BF)
            key_grad = join_pair(dot(score_grad_t, q3), low) * HDIM**-0.5
            all_ref[at, spans[1]] = key_grad.astype(BF)
            all_ref[at, spans[2]] = value_grad.astype(BF)
        return carry

    lax.fori_loop(0, HEADS // 2, heads, 0)
    value_at = 2 * width
    sums_ref[...] = jnp.concatenate(
        [
            small1_ref[...],
            small2_ref[...],
            col_sum(all_ref[:, :width].astype(F32)),
            col_sum(all_ref[:, value_at:].astype(F32)),
            jnp.zeros((SUM_ROWS - 12, width), F32),
        ],
        axis=0,
    )
    send_ref[loc:, :] = jnp.zeros((2 * SUM_ROWS, send_ref.shape[1]), BF)
    pack_sums(sums_ref[...], send_ref, loc)
    block = 3 * width // groups
    for s in range(groups):
        rel = s ^ me
        piece = all_ref[:, s * block : (s + 1) * block]
        for i in range(groups // 2):

            @pl.when(rel == 2 * i)
            def _():
                keep_ref[:, i * block : (i + 1) * block] = piece

            @pl.when(rel == 2 * i + 1)
            def _():
                send_ref[:loc, i * block : (i + 1) * block] = piece[:loc]
                send2_ref[:, i * block : (i + 1) * block] = piece[loc:]


def pack_sums(value, ref, at):
    high = value.astype(BF)
    ref[at : at + SUM_ROWS, : value.shape[1]] = high
    ref[at + SUM_ROWS : at + 2 * SUM_ROWS, : value.shape[1]] = (value - high.astype(F32)).astype(BF)


def read_sums(ref, at, width):
    high = ref[at : at + SUM_ROWS, :width].astype(F32)
    return high + ref[at + SUM_ROWS : at + 2 * SUM_ROWS, :width].astype(F32)


def turn_rows(d, dp, tmp_ref, turned_ref, block_rows, part):
    rows = block_rows // 2
    for j, rel in enumerate(low_first(dp)):
        start = pl.multiple_of((rel ^ d) * block_rows + part * rows, rows)
        turned_ref[j * rows : (j + 1) * rows, :] = tmp_ref[pl.ds(start, rows), :]


def low_first(dp):
    bits = dp.bit_length() - 1
    return [sum(((j >> (bits - 1 - k)) & 1) << k for k in range(bits)) for j in range(dp)]


def both_left(mine, peer):
    return jnp.concatenate([mine.T, peer.T], axis=1)


def by_halves(pieces, base, width):
    return [
        jnp.concatenate([r[:, base + x * width : base + (x + 1) * width] for r in pieces], axis=0)
        for x in range(2)
    ]


def put(result, part, x, keeps, sends):
    total = result.shape[0]
    half = total // 2
    if part == 0:
        (sends if x else keeps)[0][:total] = result
    else:
        keeps[1][x * half : (x + 1) * half] = result[:half]
        sends[1][x * half : (x + 1) * half] = result[half:]


def in_kernel(dp, d_ref, acts, acts_peer, mine, peer, keep0, send0, keep1, send1, tmp, *turned):
    width = acts.shape[1]
    tmp[...] = both_left(acts[...], acts_peer[...])
    wide = (mine.shape[1] - width // 2) // 2
    rights = by_halves((mine, peer), 0, wide)
    for part in range(2):
        turn_rows(d_ref[0], dp, tmp, turned[part], width // dp, part)
        for x in range(2):
            result = dot(turned[part][...], rights[x]).astype(BF)
            put(result, part, x, (keep0, keep1), (send0, send1))


def qkv_kernel(
    dp,
    ids_ref,
    tok,
    tok_prev,
    tok_next,
    ctx,
    ctx_peer,
    mine,
    peer,
    peer2,
    out_mine,
    out_peer,
    sums_ref,
    keep0,
    send0,
    keep1,
    send1,
    total_ref,
    tmp,
    tmp2,
    *turned,
):
    rows, width = tok.shape
    d = ids_ref[0]
    other = jnp.where(ids_ref[1] % 2 == 0, tok_next[...], tok_prev[...])
    tmp[...] = both_left(tok[...], other)
    tmp2[...] = both_left(ctx[...], ctx_peer[...])
    half = peer2.shape[0]
    rights = by_halves((mine, peer.at[:half], peer2), 0, mine.shape[1] // 2)
    outs = by_halves((out_mine, out_peer), 0, out_mine.shape[1] // 2)
    for part in range(2):
        turn_rows(d, dp, tmp, turned[part], width // dp, part)
        turn_rows(d, dp, tmp2, turned[2 + part], width // dp, part)
        for x in range(2):
            result = jnp.concatenate(
                [dot(turned[part][...], rights[x]), dot(turned[2 + part][...], outs[x])], axis=1
            ).astype(BF)
            put(result, part, x, (keep0, keep1), (send0, send1))
    total = sums_ref[...] + read_sums(peer, half, width)
    total_ref[...] = total
    pack_sums(total, send0, keep0.shape[0])


def back_kernel(dp, d_ref, hid, hid_peer, feed, feed_peer, keep0, send0, keep1, send1):
    d = d_ref[0]
    chunk = hid.shape[1] // dp
    side = feed.shape[1] // 2
    rows = side // 4
    turned = [feed[...].T, feed_peer[...].T]
    first, second, *rest = HALVING["back"]
    orders = [(first, second, *rest), (second, first, *rest)]
    for rel in range(dp):
        span = pl.ds(pl.multiple_of((rel ^ d) * chunk, chunk), chunk)
        result = (dot(turned[0], hid[:, span]) + dot(turned[1], hid_peer[:, span])).astype(BF)
        for x in range(2):
            bits = 2 * x + 4 * rel
            for part, refs in enumerate(((keep0, send0), (keep1, send1))):
                at = 0
                for bit in orders[part]:
                    at = 2 * at + ((bits >> bit) & 1)
                ref, at = refs[at // dp], at % dp
                for h in range(2):
                    start = x * side + h * 2 * rows + part * rows
                    ref[at * rows : (at + 1) * rows, h * chunk : (h + 1) * chunk] = result[
                        start : start + rows
                    ]


def total_of(keep, got):
    return keep[...].astype(F32) + got[: keep.shape[0]].astype(F32)


def step_sums(sums_ref, got, at, total_ref, send, send_at):
    total = sums_ref[...] + read_sums(got, at, sums_ref.shape[1])
    total_ref[...] = total
    if send is not None:
        pack_sums(total, send, send_at)


def first_step(keep0, got0, keep1, got1, *refs):
    if len(refs) == 6:
        sums_ref, new0, send0, new1, send1, total_ref = refs
        step_sums(sums_ref, got0, keep0.shape[0], total_ref, send0, keep0.shape[0] // 2)
    else:
        new0, send0, new1, send1 = refs
    half = keep0.shape[0] // 2
    for keep, got, new, send in ((keep0, got0, new0, send0), (keep1, got1, new1, send1)):
        total = total_of(keep, got).astype(BF)
        new[...] = total[:half]
        send[:half] = total[half:]


def second_step(rows, keep0, got0, keep1, got1, *refs):
    if len(refs) == 4:
        sums_ref, new, send, total_ref = refs
        step_sums(sums_ref, got0, keep0.shape[0], total_ref, send, new.shape[0])
    else:
        new, send = refs
    half = keep0.shape[0] // 2
    for part, (keep, got) in enumerate(((keep0, got0), (keep1, got1))):
        total = total_of(keep, got).astype(BF)
        for b in range(half // rows):
            at = (2 * b + part) * rows
            new[at : at + rows] = total[b * rows : (b + 1) * rows]
            send[at : at + rows] = total[half + b * rows : half + (b + 1) * rows]


def third_step(keep, got, *refs):
    if len(refs) == 4:
        sums_ref, new, send, total_ref = refs
        step_sums(sums_ref, got, keep.shape[0], total_ref, send, new.shape[0])
    else:
        new, send = refs
    half = keep.shape[0] // 2
    total = total_of(keep, got).astype(BF)
    new[...] = total[:half]
    send[:half] = total[half:]


def last_step(kind, keep, got, *refs):
    total = total_of(keep, got)
    if kind == "back":
        chunk = total.shape[1] // 2
        refs[0][...] = jnp.concatenate([total[:, :chunk].T, total[:, chunk:].T], axis=1)
    elif kind == "in":
        refs[0][...] = total
    else:
        sums_ref, qkv_ref, out_ref, total_ref = refs
        qkv_ref[...] = total[:, : qkv_ref.shape[1]]
        out_ref[...] = total[:, qkv_ref.shape[1] :]
        step_sums(sums_ref, got, keep.shape[0], total_ref, None, 0)


HALVING = {"back": (2, 3, 1, 4), "in": (1, 2, 3, 4), "qkv": (1, 2, 3, 4)}


def flip(value, bit):
    count = lax.axis_size("dp") * lax.axis_size("seq")
    return lax.ppermute(value, BOTH, [(i, i ^ (1 << bit)) for i in range(count)])


class Reduction:
    def __init__(self, kind, parts, sums=None):
        self.kind, self.keeps, self.sums = kind, parts[0::2], sums
        self.at, self.result = 0, None
        self.gots = tuple(flip(v, b) for v, b in zip(parts[1::2], HALVING[kind]))

    def step(self, outs):
        extra = 0 if self.sums is None else 2 * SUM_ROWS
        total = self.keeps[0].shape[0]
        width = self.keeps[0].shape[1]
        half = total // 2
        operands = [v for pair in zip(self.keeps, self.gots) for v in pair]
        sums = () if self.sums is None else (shape_of(SUM_ROWS, width, dtype=F32),)
        if self.at == 0:
            kernel = first_step
            shapes = (half, half + extra, half, half)
        elif self.at == 1:
            kernel = functools.partial(second_step, outs["rows"])
            shapes = (total, total + extra)
        else:
            kernel, shapes = third_step, (half, half + extra)
        shapes = tuple(shape_of(n, width) for n in shapes) + sums
        last = self.at > 1 and "last" in outs
        if last:
            kernel = functools.partial(last_step, self.kind)
            shapes = tuple(shape_of(*dims, dtype=F32) for dims in outs["last"]) + sums
        if self.sums is not None:
            operands.append(self.sums)
        result = pl.pallas_call(
            kernel,
            name=f"add_{self.kind}_{self.at}",
            cost_estimate=cost(1),
            out_shape=shapes,
            in_specs=[VMEM] * len(operands),
            out_specs=(VMEM,) * len(shapes),
            compiler_params=params(12),
        )(*operands)
        if self.sums is not None:
            self.sums = result[-1]
        self.at += 1
        if last:
            self.result = result
            return
        self.keeps = result[0 : len(shapes) - len(sums) : 2]
        sends = result[1 : len(shapes) - len(sums) : 2]
        bits = HALVING[self.kind]
        bits = bits[1::-1] if self.at == 1 else bits[self.at :]
        self.gots = tuple(flip(v, b) for v, b in zip(sends, bits))


def wait_for(unit, done):
    got, *rest = unit.gots
    if done.result is None:
        keep, *others = done.keeps
        got, keep = lax.optimization_barrier((got, keep))
        done.keeps = (keep, *others)
    else:
        first, *others = done.result
        got, first = lax.optimization_barrier((got, first))
        done.result = (first, *others)
    unit.gots = (got, *rest)


def plain_reduce(left, right):
    dp = lax.axis_size("dp")
    part = jnp.einsum("tk,xtw->xkw", left, right, preferred_element_type=F32).astype(BF)
    part = part[0].astype(F32) + flip(part[1], 1).astype(F32)
    part = part.reshape(dp, left.shape[1] // dp, right.shape[2]).astype(BF)
    part = jnp.take(part, jnp.arange(dp) ^ lax.axis_index("dp"), axis=0)
    for bit in reversed(range(dp.bit_length() - 1)):
        half = part.shape[0] // 2
        part = part[:half].astype(F32) + flip(part[half:], 2 + bit).astype(F32)
        part = part.astype(BF) if bit else part
    return part[0]


def plain_sum(value, low):
    count = lax.axis_size("dp") * lax.axis_size("seq")
    for bit in range(low, count.bit_length() - 1):
        value = value + flip(value, bit)
    return value


def shape_of(*dims, dtype=BF):
    return jax.ShapeDtypeStruct(dims, dtype)


def cost(us):
    return pl.CostEstimate(flops=int(us * 1e6), bytes_accessed=int(us * 1e4), transcendentals=0)


def params(mib):
    return pltpu.CompilerParams(vmem_limit_bytes=mib << 20)


def local(
    tokens,
    segment_ids,
    padding,
    w_qkv,
    b_query,
    b_value,
    w_out,
    b_out,
    ln1_gain,
    ln1_bias,
    w_in,
    b_in,
    w_back,
    b_back,
    ln2_gain,
    ln2_bias,
    out_grad,
):
    seqs, loc, width = tokens.shape
    groups, dp = lax.axis_size("seq"), lax.axis_size("dp")
    dp_bits = dp.bit_length() - 1
    ff = w_in.shape[1]
    rows = seqs * loc
    me = lax.axis_index("seq").astype(jnp.int32).reshape(1)
    d = lax.axis_index("dp").astype(jnp.int32).reshape(1)
    up = [(i, i + 1) for i in range(groups - 1)]
    down = [(i + 1, i) for i in range(groups - 1)]

    def around(value):
        return lax.ppermute(value, "seq", up), lax.ppermute(value, "seq", down)

    flat = tokens.reshape(rows, width)
    tok_prev, tok_next = around(flat)
    vec1 = jnp.concatenate([b_query, b_value, b_out, ln1_gain])
    vec2 = jnp.concatenate([ln1_bias, b_back, ln2_gain, ln2_bias])
    ids = jnp.stack([segment_ids, padding])
    own_qkv, mask, mask_t = pl.pallas_call(
        functools.partial(own_kernel, groups),
        name="own_projections",
        cost_estimate=cost(4),
        out_shape=(
            shape_of(rows, 3 * width),
            shape_of(seqs, loc, 3 * loc, dtype=F32),
            shape_of(seqs, loc, 3 * loc, dtype=F32),
        ),
        in_specs=[SMEM] + [VMEM] * 4,
        out_specs=(VMEM,) * 3,
        compiler_params=params(50),
    )(me, ids, flat, vec1, w_qkv)
    extra = width // groups * 2
    acts_width = ff + 2 * width + extra
    near_qkv, acts, feed_grad, slope, lse, normed, inverse, grad_two, result, feed_keep, small1 = (
        pl.pallas_call(
            functools.partial(forward_kernel, groups),
            name="layer_forward",
            cost_estimate=cost(16),
            out_shape=(
                shape_of(2, rows, 3 * width),
                shape_of(rows, acts_width),
                shape_of(rows, width),
                shape_of(rows, ff),
                shape_of(rows, 128, dtype=F32),
                shape_of(rows, width, dtype=F32),
                shape_of(rows, 1, dtype=F32),
                shape_of(rows, width, dtype=F32),
                shape_of(rows, width),
                shape_of(rows, extra),
                shape_of(3, width, dtype=F32),
            ),
            in_specs=[SMEM] + [VMEM] * 9 + [HBM] * 4,
            out_specs=(VMEM,) * 11,
            scratch_shapes=[
                pltpu.VMEM((width, width), BF),
                pltpu.VMEM((width, ff), BF),
                pltpu.VMEM((ff, width), BF),
                pltpu.VMEM((rows, width), BF),
                pltpu.VMEM((rows, width), BF),
                pltpu.SemaphoreType.DMA((4,)),
            ],
            compiler_params=params(46),
        )(
            me,
            tok_prev,
            tok_next,
            flat,
            own_qkv,
            mask,
            vec1,
            vec2,
            b_in,
            w_qkv,
            out_grad.reshape(rows, width),
            w_out,
            w_in,
            w_back,
        )
    )
    acts_peer = flip(acts, 0)

    side = 2 * (ff // groups) + extra
    grads_keep, grads_send, msg, grad_one, small2 = pl.pallas_call(
        functools.partial(backward_kernel, groups),
        name="layer_backward",
            cost_estimate=cost(8),
        out_shape=(
            shape_of(rows, side),
            shape_of(rows, side),
            shape_of(rows, width + 128),
            shape_of(rows, width, dtype=F32),
            shape_of(7, width, dtype=F32),
        ),
        in_specs=[SMEM] + [VMEM] * 8 + [HBM] * 3,
        out_specs=(VMEM,) * 5,
        scratch_shapes=[
            pltpu.VMEM((ff, width), BF),
            pltpu.VMEM((width, ff), BF),
            pltpu.VMEM((width, width), BF),
            pltpu.SemaphoreType.DMA((2 * groups + 1,)),
        ],
        compiler_params=params(44),
    )(me, feed_grad, slope, grad_two, normed, inverse, acts, lse, vec1, w_back, w_in, w_out)
    msg_prev, msg_next = around(msg)
    grads_peer = flip(grads_send, 0)

    kernels = (width // dp) % 32 == 0 and (ff // dp) % 128 == 0 and dp == 8
    small = width // groups
    wide = ff // groups
    qkv_block = 3 * width // groups
    block_rows = width // dp
    part_rows = dp * block_rows // 2
    base = ff + 2 * width

    def acts_block(i):
        return pl.BlockSpec((rows, width), lambda g: (0, i))

    first_at, ctx_at = ff // width, ff // width + 1
    out_at = 2 * wide // extra
    if kernels:
        back = pl.pallas_call(
            functools.partial(back_kernel, dp),
            name="grad_w_back",
            cost_estimate=cost(3),
            grid=(1,),
            out_shape=(shape_of(part_rows, width),) * 4,
            in_specs=[
                SMEM,
                pl.BlockSpec((rows, ff), lambda i: (0, 0)),
                pl.BlockSpec((rows, ff), lambda i: (0, 0)),
                pl.BlockSpec((rows, extra), lambda i: (0, 0)),
                pl.BlockSpec((rows, extra), lambda i: (0, base // extra)),
            ],
            compiler_params=params(16),
        )(d, acts, acts_peer, feed_keep, acts_peer)
        whole = pl.BlockSpec((rows, side), lambda g: (0, 0))
        inner = pl.pallas_call(
            functools.partial(in_kernel, dp),
            name="grad_w_in",
            cost_estimate=cost(4),
            grid=(1,),
            out_shape=(shape_of(part_rows, wide),) * 4,
            in_specs=[SMEM, acts_block(first_at), acts_block(first_at), whole, whole],
            scratch_shapes=[pltpu.VMEM((width, 2 * rows), BF)]
            + [pltpu.VMEM((width // 2, 2 * rows), BF)] * 2,
            compiler_params=params(16),
        )(d, acts, acts_peer, grads_keep, grads_peer)
        red_back = Reduction("back", back)
        red_in = Reduction("in", inner)
        msg_prev, msg_next, keep_a, keep_b = lax.optimization_barrier(
            (msg_prev, msg_next, red_back.keeps[0], red_in.keeps[0])
        )
        red_back.keeps = (keep_a, red_back.keeps[1])
        red_in.keeps = (keep_b, red_in.keeps[1])

    qkv_grad, qkv_keep, qkv_send, qkv_send2, sums = pl.pallas_call(
        functools.partial(attend_back_kernel, groups),
        name="attend_backward",
        cost_estimate=cost(11),
        out_shape=(
            shape_of(rows, 3 * width),
            shape_of(rows, 2 * qkv_block),
            shape_of(loc + 2 * SUM_ROWS, 2 * qkv_block),
            shape_of(rows - loc, 2 * qkv_block),
            shape_of(SUM_ROWS, width, dtype=F32),
        ),
        in_specs=[SMEM] + [VMEM] * 9,
        out_specs=(VMEM,) * 5,
        scratch_shapes=[pltpu.VMEM((2, 3, 128, loc), F32)],
        compiler_params=params(16),
    )(me, mask, mask_t, near_qkv, own_qkv, msg_prev, msg, msg_next, small1, small2)
    if kernels:
        red_back.step({})
        qkv_send, keep_a = lax.optimization_barrier((qkv_send, red_back.keeps[0]))
        red_back.keeps = (keep_a, red_back.keeps[1])
    qkv_peer, qkv_peer2 = flip(qkv_send, 0), flip(qkv_send2, 0)
    input_grad = grad_one + dot(qkv_grad, w_qkv, 1, 1)
    if kernels:
        red_in.step({})
        *qkv, sums = pl.pallas_call(
            functools.partial(qkv_kernel, dp),
            name="grad_w_qkv_out",
            cost_estimate=cost(3),
            out_shape=(
                shape_of(part_rows, width),
                shape_of(part_rows + 2 * SUM_ROWS, width),
                shape_of(part_rows, width),
                shape_of(part_rows, width),
                shape_of(SUM_ROWS, width, dtype=F32),
            ),
            grid=(1,),
            in_specs=[SMEM]
            + [pl.BlockSpec((rows, width), lambda i: (0, 0))] * 3
            + [acts_block(ctx_at)] * 2
            + [pl.BlockSpec((rows, 2 * qkv_block), lambda i: (0, 0))]
            + [pl.BlockSpec((loc + 2 * SUM_ROWS, 2 * qkv_block), lambda i: (0, 0))]
            + [pl.BlockSpec((rows - loc, 2 * qkv_block), lambda i: (0, 0))]
            + [pl.BlockSpec((rows, extra), lambda i: (0, out_at))] * 2
            + [pl.BlockSpec((SUM_ROWS, width), lambda i: (0, 0))],
            scratch_shapes=[pltpu.VMEM((width, 2 * rows), BF)] * 2
            + [pltpu.VMEM((width // 2, 2 * rows), BF)] * 4,
            compiler_params=params(20),
        )(
            jnp.concatenate([d, me]),
            flat,
            tok_prev,
            tok_next,
            acts,
            acts_peer,
            qkv_keep,
            qkv_peer,
            qkv_peer2,
            grads_keep,
            grads_peer,
            sums,
        )
        qkv[3], keep_b = lax.optimization_barrier((qkv[3], red_in.keeps[0]))
        red_in.keeps = (keep_b, red_in.keeps[1])
        red_qkv = Reduction("qkv", qkv, sums)
        units = (red_back, red_in, red_qkv)
        last = (
            ((ff // dp, small),),
            ((block_rows, wide),),
            ((block_rows, qkv_block), (block_rows, small)),
        )
        done = None
        for k in EVENTS if dp_bits == 3 else [0, 1, 2] * (dp_bits + 1):
            if units[k].at > dp_bits:
                continue
            outs = {"rows": block_rows // 2}
            if units[k].at == dp_bits:
                outs["last"] = last[k]
            if done is not None and done is not units[k]:
                wait_for(units[k], done)
            units[k].step(outs)
            done = units[k]
        g_back = red_back.result[0]
        g_in = red_in.result[0]
        g_qkv, g_out, sums = red_qkv.result
    else:

        def by_x(v, w):
            return v.reshape(v.shape[0], 2, w).transpose(1, 0, 2)

        def pile(a, b):
            return jnp.concatenate([a, b], axis=0)

        feeds = by_x(pile(feed_keep, acts_peer[:, base:]), small)
        g_back = plain_reduce(pile(acts[:, :ff], acts_peer[:, :ff]), feeds)
        grads = pile(grads_keep, grads_peer)
        lefts = pile(acts, acts_peer)
        g_in = plain_reduce(lefts[:, ff : ff + width], by_x(grads[:, : 2 * wide], wide))
        g_out = plain_reduce(lefts[:, ff + width : base], by_x(grads[:, 2 * wide :], small))
        other = jnp.where(me[0] % 2 == 0, tok_next, tok_prev)
        grads = by_x(pile(qkv_keep, pile(qkv_peer[:loc], qkv_peer2)), qkv_block)
        g_qkv = plain_reduce(pile(flat, other), grads)
        sums = plain_sum(sums, 0)
    b_back_g, gain2, shift2 = sums[0], sums[1], sums[2]
    b_in_g = sums[3:7].reshape(-1)
    b_out_g, gain1, shift1, b_q_g, b_v_g = sums[7], sums[8], sums[9], sums[10], sums[11]
    shape = (seqs, loc, width)
    return (
        result.reshape(shape),
        input_grad.reshape(shape).astype(BF),
        g_qkv,
        b_q_g,
        b_v_g,
        g_out,
        b_out_g,
        gain1,
        shift1,
        g_in,
        b_in_g,
        g_back,
        b_back_g,
        gain2,
        shift2,
    )


EVENTS = [0, 1, 0, 2, 1, 2, 0, 1, 2, 2]


def solution(mesh):
    row = P("dp", "seq", None)
    in_specs = (row, P("dp", None), P("dp", None)) + (P(),) * 13 + (row,)
    block = P("dp", "seq")
    out_specs = (row, row, block, P(), P(), block, P(), P(), P(), block, P(), block, P(), P(), P())
    return jax.shard_map(local, mesh=mesh, in_specs=in_specs, out_specs=out_specs, check_vma=False)
```

```python
import functools

import jax
import jax.numpy as jnp
from jax import lax
from jax.experimental import pallas as pl
from jax.experimental.pallas import tpu as pltpu
from jax.sharding import PartitionSpec as P

HEADS = 12
HDIM = 64
PAIR = 2 * HDIM
LN_EPS = 1e-12
FAR = -1e9
SUM_ROWS = 16
BOTH = ("dp", "seq")
BF = jnp.bfloat16
F32 = jnp.float32
HBM = pl.BlockSpec(memory_space=pltpu.HBM)
VMEM = pl.BlockSpec(memory_space=pltpu.VMEM)
SMEM = pl.BlockSpec(memory_space=pltpu.SMEM)


def dot(a, b, ca=1, cb=0):
    return lax.dot_general(a, b, (((ca,), (cb,)), ((), ())), preferred_element_type=F32)


def mean_of(v):
    return jnp.mean(v, axis=-1, keepdims=True)


def norm_parts(values):
    center = values - mean_of(values)
    inverse = lax.rsqrt(mean_of(center * center) + LN_EPS)
    return center * inverse, inverse


def norm_pull(upstream, normed, inverse, gain):
    scaled = upstream * gain
    return (scaled - mean_of(scaled) - normed * mean_of(scaled * normed)) * inverse


def col_sum(v):
    return jnp.sum(v, axis=0, keepdims=True)


def mask_of(me, groups, ids_ref, row, loc):
    own = pl.ds(pl.multiple_of(me * loc, loc), loc)
    seg_ref, pad_ref = ids_ref.at[0], ids_ref.at[1]
    seg_t = jnp.broadcast_to(seg_ref[row : row + 1, own].astype(F32), (loc, loc)).T
    pad_t = jnp.broadcast_to(pad_ref[row : row + 1, own].astype(F32), (loc, loc)).T
    eye = lax.broadcasted_iota(jnp.int32, (loc, loc), 0) == lax.broadcasted_iota(
        jnp.int32, (loc, loc), 1
    )
    keys, queries = [], []
    for block in range(3):
        at = me + block - 1
        out_of = jnp.where((at < 0) | (at >= groups), FAR, 0.0).astype(F32)
        at = jnp.clip(at, 0, groups - 1)
        span = pl.ds(pl.multiple_of(at * loc, loc), loc)
        seg_b = seg_ref[row : row + 1, span].astype(F32)
        pad_b = pad_ref[row : row + 1, span].astype(F32)
        same = seg_t == seg_b
        seen, seen_t = pad_b == 0.0, pad_t == 0.0
        if block == 1:
            seen, seen_t = seen | eye, seen_t | eye
        keys.append(jnp.where(same & seen, 0.0, FAR) + out_of)
        queries.append(jnp.where(same & seen_t, 0.0, FAR) + out_of)
    return jnp.concatenate(keys, axis=1), jnp.concatenate(queries, axis=1)


def split_pair(v, low):
    zero = jnp.zeros_like(v)
    return jnp.concatenate([jnp.where(low, v, zero), jnp.where(low, zero, v)], axis=0)


def join_pair(v, low):
    half = v.shape[0] // 2
    return jnp.where(low, v[:half], v[half:])


def own_kernel(
    groups, me_ref, ids_ref, tok_ref, vec_ref, wqkv_hbm, qkv_ref, mask_ref, mask_t_ref, wqkv, sems
):
    me = me_ref[0]
    rows, width = tok_ref.shape
    loc = rows // 2
    copies = []
    for part in range(3):
        cols = pl.ds(part * width, width)
        copies.append(pltpu.make_async_copy(wqkv_hbm.at[:, cols], wqkv.at[:, cols], sems.at[part]))
        copies[-1].start()
    for row in range(2):
        mask_ref[row], mask_t_ref[row] = mask_of(me, groups, ids_ref, row, loc)
    vec = vec_ref[...].reshape(1, -1)
    biases = (vec[:, :width], 0.0, vec[:, width : 2 * width])
    for part in range(3):
        copies[part].wait()
        cols = slice(part * width, (part + 1) * width)
        qkv_ref[:, cols] = (dot(tok_ref[...], wqkv[:, cols]) + biases[part]).astype(BF)


def forward_kernel(
    groups,
    me_ref,
    tok_prev,
    tok_next,
    tok_own,
    own_ref,
    mask_ref,
    vec_ref,
    vec2_ref,
    b_in_ref,
    wqkv,
    og_hbm,
    wout_hbm,
    win_hbm,
    wback_hbm,
    qkv_ref,
    acts_ref,
    feed_ref,
    slope_ref,
    lse_ref,
    normed_ref,
    inv_ref,
    gtwo_ref,
    out_ref,
    keep_ref,
    small_ref,
    wout,
    win,
    wback,
    ctx_ref,
    og_ref,
    sems,
):
    me = me_ref[0]
    rows, width = tok_own.shape
    loc = rows // 2
    ff = win.shape[1]
    pairs = ((wout_hbm, wout), (win_hbm, win), (wback_hbm, wback), (og_hbm, og_ref))
    copies = [pltpu.make_async_copy(a, b, sems.at[i]) for i, (a, b) in enumerate(pairs)]
    for copy in copies:
        copy.start()
    vec, vec2 = vec_ref[...].reshape(1, -1), vec2_ref[...].reshape(1, -1)
    b_query, b_value, b_out, gain1 = (vec[:, i * width : (i + 1) * width] for i in range(4))
    shift1, b_back, gain2, shift2 = (vec2[:, i * width : (i + 1) * width] for i in range(4))
    b_in = b_in_ref[...].reshape(1, -1)
    b_qkv = (b_query, 0.0, b_value)
    for part in range(3):
        cols = slice(part * width, (part + 1) * width)
        for block, tok in enumerate((tok_prev, tok_next)):
            qkv_ref[block, :, cols] = (dot(tok[...], wqkv[:, cols]) + b_qkv[part]).astype(BF)
    blocks = (qkv_ref.at[0], own_ref, qkv_ref.at[1])
    low = lax.broadcasted_iota(jnp.int32, (loc, PAIR), 1) < HDIM
    lanes = lax.broadcasted_iota(jnp.int32, (loc, 128), 1)

    def attend(p, totals):
        spans = [pl.ds(pl.multiple_of(p * PAIR + part * width, PAIR), PAIR) for part in range(3)]
        result = []
        for row in range(2):
            at = slice(row * loc, (row + 1) * loc)
            q2 = split_pair(own_ref[at, spans[0]], low) * jnp.asarray(HDIM**-0.5, BF)
            k3 = jnp.concatenate([b[at, spans[1]] for b in blocks], axis=0)
            v3 = jnp.concatenate([b[at, spans[2]] for b in blocks], axis=0)
            mask = mask_ref[row]
            scores = dot(q2, k3, 1, 1) + jnp.concatenate([mask, mask], axis=0)
            top = jnp.max(scores, axis=-1, keepdims=True)
            powers = jnp.exp(scores - top)
            total = jnp.sum(powers, axis=-1, keepdims=True)
            probs = (powers * (1.0 / total)).astype(BF)
            ctx_ref[at, pl.ds(pl.multiple_of(p * PAIR, PAIR), PAIR)] = join_pair(
                dot(probs, v3), low
            ).astype(BF)
            lse = top + jnp.log(total)
            old = totals[row]
            old = jnp.where(lanes == 2 * p, lse[:loc], old)
            result.append(jnp.where(lanes == 2 * p + 1, lse[loc:], old))
        return tuple(result)

    zero = jnp.zeros((loc, 128), F32)
    totals = lax.fori_loop(0, HEADS // 2, attend, (zero, zero), unroll=3)
    lse_ref[:loc, :] = totals[0]
    lse_ref[loc:, :] = totals[1]
    context = ctx_ref[...]
    acts_ref[:, ff + width : ff + 2 * width] = context
    copies[0].wait()
    branch = dot(context, wout[...]) + b_out
    normed, inverse = norm_parts(tok_own[...].astype(F32) + branch)
    normed_ref[...] = normed
    inv_ref[...] = inverse
    first = normed * gain1 + shift1
    first_low = first.astype(BF)
    acts_ref[:, ff : ff + width] = first_low
    copies[1].wait()
    copies[2].wait()
    feed = first + b_back
    for c in range(ff // width):
        cols = slice(c * width, (c + 1) * width)
        before = dot(first_low, win[:, cols]) + b_in[:, cols]
        cdf = 0.5 + 0.5 * lax.erf(before * (0.5**0.5))
        hidden = (before * cdf).astype(BF)
        acts_ref[:, cols] = hidden
        bell = jnp.exp(-0.5 * before * before) * (0.3989422804014327)
        slope_ref[:, cols] = (cdf + before * bell).astype(BF)
        feed = feed + dot(hidden, wback[cols, :])
    normed2, inverse2 = norm_parts(feed)
    out_ref[...] = (normed2 * gain2 + shift2).astype(BF)
    copies[3].wait()
    upstream = og_ref[...].astype(F32)
    grad_two = norm_pull(upstream, normed2, inverse2, gain2)
    gtwo_ref[...] = grad_two
    feed_grad = grad_two.astype(BF)
    feed_ref[...] = feed_grad
    small_ref[0:1, :] = col_sum(feed_grad.astype(F32))
    small_ref[1:2, :] = col_sum(upstream * normed2)
    small_ref[2:3, :] = col_sum(upstream)
    base = ff + 2 * width
    block = width // groups
    for s in range(groups):
        rel = s ^ me
        piece = feed_grad[:, s * block : (s + 1) * block]
        for i in range(groups // 2):

            @pl.when(rel == 2 * i)
            def _():
                keep_ref[:, i * block : (i + 1) * block] = piece

            @pl.when(rel == 2 * i + 1)
            def _():
                acts_ref[:, base + i * block : base + (i + 1) * block] = piece


def backward_kernel(
    groups,
    me_ref,
    feed_ref,
    slope_ref,
    gtwo_ref,
    normed_ref,
    inv_ref,
    acts_ref,
    lse_ref,
    vec_ref,
    wout,
    win,
    wback,
    keep_ref,
    send_ref,
    msg_ref,
    gone_ref,
    small_ref,
):
    me = me_ref[0]
    rows, width = feed_ref.shape
    ff = win.shape[1]
    block = ff // groups
    spans = [pl.ds(pl.multiple_of((i ^ me) * block, block), block) for i in range(groups)]
    feed_grad = feed_ref[...]
    first_grad = gtwo_ref[...]
    for i, span in enumerate(spans):
        s = i ^ me
        hidden_grad = dot(feed_grad, wback[span, :], 1, 1)
        before_grad = (hidden_grad * slope_ref[:, span].astype(F32)).astype(BF)
        small_ref[pl.ds(s, 1), :] = col_sum(before_grad.astype(F32))
        target = send_ref if i % 2 else keep_ref
        target[:, (i // 2) * block : (i // 2 + 1) * block] = before_grad
        first_grad = first_grad + dot(before_grad, win[:, span], 1, 1)
    normed = normed_ref[...]
    grad_one = norm_pull(first_grad, normed, inv_ref[...], vec_ref[3 * width :].reshape(1, -1))
    gone_ref[...] = grad_one
    branch_grad = grad_one.astype(BF)
    small_ref[4:5, :] = col_sum(branch_grad.astype(F32))
    small_ref[5:6, :] = col_sum(first_grad * normed)
    small_ref[6:7, :] = col_sum(first_grad)
    context_grad = dot(branch_grad, wout[...], 1, 1).astype(BF)
    msg_ref[:, :width] = context_grad
    product = context_grad.astype(F32) * acts_ref[:, ff + width : ff + 2 * width].astype(F32)
    lanes = lax.broadcasted_iota(jnp.int32, (rows, 128), 1)
    low = lanes < HDIM
    delta = jnp.zeros((rows, 128), F32)
    for p in range(HEADS // 2):
        tile = product[:, p * PAIR : (p + 1) * PAIR]
        both = jnp.sum(tile, axis=-1, keepdims=True)
        even = jnp.sum(jnp.where(low, tile, 0.0), axis=-1, keepdims=True)
        delta = jnp.where(lanes == 2 * p, even, delta)
        delta = jnp.where(lanes == 2 * p + 1, both - even, delta)
    packed = jnp.zeros((rows, 128), F32)
    shift = 0
    for value in (lse_ref[...], delta):
        for _ in range(3):
            term = value.astype(BF).astype(F32)
            packed = packed + (pltpu.roll(term, shift, 1) if shift else term)
            value = value - term
            shift += 16
    msg_ref[:, width:] = packed.astype(BF)
    base = 2 * block
    small = width // groups
    for s in range(groups):
        rel = s ^ me
        piece = branch_grad[:, s * small : (s + 1) * small]
        for i in range(groups // 2):

            @pl.when(rel == 2 * i)
            def _():
                keep_ref[:, base + i * small : base + (i + 1) * small] = piece

            @pl.when(rel == 2 * i + 1)
            def _():
                send_ref[:, base + i * small : base + (i + 1) * small] = piece


def attend_back_kernel(
    groups,
    me_ref,
    mask_ref,
    mask_t_ref,
    near_ref,
    own_ref,
    msg_prev,
    msg_own,
    msg_next,
    small1_ref,
    small2_ref,
    all_ref,
    keep_ref,
    send_ref,
    send2_ref,
    sums_ref,
    info_t_ref,
):
    me = me_ref[0]
    rows = msg_own.shape[0]
    width = own_ref.shape[1] // 3
    loc = rows // 2
    msgs = (msg_prev, msg_own, msg_next)
    blocks = (near_ref.at[0], own_ref, near_ref.at[1])
    own_info = []
    for row in range(2):
        at = slice(row * loc, (row + 1) * loc)
        for b in range(3):
            raw = msgs[b][at, width:].astype(F32)
            info = raw + pltpu.roll(raw, 112, 1) + pltpu.roll(raw, 96, 1)
            if b == 1:
                own_info.append(info)
            info_t_ref[row, b] = info.T
    low = lax.broadcasted_iota(jnp.int32, (loc, PAIR), 1) < HDIM
    lanes = lax.broadcasted_iota(jnp.int32, (loc, 128), 1)
    scale = jnp.asarray(HDIM**-0.5, BF)

    def column(info, lane):
        return jnp.sum(jnp.where(lanes == lane, info, 0.0), axis=-1, keepdims=True)

    def heads(p, carry):
        spans = [pl.ds(pl.multiple_of(p * PAIR + part * width, PAIR), PAIR) for part in range(3)]
        for row in range(2):
            at = slice(row * loc, (row + 1) * loc)
            info = own_info[row]
            lse2 = jnp.concatenate([column(info, 2 * p), column(info, 2 * p + 1)], axis=0)
            delta2 = jnp.concatenate([column(info, 48 + 2 * p), column(info, 49 + 2 * p)], axis=0)
            q3 = jnp.concatenate([b[at, spans[0]] for b in blocks], axis=0)
            k3 = jnp.concatenate([b[at, spans[1]] for b in blocks], axis=0)
            v3 = jnp.concatenate([b[at, spans[2]] for b in blocks], axis=0)
            u3 = jnp.concatenate([m[at, spans[0]] for m in msgs], axis=0)
            mask = mask_ref[row]
            scores = dot(split_pair(q3[loc : 2 * loc], low) * scale, k3, 1, 1)
            probs = jnp.exp(scores + jnp.concatenate([mask, mask], axis=0) - lse2)
            prob_grad = dot(split_pair(u3[loc : 2 * loc], low), v3, 1, 1)
            score_grad = (probs * (prob_grad - delta2)).astype(BF)
            query_grad = join_pair(dot(score_grad, k3), low) * HDIM**-0.5
            all_ref[at, spans[0]] = query_grad.astype(BF)

            def line(which):
                halves = []
                for h in range(2):
                    parts = [info_t_ref[row, b, pl.ds(which + 2 * p + h, 1), :] for b in range(3)]
                    halves.append(
                        jnp.broadcast_to(jnp.concatenate(parts, axis=1), (loc, 3 * loc))
                    )
                return jnp.concatenate(halves, axis=0)

            mask_t = mask_t_ref[row]
            scores_t = dot(split_pair(k3[loc : 2 * loc], low) * scale, q3, 1, 1)
            probs_t = jnp.exp(scores_t + jnp.concatenate([mask_t, mask_t], axis=0) - line(0))
            value_grad = join_pair(dot(probs_t.astype(BF), u3), low)
            prob_grad_t = dot(split_pair(v3[loc : 2 * loc], low), u3, 1, 1)
            score_grad_t = (probs_t * (prob_grad_t - line(48))).astype(BF)
            key_grad = join_pair(dot(score_grad_t, q3), low) * HDIM**-0.5
            all_ref[at, spans[1]] = key_grad.astype(BF)
            all_ref[at, spans[2]] = value_grad.astype(BF)
        return carry

    lax.fori_loop(0, HEADS // 2, heads, 0, unroll=3)
    value_at = 2 * width
    sums_ref[...] = jnp.concatenate(
        [
            small1_ref[...],
            small2_ref[...],
            col_sum(all_ref[:, :width].astype(F32)),
            col_sum(all_ref[:, value_at:].astype(F32)),
            jnp.zeros((SUM_ROWS - 12, width), F32),
        ],
        axis=0,
    )
    send_ref[loc:, :] = jnp.zeros((2 * SUM_ROWS, send_ref.shape[1]), BF)
    pack_sums(sums_ref[...], send_ref, loc)
    block = 3 * width // groups
    for s in range(groups):
        rel = s ^ me
        piece = all_ref[:, s * block : (s + 1) * block]
        for i in range(groups // 2):

            @pl.when(rel == 2 * i)
            def _():
                keep_ref[:, i * block : (i + 1) * block] = piece

            @pl.when(rel == 2 * i + 1)
            def _():
                send_ref[:loc, i * block : (i + 1) * block] = piece[:loc]
                send2_ref[:, i * block : (i + 1) * block] = piece[loc:]


def pack_sums(value, ref, at):
    high = value.astype(BF)
    ref[at : at + SUM_ROWS, : value.shape[1]] = high
    ref[at + SUM_ROWS : at + 2 * SUM_ROWS, : value.shape[1]] = (value - high.astype(F32)).astype(BF)


def read_sums(ref, at, width):
    high = ref[at : at + SUM_ROWS, :width].astype(F32)
    return high + ref[at + SUM_ROWS : at + 2 * SUM_ROWS, :width].astype(F32)


def turn_rows(d, dp, tmp_ref, turned_ref, block_rows, part):
    rows = block_rows // 2
    for j, rel in enumerate(low_first(dp)):
        start = pl.multiple_of((rel ^ d) * block_rows + part * rows, rows)
        turned_ref[j * rows : (j + 1) * rows, :] = tmp_ref[pl.ds(start, rows), :]


def low_first(dp):
    bits = dp.bit_length() - 1
    return [sum(((j >> (bits - 1 - k)) & 1) << k for k in range(bits)) for j in range(dp)]


def both_left(mine, peer):
    return jnp.concatenate([mine.T, peer.T], axis=1)


def by_halves(pieces, base, width):
    return [
        jnp.concatenate([r[:, base + x * width : base + (x + 1) * width] for r in pieces], axis=0)
        for x in range(2)
    ]


def put(result, part, x, keeps, sends):
    total = result.shape[0]
    half = total // 2
    if part == 0:
        (sends if x else keeps)[0][:total] = result
    else:
        keeps[1][x * half : (x + 1) * half] = result[:half]
        sends[1][x * half : (x + 1) * half] = result[half:]


def in_kernel(dp, d_ref, acts, acts_peer, mine, peer, keep0, send0, keep1, send1, tmp, *turned):
    width = acts.shape[1]
    tmp[...] = both_left(acts[...], acts_peer[...])
    wide = (mine.shape[1] - width // 2) // 2
    rights = by_halves((mine, peer), 0, wide)
    for part in range(2):
        turn_rows(d_ref[0], dp, tmp, turned[part], width // dp, part)
        for x in range(2):
            result = dot(turned[part][...], rights[x]).astype(BF)
            put(result, part, x, (keep0, keep1), (send0, send1))


def qkv_kernel(
    dp,
    ids_ref,
    tok,
    tok_prev,
    tok_next,
    ctx,
    ctx_peer,
    mine,
    peer,
    peer2,
    out_mine,
    out_peer,
    sums_ref,
    keep0,
    send0,
    keep1,
    send1,
    total_ref,
    tmp,
    tmp2,
    *turned,
):
    rows, width = tok.shape
    d = ids_ref[0]
    other = jnp.where(ids_ref[1] % 2 == 0, tok_next[...], tok_prev[...])
    tmp[...] = both_left(tok[...], other)
    tmp2[...] = both_left(ctx[...], ctx_peer[...])
    half = peer2.shape[0]
    rights = by_halves((mine, peer.at[:half], peer2), 0, mine.shape[1] // 2)
    outs = by_halves((out_mine, out_peer), 0, out_mine.shape[1] // 2)
    for part in range(2):
        turn_rows(d, dp, tmp, turned[part], width // dp, part)
        turn_rows(d, dp, tmp2, turned[2 + part], width // dp, part)
        for x in range(2):
            result = jnp.concatenate(
                [dot(turned[part][...], rights[x]), dot(turned[2 + part][...], outs[x])], axis=1
            ).astype(BF)
            put(result, part, x, (keep0, keep1), (send0, send1))
    total = sums_ref[...] + read_sums(peer, half, width)
    total_ref[...] = total
    pack_sums(total, send0, keep0.shape[0])


def back_kernel(dp, d_ref, hid, hid_peer, feed, feed_peer, keep0, send0, keep1, send1):
    d = d_ref[0]
    chunk = hid.shape[1] // dp
    side = feed.shape[1] // 2
    rows = side // 4
    turned = [feed[...].T, feed_peer[...].T]
    first, second, *rest = HALVING["back"]
    orders = [(first, second, *rest), (second, first, *rest)]
    for rel in range(dp):
        span = pl.ds(pl.multiple_of((rel ^ d) * chunk, chunk), chunk)
        result = (dot(turned[0], hid[:, span]) + dot(turned[1], hid_peer[:, span])).astype(BF)
        for x in range(2):
            bits = 2 * x + 4 * rel
            for part, refs in enumerate(((keep0, send0), (keep1, send1))):
                at = 0
                for bit in orders[part]:
                    at = 2 * at + ((bits >> bit) & 1)
                ref, at = refs[at // dp], at % dp
                for h in range(2):
                    start = x * side + h * 2 * rows + part * rows
                    ref[at * rows : (at + 1) * rows, h * chunk : (h + 1) * chunk] = result[
                        start : start + rows
                    ]


def total_of(keep, got):
    return keep[...].astype(F32) + got[: keep.shape[0]].astype(F32)


def step_sums(sums_ref, got, at, total_ref, send, send_at):
    total = sums_ref[...] + read_sums(got, at, sums_ref.shape[1])
    total_ref[...] = total
    if send is not None:
        pack_sums(total, send, send_at)


def first_step(keep0, got0, keep1, got1, *refs):
    if len(refs) == 6:
        sums_ref, new0, send0, new1, send1, total_ref = refs
        step_sums(sums_ref, got0, keep0.shape[0], total_ref, send0, keep0.shape[0] // 2)
    else:
        new0, send0, new1, send1 = refs
    half = keep0.shape[0] // 2
    for keep, got, new, send in ((keep0, got0, new0, send0), (keep1, got1, new1, send1)):
        total = total_of(keep, got).astype(BF)
        new[...] = total[:half]
        send[:half] = total[half:]


def second_step(rows, keep0, got0, keep1, got1, *refs):
    if len(refs) == 4:
        sums_ref, new, send, total_ref = refs
        step_sums(sums_ref, got0, keep0.shape[0], total_ref, send, new.shape[0])
    else:
        new, send = refs
    half = keep0.shape[0] // 2
    for part, (keep, got) in enumerate(((keep0, got0), (keep1, got1))):
        total = total_of(keep, got).astype(BF)
        for b in range(half // rows):
            at = (2 * b + part) * rows
            new[at : at + rows] = total[b * rows : (b + 1) * rows]
            send[at : at + rows] = total[half + b * rows : half + (b + 1) * rows]


def third_step(keep, got, *refs):
    if len(refs) == 4:
        sums_ref, new, send, total_ref = refs
        step_sums(sums_ref, got, keep.shape[0], total_ref, send, new.shape[0])
    else:
        new, send = refs
    half = keep.shape[0] // 2
    total = total_of(keep, got).astype(BF)
    new[...] = total[:half]
    send[:half] = total[half:]


def last_step(kind, keep, got, *refs):
    total = total_of(keep, got)
    if kind == "back":
        chunk = total.shape[1] // 2
        refs[0][...] = jnp.concatenate([total[:, :chunk].T, total[:, chunk:].T], axis=1)
    elif kind == "in":
        refs[0][...] = total
    else:
        sums_ref, qkv_ref, out_ref, total_ref = refs
        qkv_ref[...] = total[:, : qkv_ref.shape[1]]
        out_ref[...] = total[:, qkv_ref.shape[1] :]
        step_sums(sums_ref, got, keep.shape[0], total_ref, None, 0)


HALVING = {"back": (2, 3, 1, 4), "in": (1, 2, 3, 4), "qkv": (1, 2, 3, 4)}


def flip(value, bit):
    count = lax.axis_size("dp") * lax.axis_size("seq")
    return lax.ppermute(value, BOTH, [(i, i ^ (1 << bit)) for i in range(count)])


class Reduction:
    def __init__(self, kind, parts, sums=None):
        self.kind, self.keeps, self.sums = kind, parts[0::2], sums
        self.at, self.result = 0, None
        self.gots = tuple(flip(v, b) for v, b in zip(parts[1::2], HALVING[kind]))

    def step(self, outs):
        extra = 0 if self.sums is None else 2 * SUM_ROWS
        total = self.keeps[0].shape[0]
        width = self.keeps[0].shape[1]
        half = total // 2
        operands = [v for pair in zip(self.keeps, self.gots) for v in pair]
        sums = () if self.sums is None else (shape_of(SUM_ROWS, width, dtype=F32),)
        if self.at == 0:
            kernel = first_step
            shapes = (half, half + extra, half, half)
        elif self.at == 1:
            kernel = functools.partial(second_step, outs["rows"])
            shapes = (total, total + extra)
        else:
            kernel, shapes = third_step, (half, half + extra)
        shapes = tuple(shape_of(n, width) for n in shapes) + sums
        last = self.at > 1 and "last" in outs
        if last:
            kernel = functools.partial(last_step, self.kind)
            shapes = tuple(shape_of(*dims, dtype=F32) for dims in outs["last"]) + sums
        if self.sums is not None:
            operands.append(self.sums)
        result = pl.pallas_call(
            kernel,
            name=f"add_{self.kind}_{self.at}",
            cost_estimate=cost(1),
            out_shape=shapes,
            in_specs=[VMEM] * len(operands),
            out_specs=(VMEM,) * len(shapes),
            compiler_params=params(12),
        )(*operands)
        if self.sums is not None:
            self.sums = result[-1]
        self.at += 1
        if last:
            self.result = result
            return
        self.keeps = result[0 : len(shapes) - len(sums) : 2]
        sends = result[1 : len(shapes) - len(sums) : 2]
        bits = HALVING[self.kind]
        bits = bits[1::-1] if self.at == 1 else bits[self.at :]
        self.gots = tuple(flip(v, b) for v, b in zip(sends, bits))


def wait_for(unit, done):
    got, *rest = unit.gots
    if done.result is None:
        keep, *others = done.keeps
        got, keep = lax.optimization_barrier((got, keep))
        done.keeps = (keep, *others)
    else:
        first, *others = done.result
        got, first = lax.optimization_barrier((got, first))
        done.result = (first, *others)
    unit.gots = (got, *rest)


def plain_reduce(left, right):
    dp = lax.axis_size("dp")
    part = jnp.einsum("tk,xtw->xkw", left, right, preferred_element_type=F32).astype(BF)
    part = part[0].astype(F32) + flip(part[1], 1).astype(F32)
    part = part.reshape(dp, left.shape[1] // dp, right.shape[2]).astype(BF)
    part = jnp.take(part, jnp.arange(dp) ^ lax.axis_index("dp"), axis=0)
    for bit in reversed(range(dp.bit_length() - 1)):
        half = part.shape[0] // 2
        part = part[:half].astype(F32) + flip(part[half:], 2 + bit).astype(F32)
        part = part.astype(BF) if bit else part
    return part[0]


def plain_sum(value, low):
    count = lax.axis_size("dp") * lax.axis_size("seq")
    for bit in range(low, count.bit_length() - 1):
        value = value + flip(value, bit)
    return value


def shape_of(*dims, dtype=BF):
    return jax.ShapeDtypeStruct(dims, dtype)


def cost(us):
    return pl.CostEstimate(flops=int(us * 1e6), bytes_accessed=int(us * 1e4), transcendentals=0)


def params(mib):
    return pltpu.CompilerParams(vmem_limit_bytes=mib << 20)


def local(
    tokens,
    segment_ids,
    padding,
    w_qkv,
    b_query,
    b_value,
    w_out,
    b_out,
    ln1_gain,
    ln1_bias,
    w_in,
    b_in,
    w_back,
    b_back,
    ln2_gain,
    ln2_bias,
    out_grad,
):
    seqs, loc, width = tokens.shape
    groups, dp = lax.axis_size("seq"), lax.axis_size("dp")
    dp_bits = dp.bit_length() - 1
    ff = w_in.shape[1]
    rows = seqs * loc
    me = lax.axis_index("seq").astype(jnp.int32).reshape(1)
    d = lax.axis_index("dp").astype(jnp.int32).reshape(1)
    up = [(i, i + 1) for i in range(groups - 1)]
    down = [(i + 1, i) for i in range(groups - 1)]

    def around(value):
        return lax.ppermute(value, "seq", up), lax.ppermute(value, "seq", down)

    flat = tokens.reshape(rows, width)
    tok_prev, tok_next = around(flat)
    vec1 = jnp.concatenate([b_query, b_value, b_out, ln1_gain])
    vec2 = jnp.concatenate([ln1_bias, b_back, ln2_gain, ln2_bias])
    ids = jnp.stack([segment_ids, padding])
    own_qkv, mask, mask_t, wqkv = pl.pallas_call(
        functools.partial(own_kernel, groups),
        name="own_projections",
        cost_estimate=cost(4),
        out_shape=(
            shape_of(rows, 3 * width),
            shape_of(seqs, loc, 3 * loc, dtype=F32),
            shape_of(seqs, loc, 3 * loc, dtype=F32),
            shape_of(*w_qkv.shape),
        ),
        in_specs=[SMEM] + [VMEM] * 3 + [HBM],
        out_specs=(VMEM,) * 4,
        scratch_shapes=[pltpu.SemaphoreType.DMA((3,))],
        compiler_params=params(48),
    )(me, ids, flat, vec1, w_qkv)
    extra = width // groups * 2
    acts_width = ff + 2 * width + extra
    near_qkv, acts, feed_grad, slope, lse, normed, inverse, grad_two, result, feed_keep, small1, *weights = (
        pl.pallas_call(
            functools.partial(forward_kernel, groups),
            name="layer_forward",
            cost_estimate=cost(16),
            out_shape=(
                shape_of(2, rows, 3 * width),
                shape_of(rows, acts_width),
                shape_of(rows, width),
                shape_of(rows, ff),
                shape_of(rows, 128, dtype=F32),
                shape_of(rows, width, dtype=F32),
                shape_of(rows, 1, dtype=F32),
                shape_of(rows, width, dtype=F32),
                shape_of(rows, width),
                shape_of(rows, extra),
                shape_of(3, width, dtype=F32),
                *(shape_of(*w.shape) for w in (w_out, w_in, w_back)),
            ),
            in_specs=[SMEM] + [VMEM] * 9 + [HBM] * 4,
            out_specs=(VMEM,) * 14,
            scratch_shapes=[
                pltpu.VMEM((rows, width), BF),
                pltpu.VMEM((rows, width), BF),
                pltpu.SemaphoreType.DMA((4,)),
            ],
            compiler_params=params(24),
        )(
            me,
            tok_prev,
            tok_next,
            flat,
            own_qkv,
            mask,
            vec1,
            vec2,
            b_in,
            wqkv,
            out_grad.reshape(rows, width),
            w_out,
            w_in,
            w_back,
        )
    )
    acts_peer = flip(acts, 0)

    side = 2 * (ff // groups) + extra
    grads_keep, grads_send, msg, grad_one, small2 = pl.pallas_call(
        functools.partial(backward_kernel, groups),
        name="layer_backward",
            cost_estimate=cost(8),
        out_shape=(
            shape_of(rows, side),
            shape_of(rows, side),
            shape_of(rows, width + 128),
            shape_of(rows, width, dtype=F32),
            shape_of(7, width, dtype=F32),
        ),
        in_specs=[SMEM] + [VMEM] * 11,
        out_specs=(VMEM,) * 5,
        compiler_params=params(12),
    )(me, feed_grad, slope, grad_two, normed, inverse, acts, lse, vec1, *weights)
    msg_prev, msg_next = around(msg)
    grads_peer = flip(grads_send, 0)

    kernels = (width // dp) % 32 == 0 and (ff // dp) % 128 == 0 and dp == 8
    small = width // groups
    wide = ff // groups
    qkv_block = 3 * width // groups
    block_rows = width // dp
    part_rows = dp * block_rows // 2
    base = ff + 2 * width

    def acts_block(i):
        return pl.BlockSpec((rows, width), lambda g: (0, i))

    first_at, ctx_at = ff // width, ff // width + 1
    out_at = 2 * wide // extra
    if kernels:
        back = pl.pallas_call(
            functools.partial(back_kernel, dp),
            name="grad_w_back",
            cost_estimate=cost(3),
            grid=(1,),
            out_shape=(shape_of(part_rows, width),) * 4,
            in_specs=[
                SMEM,
                pl.BlockSpec((rows, ff), lambda i: (0, 0)),
                pl.BlockSpec((rows, ff), lambda i: (0, 0)),
                pl.BlockSpec((rows, extra), lambda i: (0, 0)),
                pl.BlockSpec((rows, extra), lambda i: (0, base // extra)),
            ],
            compiler_params=params(16),
        )(d, acts, acts_peer, feed_keep, acts_peer)
        grads_keep, msg_prev, msg_next = lax.optimization_barrier((grads_keep, msg_prev, msg_next))
        whole = pl.BlockSpec((rows, side), lambda g: (0, 0))
        inner = pl.pallas_call(
            functools.partial(in_kernel, dp),
            name="grad_w_in",
            cost_estimate=cost(4),
            grid=(1,),
            out_shape=(shape_of(part_rows, wide),) * 4,
            in_specs=[SMEM, acts_block(first_at), acts_block(first_at), whole, whole],
            scratch_shapes=[pltpu.VMEM((width, 2 * rows), BF)]
            + [pltpu.VMEM((width // 2, 2 * rows), BF)] * 2,
            compiler_params=params(16),
        )(d, acts, acts_peer, grads_keep, grads_peer)
        red_back = Reduction("back", back)
        red_in = Reduction("in", inner)
        msg_prev, msg_next, keep_a, keep_b = lax.optimization_barrier(
            (msg_prev, msg_next, red_back.keeps[0], red_in.keeps[0])
        )
        red_back.keeps = (keep_a, red_back.keeps[1])
        red_in.keeps = (keep_b, red_in.keeps[1])

    qkv_grad, qkv_keep, qkv_send, qkv_send2, sums = pl.pallas_call(
        functools.partial(attend_back_kernel, groups),
        name="attend_backward",
        cost_estimate=cost(11),
        out_shape=(
            shape_of(rows, 3 * width),
            shape_of(rows, 2 * qkv_block),
            shape_of(loc + 2 * SUM_ROWS, 2 * qkv_block),
            shape_of(rows - loc, 2 * qkv_block),
            shape_of(SUM_ROWS, width, dtype=F32),
        ),
        in_specs=[SMEM] + [VMEM] * 9,
        out_specs=(VMEM,) * 5,
        scratch_shapes=[pltpu.VMEM((2, 3, 128, loc), F32)],
        compiler_params=params(16),
    )(me, mask, mask_t, near_qkv, own_qkv, msg_prev, msg, msg_next, small1, small2)
    if kernels:
        red_back.step({})
        qkv_send, keep_a = lax.optimization_barrier((qkv_send, red_back.keeps[0]))
        red_back.keeps = (keep_a, red_back.keeps[1])
    qkv_peer, qkv_peer2 = flip(qkv_send, 0), flip(qkv_send2, 0)
    input_grad = grad_one + dot(qkv_grad, w_qkv, 1, 1)
    if kernels:
        red_in.step({})
        *qkv, sums = pl.pallas_call(
            functools.partial(qkv_kernel, dp),
            name="grad_w_qkv_out",
            cost_estimate=cost(3),
            out_shape=(
                shape_of(part_rows, width),
                shape_of(part_rows + 2 * SUM_ROWS, width),
                shape_of(part_rows, width),
                shape_of(part_rows, width),
                shape_of(SUM_ROWS, width, dtype=F32),
            ),
            grid=(1,),
            in_specs=[SMEM]
            + [pl.BlockSpec((rows, width), lambda i: (0, 0))] * 3
            + [acts_block(ctx_at)] * 2
            + [pl.BlockSpec((rows, 2 * qkv_block), lambda i: (0, 0))]
            + [pl.BlockSpec((loc + 2 * SUM_ROWS, 2 * qkv_block), lambda i: (0, 0))]
            + [pl.BlockSpec((rows - loc, 2 * qkv_block), lambda i: (0, 0))]
            + [pl.BlockSpec((rows, extra), lambda i: (0, out_at))] * 2
            + [pl.BlockSpec((SUM_ROWS, width), lambda i: (0, 0))],
            scratch_shapes=[pltpu.VMEM((width, 2 * rows), BF)] * 2
            + [pltpu.VMEM((width // 2, 2 * rows), BF)] * 4,
            compiler_params=params(20),
        )(
            jnp.concatenate([d, me]),
            flat,
            tok_prev,
            tok_next,
            acts,
            acts_peer,
            qkv_keep,
            qkv_peer,
            qkv_peer2,
            grads_keep,
            grads_peer,
            sums,
        )
        qkv[3], keep_b = lax.optimization_barrier((qkv[3], red_in.keeps[0]))
        red_in.keeps = (keep_b, red_in.keeps[1])
        red_qkv = Reduction("qkv", qkv, sums)
        units = (red_back, red_in, red_qkv)
        last = (
            ((ff // dp, small),),
            ((block_rows, wide),),
            ((block_rows, qkv_block), (block_rows, small)),
        )
        done = None
        for k in EVENTS if dp_bits == 3 else [0, 1, 2] * (dp_bits + 1):
            if units[k].at > dp_bits:
                continue
            outs = {"rows": block_rows // 2}
            if units[k].at == dp_bits:
                outs["last"] = last[k]
            if done is not None and done is not units[k]:
                wait_for(units[k], done)
            units[k].step(outs)
            done = units[k]
        g_back = red_back.result[0]
        g_in = red_in.result[0]
        g_qkv, g_out, sums = red_qkv.result
    else:

        def by_x(v, w):
            return v.reshape(v.shape[0], 2, w).transpose(1, 0, 2)

        def pile(a, b):
            return jnp.concatenate([a, b], axis=0)

        feeds = by_x(pile(feed_keep, acts_peer[:, base:]), small)
        g_back = plain_reduce(pile(acts[:, :ff], acts_peer[:, :ff]), feeds)
        grads = pile(grads_keep, grads_peer)
        lefts = pile(acts, acts_peer)
        g_in = plain_reduce(lefts[:, ff : ff + width], by_x(grads[:, : 2 * wide], wide))
        g_out = plain_reduce(lefts[:, ff + width : base], by_x(grads[:, 2 * wide :], small))
        other = jnp.where(me[0] % 2 == 0, tok_next, tok_prev)
        grads = by_x(pile(qkv_keep, pile(qkv_peer[:loc], qkv_peer2)), qkv_block)
        g_qkv = plain_reduce(pile(flat, other), grads)
        sums = plain_sum(sums, 0)
    b_back_g, gain2, shift2 = sums[0], sums[1], sums[2]
    b_in_g = sums[3:7].reshape(-1)
    b_out_g, gain1, shift1, b_q_g, b_v_g = sums[7], sums[8], sums[9], sums[10], sums[11]
    shape = (seqs, loc, width)
    return (
        result.reshape(shape),
        input_grad.reshape(shape).astype(BF),
        g_qkv,
        b_q_g,
        b_v_g,
        g_out,
        b_out_g,
        gain1,
        shift1,
        g_in,
        b_in_g,
        g_back,
        b_back_g,
        gain2,
        shift2,
    )


EVENTS = [0, 1, 0, 2, 1, 2, 0, 1, 2, 2]


def solution(mesh):
    row = P("dp", "seq", None)
    in_specs = (row, P("dp", None), P("dp", None)) + (P(),) * 13 + (row,)
    block = P("dp", "seq")
    out_specs = (row, row, block, P(), P(), block, P(), P(), P(), block, P(), block, P(), P(), P())
    return jax.shard_map(local, mesh=mesh, in_specs=in_specs, out_specs=out_specs, check_vma=False)
```

```python
import functools

import jax
import jax.numpy as jnp
from jax import lax
from jax.experimental import pallas as pl
from jax.experimental.pallas import tpu as pltpu
from jax.sharding import PartitionSpec as P

HEADS = 12
HDIM = 64
PAIR = 2 * HDIM
LN_EPS = 1e-12
FAR = -1e9
SUM_ROWS = 16
BOTH = ("dp", "seq")
BF = jnp.bfloat16
F32 = jnp.float32
HBM = pl.BlockSpec(memory_space=pltpu.HBM)
VMEM = pl.BlockSpec(memory_space=pltpu.VMEM)
SMEM = pl.BlockSpec(memory_space=pltpu.SMEM)


def dot(a, b, ca=1, cb=0):
    return lax.dot_general(a, b, (((ca,), (cb,)), ((), ())), preferred_element_type=F32)


def mean_of(v):
    return jnp.mean(v, axis=-1, keepdims=True)


def norm_parts(values):
    center = values - mean_of(values)
    inverse = lax.rsqrt(mean_of(center * center) + LN_EPS)
    return center * inverse, inverse


def norm_pull(upstream, normed, inverse, gain):
    scaled = upstream * gain
    return (scaled - mean_of(scaled) - normed * mean_of(scaled * normed)) * inverse


def col_sum(v):
    return jnp.sum(v, axis=0, keepdims=True)


def mask_of(me, groups, ids_ref, row, loc):
    own = pl.ds(pl.multiple_of(me * loc, loc), loc)
    seg_ref, pad_ref = ids_ref.at[0], ids_ref.at[1]
    seg_t = jnp.broadcast_to(seg_ref[row : row + 1, own].astype(F32), (loc, loc)).T
    pad_t = jnp.broadcast_to(pad_ref[row : row + 1, own].astype(F32), (loc, loc)).T
    eye = lax.broadcasted_iota(jnp.int32, (loc, loc), 0) == lax.broadcasted_iota(
        jnp.int32, (loc, loc), 1
    )
    keys, queries = [], []
    for block in range(3):
        at = me + block - 1
        out_of = jnp.where((at < 0) | (at >= groups), FAR, 0.0).astype(F32)
        at = jnp.clip(at, 0, groups - 1)
        span = pl.ds(pl.multiple_of(at * loc, loc), loc)
        seg_b = seg_ref[row : row + 1, span].astype(F32)
        pad_b = pad_ref[row : row + 1, span].astype(F32)
        same = seg_t == seg_b
        seen, seen_t = pad_b == 0.0, pad_t == 0.0
        if block == 1:
            seen, seen_t = seen | eye, seen_t | eye
        keys.append(jnp.where(same & seen, 0.0, FAR) + out_of)
        queries.append(jnp.where(same & seen_t, 0.0, FAR) + out_of)
    return jnp.concatenate(keys, axis=1), jnp.concatenate(queries, axis=1)


def split_pair(v, low):
    zero = jnp.zeros_like(v)
    return jnp.concatenate([jnp.where(low, v, zero), jnp.where(low, zero, v)], axis=0)


def join_pair(v, low):
    half = v.shape[0] // 2
    return jnp.where(low, v[:half], v[half:])


def own_kernel(
    groups, me_ref, ids_ref, tok_ref, vec_ref, wqkv_hbm, qkv_ref, mask_ref, mask_t_ref, wqkv, sems
):
    me = me_ref[0]
    rows, width = tok_ref.shape
    loc = rows // 2
    copies = []
    for part in range(3):
        cols = pl.ds(part * width, width)
        copies.append(pltpu.make_async_copy(wqkv_hbm.at[:, cols], wqkv.at[:, cols], sems.at[part]))
        copies[-1].start()
    for row in range(2):
        mask_ref[row], mask_t_ref[row] = mask_of(me, groups, ids_ref, row, loc)
    vec = vec_ref[...].reshape(1, -1)
    biases = (vec[:, :width], 0.0, vec[:, width : 2 * width])
    for part in range(3):
        copies[part].wait()
        cols = slice(part * width, (part + 1) * width)
        qkv_ref[:, cols] = (dot(tok_ref[...], wqkv[:, cols]) + biases[part]).astype(BF)


def forward_kernel(
    groups,
    me_ref,
    tok_prev,
    tok_next,
    tok_own,
    own_ref,
    mask_ref,
    vec_ref,
    vec2_ref,
    b_in_ref,
    wqkv,
    og_hbm,
    wout_hbm,
    win_hbm,
    wback_hbm,
    qkv_ref,
    acts_ref,
    feed_ref,
    slope_ref,
    lse_ref,
    normed_ref,
    inv_ref,
    gtwo_ref,
    out_ref,
    keep_ref,
    small_ref,
    wout,
    win,
    wback,
    ctx_ref,
    og_ref,
    sems,
):
    me = me_ref[0]
    rows, width = tok_own.shape
    loc = rows // 2
    ff = win.shape[1]
    pairs = ((wout_hbm, wout), (win_hbm, win), (wback_hbm, wback), (og_hbm, og_ref))
    copies = [pltpu.make_async_copy(a, b, sems.at[i]) for i, (a, b) in enumerate(pairs)]
    for copy in copies:
        copy.start()
    vec, vec2 = vec_ref[...].reshape(1, -1), vec2_ref[...].reshape(1, -1)
    b_query, b_value, b_out, gain1 = (vec[:, i * width : (i + 1) * width] for i in range(4))
    shift1, b_back, gain2, shift2 = (vec2[:, i * width : (i + 1) * width] for i in range(4))
    b_in = b_in_ref[...].reshape(1, -1)
    b_qkv = (b_query, 0.0, b_value)
    for part in range(3):
        cols = slice(part * width, (part + 1) * width)
        for block, tok in enumerate((tok_prev, tok_next)):
            qkv_ref[block, :, cols] = (dot(tok[...], wqkv[:, cols]) + b_qkv[part]).astype(BF)
    blocks = (qkv_ref.at[0], own_ref, qkv_ref.at[1])
    low = lax.broadcasted_iota(jnp.int32, (loc, PAIR), 1) < HDIM
    lanes = lax.broadcasted_iota(jnp.int32, (loc, 128), 1)

    def attend(p, totals):
        spans = [pl.ds(pl.multiple_of(p * PAIR + part * width, PAIR), PAIR) for part in range(3)]
        result = []
        for row in range(2):
            at = slice(row * loc, (row + 1) * loc)
            q2 = split_pair(own_ref[at, spans[0]], low) * jnp.asarray(HDIM**-0.5, BF)
            k3 = jnp.concatenate([b[at, spans[1]] for b in blocks], axis=0)
            v3 = jnp.concatenate([b[at, spans[2]] for b in blocks], axis=0)
            mask = mask_ref[row]
            scores = dot(q2, k3, 1, 1) + jnp.concatenate([mask, mask], axis=0)
            top = jnp.max(scores, axis=-1, keepdims=True)
            powers = jnp.exp(scores - top)
            total = jnp.sum(powers, axis=-1, keepdims=True)
            probs = (powers * (1.0 / total)).astype(BF)
            ctx_ref[at, pl.ds(pl.multiple_of(p * PAIR, PAIR), PAIR)] = join_pair(
                dot(probs, v3), low
            ).astype(BF)
            lse = top + jnp.log(total)
            old = totals[row]
            old = jnp.where(lanes == 2 * p, lse[:loc], old)
            result.append(jnp.where(lanes == 2 * p + 1, lse[loc:], old))
        return tuple(result)

    zero = jnp.zeros((loc, 128), F32)
    totals = lax.fori_loop(0, HEADS // 2, attend, (zero, zero), unroll=3)
    lse_ref[:loc, :] = totals[0]
    lse_ref[loc:, :] = totals[1]
    context = ctx_ref[...]
    acts_ref[:, ff + width : ff + 2 * width] = context
    copies[0].wait()
    branch = dot(context, wout[...]) + b_out
    normed, inverse = norm_parts(tok_own[...].astype(F32) + branch)
    normed_ref[...] = normed
    inv_ref[...] = inverse
    first = normed * gain1 + shift1
    first_low = first.astype(BF)
    acts_ref[:, ff : ff + width] = first_low
    copies[1].wait()
    copies[2].wait()
    feed = first + b_back
    for c in range(ff // width):
        cols = slice(c * width, (c + 1) * width)
        before = dot(first_low, win[:, cols]) + b_in[:, cols]
        cdf = 0.5 + 0.5 * lax.erf(before * (0.5**0.5))
        hidden = (before * cdf).astype(BF)
        acts_ref[:, cols] = hidden
        bell = jnp.exp(-0.5 * before * before) * (0.3989422804014327)
        slope_ref[:, cols] = (cdf + before * bell).astype(BF)
        feed = feed + dot(hidden, wback[cols, :])
    normed2, inverse2 = norm_parts(feed)
    out_ref[...] = (normed2 * gain2 + shift2).astype(BF)
    copies[3].wait()
    upstream = og_ref[...].astype(F32)
    grad_two = norm_pull(upstream, normed2, inverse2, gain2)
    gtwo_ref[...] = grad_two
    feed_grad = grad_two.astype(BF)
    feed_ref[...] = feed_grad
    small_ref[0:1, :] = col_sum(feed_grad.astype(F32))
    small_ref[1:2, :] = col_sum(upstream * normed2)
    small_ref[2:3, :] = col_sum(upstream)
    base = ff + 2 * width
    block = width // groups
    for s in range(groups):
        rel = s ^ me
        piece = feed_grad[:, s * block : (s + 1) * block]
        for i in range(groups // 2):

            @pl.when(rel == 2 * i)
            def _():
                keep_ref[:, i * block : (i + 1) * block] = piece

            @pl.when(rel == 2 * i + 1)
            def _():
                acts_ref[:, base + i * block : base + (i + 1) * block] = piece


def backward_kernel(
    groups,
    me_ref,
    feed_ref,
    slope_ref,
    gtwo_ref,
    normed_ref,
    inv_ref,
    acts_ref,
    lse_ref,
    vec_ref,
    wout,
    win,
    wback,
    keep_ref,
    send_ref,
    msg_ref,
    gone_ref,
    small_ref,
):
    me = me_ref[0]
    rows, width = feed_ref.shape
    ff = win.shape[1]
    block = ff // groups
    spans = [pl.ds(pl.multiple_of((i ^ me) * block, block), block) for i in range(groups)]
    feed_grad = feed_ref[...]
    first_grad = gtwo_ref[...]
    for i, span in enumerate(spans):
        s = i ^ me
        hidden_grad = dot(feed_grad, wback[span, :], 1, 1)
        before_grad = (hidden_grad * slope_ref[:, span].astype(F32)).astype(BF)
        small_ref[pl.ds(s, 1), :] = col_sum(before_grad.astype(F32))
        target = send_ref if i % 2 else keep_ref
        target[:, (i // 2) * block : (i // 2 + 1) * block] = before_grad
        first_grad = first_grad + dot(before_grad, win[:, span], 1, 1)
    normed = normed_ref[...]
    grad_one = norm_pull(first_grad, normed, inv_ref[...], vec_ref[3 * width :].reshape(1, -1))
    gone_ref[...] = grad_one
    branch_grad = grad_one.astype(BF)
    small_ref[4:5, :] = col_sum(branch_grad.astype(F32))
    small_ref[5:6, :] = col_sum(first_grad * normed)
    small_ref[6:7, :] = col_sum(first_grad)
    context_grad = dot(branch_grad, wout[...], 1, 1).astype(BF)
    msg_ref[:, :width] = context_grad
    product = context_grad.astype(F32) * acts_ref[:, ff + width : ff + 2 * width].astype(F32)
    lanes = lax.broadcasted_iota(jnp.int32, (rows, 128), 1)
    low = lanes < HDIM
    delta = jnp.zeros((rows, 128), F32)
    for p in range(HEADS // 2):
        tile = product[:, p * PAIR : (p + 1) * PAIR]
        both = jnp.sum(tile, axis=-1, keepdims=True)
        even = jnp.sum(jnp.where(low, tile, 0.0), axis=-1, keepdims=True)
        delta = jnp.where(lanes == 2 * p, even, delta)
        delta = jnp.where(lanes == 2 * p + 1, both - even, delta)
    packed = jnp.zeros((rows, 128), F32)
    shift = 0
    for value in (lse_ref[...], delta):
        for _ in range(3):
            term = value.astype(BF).astype(F32)
            packed = packed + (pltpu.roll(term, shift, 1) if shift else term)
            value = value - term
            shift += 16
    msg_ref[:, width:] = packed.astype(BF)
    base = 2 * block
    small = width // groups
    for s in range(groups):
        rel = s ^ me
        piece = branch_grad[:, s * small : (s + 1) * small]
        for i in range(groups // 2):

            @pl.when(rel == 2 * i)
            def _():
                keep_ref[:, base + i * small : base + (i + 1) * small] = piece

            @pl.when(rel == 2 * i + 1)
            def _():
                send_ref[:, base + i * small : base + (i + 1) * small] = piece


def attend_back_kernel(
    groups,
    me_ref,
    mask_ref,
    mask_t_ref,
    near_ref,
    own_ref,
    msg_prev,
    msg_own,
    msg_next,
    small1_ref,
    small2_ref,
    all_ref,
    keep_ref,
    send_ref,
    send2_ref,
    sums_ref,
    info_t_ref,
):
    me = me_ref[0]
    rows = msg_own.shape[0]
    width = own_ref.shape[1] // 3
    loc = rows // 2
    msgs = (msg_prev, msg_own, msg_next)
    blocks = (near_ref.at[0], own_ref, near_ref.at[1])
    own_info = []
    for row in range(2):
        at = slice(row * loc, (row + 1) * loc)
        for b in range(3):
            raw = msgs[b][at, width:].astype(F32)
            info = raw + pltpu.roll(raw, 112, 1) + pltpu.roll(raw, 96, 1)
            if b == 1:
                own_info.append(info)
            info_t_ref[row, b] = info.T
    low = lax.broadcasted_iota(jnp.int32, (loc, PAIR), 1) < HDIM
    lanes = lax.broadcasted_iota(jnp.int32, (loc, 128), 1)
    scale = jnp.asarray(HDIM**-0.5, BF)

    def column(info, lane):
        return jnp.sum(jnp.where(lanes == lane, info, 0.0), axis=-1, keepdims=True)

    def heads(p, carry):
        spans = [pl.ds(pl.multiple_of(p * PAIR + part * width, PAIR), PAIR) for part in range(3)]
        for row in range(2):
            at = slice(row * loc, (row + 1) * loc)
            info = own_info[row]
            lse2 = jnp.concatenate([column(info, 2 * p), column(info, 2 * p + 1)], axis=0)
            delta2 = jnp.concatenate([column(info, 48 + 2 * p), column(info, 49 + 2 * p)], axis=0)
            q3 = jnp.concatenate([b[at, spans[0]] for b in blocks], axis=0)
            k3 = jnp.concatenate([b[at, spans[1]] for b in blocks], axis=0)
            v3 = jnp.concatenate([b[at, spans[2]] for b in blocks], axis=0)
            u3 = jnp.concatenate([m[at, spans[0]] for m in msgs], axis=0)
            mask = mask_ref[row]
            scores = dot(split_pair(q3[loc : 2 * loc], low) * scale, k3, 1, 1)
            probs = jnp.exp(scores + jnp.concatenate([mask, mask], axis=0) - lse2)
            prob_grad = dot(split_pair(u3[loc : 2 * loc], low), v3, 1, 1)
            score_grad = (probs * (prob_grad - delta2)).astype(BF)
            query_grad = join_pair(dot(score_grad, k3), low) * HDIM**-0.5
            all_ref[at, spans[0]] = query_grad.astype(BF)

            def line(which):
                halves = []
                for h in range(2):
                    parts = [info_t_ref[row, b, pl.ds(which + 2 * p + h, 1), :] for b in range(3)]
                    halves.append(
                        jnp.broadcast_to(jnp.concatenate(parts, axis=1), (loc, 3 * loc))
                    )
                return jnp.concatenate(halves, axis=0)

            mask_t = mask_t_ref[row]
            scores_t = dot(split_pair(k3[loc : 2 * loc], low) * scale, q3, 1, 1)
            probs_t = jnp.exp(scores_t + jnp.concatenate([mask_t, mask_t], axis=0) - line(0))
            value_grad = join_pair(dot(probs_t.astype(BF), u3), low)
            prob_grad_t = dot(split_pair(v3[loc : 2 * loc], low), u3, 1, 1)
            score_grad_t = (probs_t * (prob_grad_t - line(48))).astype(BF)
            key_grad = join_pair(dot(score_grad_t, q3), low) * HDIM**-0.5
            all_ref[at, spans[1]] = key_grad.astype(BF)
            all_ref[at, spans[2]] = value_grad.astype(BF)
        return carry

    lax.fori_loop(0, HEADS // 2, heads, 0, unroll=3)
    value_at = 2 * width
    sums_ref[...] = jnp.concatenate(
        [
            small1_ref[...],
            small2_ref[...],
            col_sum(all_ref[:, :width].astype(F32)),
            col_sum(all_ref[:, value_at:].astype(F32)),
            jnp.zeros((SUM_ROWS - 12, width), F32),
        ],
        axis=0,
    )
    send_ref[loc:, :] = jnp.zeros((SUM_ROWS, send_ref.shape[1]), BF)
    pack_sums(sums_ref[...], send_ref, loc)
    block = 3 * width // groups
    for s in range(groups):
        rel = s ^ me
        piece = all_ref[:, s * block : (s + 1) * block]
        for i in range(groups // 2):

            @pl.when(rel == 2 * i)
            def _():
                keep_ref[:, i * block : (i + 1) * block] = piece

            @pl.when(rel == 2 * i + 1)
            def _():
                send_ref[:loc, i * block : (i + 1) * block] = piece[:loc]
                send2_ref[:, i * block : (i + 1) * block] = piece[loc:]


def pack_sums(value, ref, at):
    ref[at : at + SUM_ROWS, : value.shape[1]] = value.astype(BF)


def read_sums(ref, at, width):
    return ref[at : at + SUM_ROWS, :width].astype(F32)


def turn_rows(order, d, tmp_ref, turned_ref, block_rows, part):
    rows = block_rows // 2
    bits = [bit - 2 for bit in order if bit != 1]
    for j in range(1 << len(bits)):
        rel = sum(((j >> (len(bits) - 1 - k)) & 1) << bit for k, bit in enumerate(bits))
        start = pl.multiple_of((rel ^ d) * block_rows + part * rows, rows)
        turned_ref[j * rows : (j + 1) * rows, :] = tmp_ref[pl.ds(start, rows), :]


def orders_of(kind):
    first, second, *rest = HALVING[kind]
    return (first, second, *rest), (second, first, *rest)


def both_left(mine, peer):
    return jnp.concatenate([mine.T, peer.T], axis=1)


def by_halves(pieces, base, width):
    return [
        jnp.concatenate([r[:, base + x * width : base + (x + 1) * width] for r in pieces], axis=0)
        for x in range(2)
    ]


def put(result, order, x, keep, send):
    blocks = 1 << (len(order) - 1)
    rows = result.shape[0] // blocks
    k = order.index(1)
    run = blocks >> k
    for i in range(1 << k):
        at = (2 * i + x) * run
        ref, at = (keep, at) if at < blocks else (send, at - blocks)
        ref[at * rows : (at + run) * rows] = result[i * run * rows : (i + 1) * run * rows]


def in_kernel(dp, d_ref, acts, acts_peer, mine, peer, keep0, send0, keep1, send1, tmp, *turned):
    width = acts.shape[1]
    tmp[...] = both_left(acts[...], acts_peer[...])
    wide = (mine.shape[1] - width // 2) // 2
    rights = by_halves((mine, peer), 0, wide)
    outs = ((keep0, send0), (keep1, send1))
    for part, order in enumerate(orders_of("in")):
        turn_rows(order, d_ref[0], tmp, turned[part], width // dp, part)
        for x in range(2):
            put(dot(turned[part][...], rights[x]).astype(BF), order, x, *outs[part])


def qkv_kernel(
    dp,
    ids_ref,
    tok,
    tok_prev,
    tok_next,
    ctx,
    ctx_peer,
    mine,
    peer,
    peer2,
    out_mine,
    out_peer,
    sums_ref,
    keep0,
    send0,
    keep1,
    send1,
    total_ref,
    tmp,
    tmp2,
    *turned,
):
    rows, width = tok.shape
    d = ids_ref[0]
    other = jnp.where(ids_ref[1] % 2 == 0, tok_next[...], tok_prev[...])
    tmp[...] = both_left(tok[...], other)
    tmp2[...] = both_left(ctx[...], ctx_peer[...])
    half = peer2.shape[0]
    rights = by_halves((mine, peer.at[:half], peer2), 0, mine.shape[1] // 2)
    outs = by_halves((out_mine, out_peer), 0, out_mine.shape[1] // 2)
    refs = ((keep0, send0), (keep1, send1))
    for part, order in enumerate(orders_of("qkv")):
        turn_rows(order, d, tmp, turned[part], width // dp, part)
        turn_rows(order, d, tmp2, turned[2 + part], width // dp, part)
        for x in range(2):
            result = jnp.concatenate(
                [dot(turned[part][...], rights[x]), dot(turned[2 + part][...], outs[x])], axis=1
            ).astype(BF)
            put(result, order, x, *refs[part])
    total = sums_ref[...] + read_sums(peer, half, width)
    total_ref[...] = total
    pack_sums(total, send0, keep0.shape[0])


def back_kernel(dp, d_ref, hid, hid_peer, feed, feed_peer, keep0, send0, keep1, send1):
    d = d_ref[0]
    chunk = hid.shape[1] // dp
    side = feed.shape[1] // 2
    rows = side // 4
    turned = [feed[...].T, feed_peer[...].T]
    orders = orders_of("back")
    for rel in range(dp):
        span = pl.ds(pl.multiple_of((rel ^ d) * chunk, chunk), chunk)
        result = (dot(turned[0], hid[:, span]) + dot(turned[1], hid_peer[:, span])).astype(BF)
        for x in range(2):
            bits = 2 * x + 4 * rel
            for part, refs in enumerate(((keep0, send0), (keep1, send1))):
                at = 0
                for bit in orders[part]:
                    at = 2 * at + ((bits >> bit) & 1)
                ref, at = refs[at // dp], at % dp
                for h in range(2):
                    start = x * side + h * 2 * rows + part * rows
                    ref[at * rows : (at + 1) * rows, h * chunk : (h + 1) * chunk] = result[
                        start : start + rows
                    ]


def total_of(keep, got):
    return keep[...].astype(F32) + got[: keep.shape[0]].astype(F32)


def step_sums(sums_ref, got, at, total_ref, send, send_at):
    total = sums_ref[...] + read_sums(got, at, sums_ref.shape[1])
    total_ref[...] = total
    if send is not None:
        pack_sums(total, send, send_at)


def first_step(keep0, got0, keep1, got1, *refs):
    if len(refs) == 6:
        sums_ref, new0, send0, new1, send1, total_ref = refs
        step_sums(sums_ref, got0, keep0.shape[0], total_ref, send0, keep0.shape[0] // 2)
    else:
        new0, send0, new1, send1 = refs
    half = keep0.shape[0] // 2
    for keep, got, new, send in ((keep0, got0, new0, send0), (keep1, got1, new1, send1)):
        total = total_of(keep, got).astype(BF)
        new[...] = total[:half]
        send[:half] = total[half:]


def second_step(rows, keep0, got0, keep1, got1, *refs):
    if len(refs) == 4:
        sums_ref, new, send, total_ref = refs
        step_sums(sums_ref, got0, keep0.shape[0], total_ref, send, new.shape[0])
    else:
        new, send = refs
    half = keep0.shape[0] // 2
    for part, (keep, got) in enumerate(((keep0, got0), (keep1, got1))):
        total = total_of(keep, got).astype(BF)
        for b in range(half // rows):
            at = (2 * b + part) * rows
            new[at : at + rows] = total[b * rows : (b + 1) * rows]
            send[at : at + rows] = total[half + b * rows : half + (b + 1) * rows]


def third_step(keep, got, *refs):
    if len(refs) == 4:
        sums_ref, new, send, total_ref = refs
        step_sums(sums_ref, got, keep.shape[0], total_ref, send, new.shape[0])
    else:
        new, send = refs
    half = keep.shape[0] // 2
    total = total_of(keep, got).astype(BF)
    new[...] = total[:half]
    send[:half] = total[half:]


def last_step(kind, keep, got, *refs):
    total = total_of(keep, got)
    if kind == "back":
        chunk = total.shape[1] // 2
        refs[0][...] = jnp.concatenate([total[:, :chunk].T, total[:, chunk:].T], axis=1)
    elif kind == "in":
        refs[0][...] = total
    else:
        sums_ref, qkv_ref, out_ref, total_ref = refs
        qkv_ref[...] = total[:, : qkv_ref.shape[1]]
        out_ref[...] = total[:, qkv_ref.shape[1] :]
        step_sums(sums_ref, got, keep.shape[0], total_ref, None, 0)


HALVING = {"back": (2, 3, 1, 4), "in": (1, 3, 2, 4), "qkv": (1, 3, 2, 4)}


def flip(value, bit):
    count = lax.axis_size("dp") * lax.axis_size("seq")
    return lax.ppermute(value, BOTH, [(i, i ^ (1 << bit)) for i in range(count)])


class Reduction:
    def __init__(self, kind, parts, sums=None):
        self.kind, self.keeps, self.sums = kind, parts[0::2], sums
        self.at, self.result = 0, None
        self.gots = tuple(flip(v, b) for v, b in zip(parts[1::2], HALVING[kind]))

    def step(self, outs):
        extra = 0 if self.sums is None else SUM_ROWS
        total = self.keeps[0].shape[0]
        width = self.keeps[0].shape[1]
        half = total // 2
        operands = [v for pair in zip(self.keeps, self.gots) for v in pair]
        sums = () if self.sums is None else (shape_of(SUM_ROWS, width, dtype=F32),)
        if self.at == 0:
            kernel = first_step
            shapes = (half, half + extra, half, half)
        elif self.at == 1:
            kernel = functools.partial(second_step, outs["rows"])
            shapes = (total, total + extra)
        else:
            kernel, shapes = third_step, (half, half + extra)
        shapes = tuple(shape_of(n, width) for n in shapes) + sums
        last = self.at > 1 and "last" in outs
        if last:
            kernel = functools.partial(last_step, self.kind)
            shapes = tuple(shape_of(*dims, dtype=F32) for dims in outs["last"]) + sums
        if self.sums is not None:
            operands.append(self.sums)
        result = pl.pallas_call(
            kernel,
            name=f"add_{self.kind}_{self.at}",
            cost_estimate=cost(1),
            out_shape=shapes,
            in_specs=[VMEM] * len(operands),
            out_specs=(VMEM,) * len(shapes),
            compiler_params=params(12),
        )(*operands)
        if self.sums is not None:
            self.sums = result[-1]
        self.at += 1
        if last:
            self.result = result
            return
        self.keeps = result[0 : len(shapes) - len(sums) : 2]
        sends = result[1 : len(shapes) - len(sums) : 2]
        bits = HALVING[self.kind]
        bits = bits[1::-1] if self.at == 1 else bits[self.at :]
        self.gots = tuple(flip(v, b) for v, b in zip(sends, bits))


def wait_for(unit, done):
    got, *rest = unit.gots
    if done.result is None:
        keep, *others = done.keeps
        got, keep = lax.optimization_barrier((got, keep))
        done.keeps = (keep, *others)
    else:
        first, *others = done.result
        got, first = lax.optimization_barrier((got, first))
        done.result = (first, *others)
    unit.gots = (got, *rest)


def plain_reduce(left, right):
    dp = lax.axis_size("dp")
    part = jnp.einsum("tk,xtw->xkw", left, right, preferred_element_type=F32).astype(BF)
    part = part[0].astype(F32) + flip(part[1], 1).astype(F32)
    part = part.reshape(dp, left.shape[1] // dp, right.shape[2]).astype(BF)
    part = jnp.take(part, jnp.arange(dp) ^ lax.axis_index("dp"), axis=0)
    for bit in reversed(range(dp.bit_length() - 1)):
        half = part.shape[0] // 2
        part = part[:half].astype(F32) + flip(part[half:], 2 + bit).astype(F32)
        part = part.astype(BF) if bit else part
    return part[0]


def plain_sum(value, low):
    count = lax.axis_size("dp") * lax.axis_size("seq")
    for bit in range(low, count.bit_length() - 1):
        value = value + flip(value, bit)
    return value


def shape_of(*dims, dtype=BF):
    return jax.ShapeDtypeStruct(dims, dtype)


def cost(us):
    return pl.CostEstimate(flops=int(us * 1e6), bytes_accessed=int(us * 1e4), transcendentals=0)


def params(mib):
    return pltpu.CompilerParams(vmem_limit_bytes=mib << 20)


def local(
    tokens,
    segment_ids,
    padding,
    w_qkv,
    b_query,
    b_value,
    w_out,
    b_out,
    ln1_gain,
    ln1_bias,
    w_in,
    b_in,
    w_back,
    b_back,
    ln2_gain,
    ln2_bias,
    out_grad,
):
    seqs, loc, width = tokens.shape
    groups, dp = lax.axis_size("seq"), lax.axis_size("dp")
    dp_bits = dp.bit_length() - 1
    ff = w_in.shape[1]
    rows = seqs * loc
    me = lax.axis_index("seq").astype(jnp.int32).reshape(1)
    d = lax.axis_index("dp").astype(jnp.int32).reshape(1)
    up = [(i, i + 1) for i in range(groups - 1)]
    down = [(i + 1, i) for i in range(groups - 1)]

    def around(value):
        return lax.ppermute(value, "seq", up), lax.ppermute(value, "seq", down)

    flat = tokens.reshape(rows, width)
    tok_prev, tok_next = around(flat)
    vec1 = jnp.concatenate([b_query, b_value, b_out, ln1_gain])
    vec2 = jnp.concatenate([ln1_bias, b_back, ln2_gain, ln2_bias])
    ids = jnp.stack([segment_ids, padding])
    own_qkv, mask, mask_t, wqkv = pl.pallas_call(
        functools.partial(own_kernel, groups),
        name="own_projections",
        cost_estimate=cost(4),
        out_shape=(
            shape_of(rows, 3 * width),
            shape_of(seqs, loc, 3 * loc, dtype=F32),
            shape_of(seqs, loc, 3 * loc, dtype=F32),
            shape_of(*w_qkv.shape),
        ),
        in_specs=[SMEM] + [VMEM] * 3 + [HBM],
        out_specs=(VMEM,) * 4,
        scratch_shapes=[pltpu.SemaphoreType.DMA((3,))],
        compiler_params=params(48),
    )(me, ids, flat, vec1, w_qkv)
    extra = width // groups * 2
    acts_width = ff + 2 * width + extra
    near_qkv, acts, feed_grad, slope, lse, normed, inverse, grad_two, result, feed_keep, small1, *weights = (
        pl.pallas_call(
            functools.partial(forward_kernel, groups),
            name="layer_forward",
            cost_estimate=cost(16),
            out_shape=(
                shape_of(2, rows, 3 * width),
                shape_of(rows, acts_width),
                shape_of(rows, width),
                shape_of(rows, ff),
                shape_of(rows, 128, dtype=F32),
                shape_of(rows, width, dtype=F32),
                shape_of(rows, 1, dtype=F32),
                shape_of(rows, width, dtype=F32),
                shape_of(rows, width),
                shape_of(rows, extra),
                shape_of(3, width, dtype=F32),
                *(shape_of(*w.shape) for w in (w_out, w_in, w_back)),
            ),
            in_specs=[SMEM] + [VMEM] * 9 + [HBM] * 4,
            out_specs=(VMEM,) * 14,
            scratch_shapes=[
                pltpu.VMEM((rows, width), BF),
                pltpu.VMEM((rows, width), BF),
                pltpu.SemaphoreType.DMA((4,)),
            ],
            compiler_params=params(24),
        )(
            me,
            tok_prev,
            tok_next,
            flat,
            own_qkv,
            mask,
            vec1,
            vec2,
            b_in,
            wqkv,
            out_grad.reshape(rows, width),
            w_out,
            w_in,
            w_back,
        )
    )
    acts_peer = flip(acts, 0)

    side = 2 * (ff // groups) + extra
    grads_keep, grads_send, msg, grad_one, small2 = pl.pallas_call(
        functools.partial(backward_kernel, groups),
        name="layer_backward",
            cost_estimate=cost(8),
        out_shape=(
            shape_of(rows, side),
            shape_of(rows, side),
            shape_of(rows, width + 128),
            shape_of(rows, width, dtype=F32),
            shape_of(7, width, dtype=F32),
        ),
        in_specs=[SMEM] + [VMEM] * 11,
        out_specs=(VMEM,) * 5,
        compiler_params=params(12),
    )(me, feed_grad, slope, grad_two, normed, inverse, acts, lse, vec1, *weights)
    msg_prev, msg_next = around(msg)
    grads_peer = flip(grads_send, 0)

    kernels = (width // dp) % 32 == 0 and (ff // dp) % 128 == 0 and dp == 8
    small = width // groups
    wide = ff // groups
    qkv_block = 3 * width // groups
    block_rows = width // dp
    part_rows = dp * block_rows // 2
    base = ff + 2 * width

    def acts_block(i):
        return pl.BlockSpec((rows, width), lambda g: (0, i))

    first_at, ctx_at = ff // width, ff // width + 1
    out_at = 2 * wide // extra
    if kernels:
        back = pl.pallas_call(
            functools.partial(back_kernel, dp),
            name="grad_w_back",
            cost_estimate=cost(3),
            grid=(1,),
            out_shape=(shape_of(part_rows, width),) * 4,
            in_specs=[
                SMEM,
                pl.BlockSpec((rows, ff), lambda i: (0, 0)),
                pl.BlockSpec((rows, ff), lambda i: (0, 0)),
                pl.BlockSpec((rows, extra), lambda i: (0, 0)),
                pl.BlockSpec((rows, extra), lambda i: (0, base // extra)),
            ],
            compiler_params=params(16),
        )(d, acts, acts_peer, feed_keep, acts_peer)
        grads_keep, msg_prev, msg_next = lax.optimization_barrier((grads_keep, msg_prev, msg_next))
        whole = pl.BlockSpec((rows, side), lambda g: (0, 0))
        inner = pl.pallas_call(
            functools.partial(in_kernel, dp),
            name="grad_w_in",
            cost_estimate=cost(4),
            grid=(1,),
            out_shape=(shape_of(part_rows, wide),) * 4,
            in_specs=[SMEM, acts_block(first_at), acts_block(first_at), whole, whole],
            scratch_shapes=[pltpu.VMEM((width, 2 * rows), BF)]
            + [pltpu.VMEM((width // 2, 2 * rows), BF)] * 2,
            compiler_params=params(16),
        )(d, acts, acts_peer, grads_keep, grads_peer)
        red_back = Reduction("back", back)
        red_in = Reduction("in", inner)
        msg_prev, msg_next, keep_a, keep_b = lax.optimization_barrier(
            (msg_prev, msg_next, red_back.keeps[0], red_in.keeps[0])
        )
        red_back.keeps = (keep_a, red_back.keeps[1])
        red_in.keeps = (keep_b, red_in.keeps[1])

    qkv_grad, qkv_keep, qkv_send, qkv_send2, sums = pl.pallas_call(
        functools.partial(attend_back_kernel, groups),
        name="attend_backward",
        cost_estimate=cost(11),
        out_shape=(
            shape_of(rows, 3 * width),
            shape_of(rows, 2 * qkv_block),
            shape_of(loc + SUM_ROWS, 2 * qkv_block),
            shape_of(rows - loc, 2 * qkv_block),
            shape_of(SUM_ROWS, width, dtype=F32),
        ),
        in_specs=[SMEM] + [VMEM] * 9,
        out_specs=(VMEM,) * 5,
        scratch_shapes=[pltpu.VMEM((2, 3, 128, loc), F32)],
        compiler_params=params(16),
    )(me, mask, mask_t, near_qkv, own_qkv, msg_prev, msg, msg_next, small1, small2)
    if kernels:
        red_back.step({})
        qkv_send, keep_a = lax.optimization_barrier((qkv_send, red_back.keeps[0]))
        red_back.keeps = (keep_a, red_back.keeps[1])
    qkv_peer, qkv_peer2 = flip(qkv_send, 0), flip(qkv_send2, 0)
    input_grad = grad_one + dot(qkv_grad, w_qkv, 1, 1)
    if kernels:
        red_in.step({})
        *qkv, sums = pl.pallas_call(
            functools.partial(qkv_kernel, dp),
            name="grad_w_qkv_out",
            cost_estimate=cost(3),
            out_shape=(
                shape_of(part_rows, width),
                shape_of(part_rows + SUM_ROWS, width),
                shape_of(part_rows, width),
                shape_of(part_rows, width),
                shape_of(SUM_ROWS, width, dtype=F32),
            ),
            grid=(1,),
            in_specs=[SMEM]
            + [pl.BlockSpec((rows, width), lambda i: (0, 0))] * 3
            + [acts_block(ctx_at)] * 2
            + [pl.BlockSpec((rows, 2 * qkv_block), lambda i: (0, 0))]
            + [pl.BlockSpec((loc + SUM_ROWS, 2 * qkv_block), lambda i: (0, 0))]
            + [pl.BlockSpec((rows - loc, 2 * qkv_block), lambda i: (0, 0))]
            + [pl.BlockSpec((rows, extra), lambda i: (0, out_at))] * 2
            + [pl.BlockSpec((SUM_ROWS, width), lambda i: (0, 0))],
            scratch_shapes=[pltpu.VMEM((width, 2 * rows), BF)] * 2
            + [pltpu.VMEM((width // 2, 2 * rows), BF)] * 4,
            compiler_params=params(20),
        )(
            jnp.concatenate([d, me]),
            flat,
            tok_prev,
            tok_next,
            acts,
            acts_peer,
            qkv_keep,
            qkv_peer,
            qkv_peer2,
            grads_keep,
            grads_peer,
            sums,
        )
        qkv[3], keep_b = lax.optimization_barrier((qkv[3], red_in.keeps[0]))
        red_in.keeps = (keep_b, red_in.keeps[1])
        red_qkv = Reduction("qkv", qkv, sums)
        units = (red_back, red_in, red_qkv)
        last = (
            ((ff // dp, small),),
            ((block_rows, wide),),
            ((block_rows, qkv_block), (block_rows, small)),
        )
        done = None
        for k in EVENTS if dp_bits == 3 else [0, 1, 2] * (dp_bits + 1):
            if units[k].at > dp_bits:
                continue
            outs = {"rows": block_rows // 2}
            if units[k].at == dp_bits:
                outs["last"] = last[k]
            if done is not None and done is not units[k]:
                wait_for(units[k], done)
            units[k].step(outs)
            done = units[k]
        g_back = red_back.result[0]
        g_in = red_in.result[0]
        g_qkv, g_out, sums = red_qkv.result
    else:

        def by_x(v, w):
            return v.reshape(v.shape[0], 2, w).transpose(1, 0, 2)

        def pile(a, b):
            return jnp.concatenate([a, b], axis=0)

        feeds = by_x(pile(feed_keep, acts_peer[:, base:]), small)
        g_back = plain_reduce(pile(acts[:, :ff], acts_peer[:, :ff]), feeds)
        grads = pile(grads_keep, grads_peer)
        lefts = pile(acts, acts_peer)
        g_in = plain_reduce(lefts[:, ff : ff + width], by_x(grads[:, : 2 * wide], wide))
        g_out = plain_reduce(lefts[:, ff + width : base], by_x(grads[:, 2 * wide :], small))
        other = jnp.where(me[0] % 2 == 0, tok_next, tok_prev)
        grads = by_x(pile(qkv_keep, pile(qkv_peer[:loc], qkv_peer2)), qkv_block)
        g_qkv = plain_reduce(pile(flat, other), grads)
        sums = plain_sum(sums, 0)
    b_back_g, gain2, shift2 = sums[0], sums[1], sums[2]
    b_in_g = sums[3:7].reshape(-1)
    b_out_g, gain1, shift1, b_q_g, b_v_g = sums[7], sums[8], sums[9], sums[10], sums[11]
    shape = (seqs, loc, width)
    return (
        result.reshape(shape),
        input_grad.reshape(shape).astype(BF),
        g_qkv,
        b_q_g,
        b_v_g,
        g_out,
        b_out_g,
        gain1,
        shift1,
        g_in,
        b_in_g,
        g_back,
        b_back_g,
        gain2,
        shift2,
    )


EVENTS = [0, 1, 0, 2, 1, 2, 0, 1, 2, 2]


def solution(mesh):
    row = P("dp", "seq", None)
    in_specs = (row, P("dp", None), P("dp", None)) + (P(),) * 13 + (row,)
    block = P("dp", "seq")
    out_specs = (row, row, block, P(), P(), block, P(), P(), P(), block, P(), block, P(), P(), P())
    return jax.shard_map(local, mesh=mesh, in_specs=in_specs, out_specs=out_specs, check_vma=False)
```

```python
import functools

import jax
import jax.numpy as jnp
from jax import lax
from jax.experimental import pallas as pl
from jax.experimental.pallas import tpu as pltpu
from jax.sharding import PartitionSpec as P

HEADS = 12
HDIM = 64
PAIR = 2 * HDIM
LN_EPS = 1e-12
FAR = -1e9
SUM_ROWS = 16
BOTH = ("dp", "seq")
BF = jnp.bfloat16
F32 = jnp.float32
HBM = pl.BlockSpec(memory_space=pltpu.HBM)
VMEM = pl.BlockSpec(memory_space=pltpu.VMEM)
SMEM = pl.BlockSpec(memory_space=pltpu.SMEM)


def dot(a, b, ca=1, cb=0):
    return lax.dot_general(a, b, (((ca,), (cb,)), ((), ())), preferred_element_type=F32)


def mean_of(v):
    return jnp.mean(v, axis=-1, keepdims=True)


def norm_parts(values):
    center = values - mean_of(values)
    inverse = lax.rsqrt(mean_of(center * center) + LN_EPS)
    return center * inverse, inverse


def norm_pull(upstream, normed, inverse, gain):
    scaled = upstream * gain
    return (scaled - mean_of(scaled) - normed * mean_of(scaled * normed)) * inverse


def col_sum(v):
    return jnp.sum(v, axis=0, keepdims=True)


def mask_of(me, groups, ids_ref, row, loc):
    own = pl.ds(pl.multiple_of(me * loc, loc), loc)
    seg_ref, pad_ref = ids_ref.at[0], ids_ref.at[1]
    seg_t = jnp.broadcast_to(seg_ref[row : row + 1, own].astype(F32), (loc, loc)).T
    pad_t = jnp.broadcast_to(pad_ref[row : row + 1, own].astype(F32), (loc, loc)).T
    eye = lax.broadcasted_iota(jnp.int32, (loc, loc), 0) == lax.broadcasted_iota(
        jnp.int32, (loc, loc), 1
    )
    keys, queries = [], []
    for block in range(3):
        at = me + block - 1
        out_of = jnp.where((at < 0) | (at >= groups), FAR, 0.0).astype(F32)
        at = jnp.clip(at, 0, groups - 1)
        span = pl.ds(pl.multiple_of(at * loc, loc), loc)
        seg_b = seg_ref[row : row + 1, span].astype(F32)
        pad_b = pad_ref[row : row + 1, span].astype(F32)
        same = seg_t == seg_b
        seen, seen_t = pad_b == 0.0, pad_t == 0.0
        if block == 1:
            seen, seen_t = seen | eye, seen_t | eye
        keys.append(jnp.where(same & seen, 0.0, FAR) + out_of)
        queries.append(jnp.where(same & seen_t, 0.0, FAR) + out_of)
    return jnp.concatenate(keys, axis=1), jnp.concatenate(queries, axis=1)


def split_pair(v, low):
    zero = jnp.zeros_like(v)
    return jnp.concatenate([jnp.where(low, v, zero), jnp.where(low, zero, v)], axis=0)


def join_pair(v, low):
    half = v.shape[0] // 2
    return jnp.where(low, v[:half], v[half:])


def own_kernel(
    groups, me_ref, ids_ref, tok_ref, vec_ref, wqkv_hbm, qkv_ref, mask_ref, mask_t_ref, wqkv, sems
):
    me = me_ref[0]
    rows, width = tok_ref.shape
    loc = rows // 2
    copies = []
    for part in range(3):
        cols = pl.ds(part * width, width)
        copies.append(pltpu.make_async_copy(wqkv_hbm.at[:, cols], wqkv.at[:, cols], sems.at[part]))
        copies[-1].start()
    for row in range(2):
        mask_ref[row], mask_t_ref[row] = mask_of(me, groups, ids_ref, row, loc)
    vec = vec_ref[...].reshape(1, -1)
    biases = (vec[:, :width], 0.0, vec[:, width : 2 * width])
    for part in range(3):
        copies[part].wait()
        cols = slice(part * width, (part + 1) * width)
        qkv_ref[:, cols] = (dot(tok_ref[...], wqkv[:, cols]) + biases[part]).astype(BF)


def forward_kernel(
    groups,
    me_ref,
    tok_prev,
    tok_next,
    tok_own,
    own_ref,
    mask_ref,
    vec_ref,
    vec2_ref,
    b_in_ref,
    wqkv,
    og_hbm,
    wout_hbm,
    win_hbm,
    wback_hbm,
    qkv_ref,
    acts_ref,
    feed_ref,
    slope_ref,
    lse_ref,
    normed_ref,
    inv_ref,
    gtwo_ref,
    out_ref,
    keep_ref,
    small_ref,
    wout,
    win,
    wback,
    ctx_ref,
    og_ref,
    sems,
):
    me = me_ref[0]
    rows, width = tok_own.shape
    loc = rows // 2
    ff = win.shape[1]
    pairs = ((wout_hbm, wout), (win_hbm, win), (wback_hbm, wback), (og_hbm, og_ref))
    copies = [pltpu.make_async_copy(a, b, sems.at[i]) for i, (a, b) in enumerate(pairs)]
    for copy in copies:
        copy.start()
    vec, vec2 = vec_ref[...].reshape(1, -1), vec2_ref[...].reshape(1, -1)
    b_query, b_value, b_out, gain1 = (vec[:, i * width : (i + 1) * width] for i in range(4))
    shift1, b_back, gain2, shift2 = (vec2[:, i * width : (i + 1) * width] for i in range(4))
    b_in = b_in_ref[...].reshape(1, -1)
    b_qkv = (b_query, 0.0, b_value)
    for part in range(3):
        cols = slice(part * width, (part + 1) * width)
        for block, tok in enumerate((tok_prev, tok_next)):
            qkv_ref[block, :, cols] = (dot(tok[...], wqkv[:, cols]) + b_qkv[part]).astype(BF)
    blocks = (qkv_ref.at[0], own_ref, qkv_ref.at[1])
    low = lax.broadcasted_iota(jnp.int32, (loc, PAIR), 1) < HDIM
    lanes = lax.broadcasted_iota(jnp.int32, (loc, 128), 1)

    def attend(p, totals):
        spans = [pl.ds(pl.multiple_of(p * PAIR + part * width, PAIR), PAIR) for part in range(3)]
        result = []
        for row in range(2):
            at = slice(row * loc, (row + 1) * loc)
            q2 = split_pair(own_ref[at, spans[0]], low) * jnp.asarray(HDIM**-0.5, BF)
            k3 = jnp.concatenate([b[at, spans[1]] for b in blocks], axis=0)
            v3 = jnp.concatenate([b[at, spans[2]] for b in blocks], axis=0)
            mask = mask_ref[row]
            scores = dot(q2, k3, 1, 1) + jnp.concatenate([mask, mask], axis=0)
            top = jnp.max(scores, axis=-1, keepdims=True)
            powers = jnp.exp(scores - top)
            total = jnp.sum(powers, axis=-1, keepdims=True)
            probs = (powers * (1.0 / total)).astype(BF)
            ctx_ref[at, pl.ds(pl.multiple_of(p * PAIR, PAIR), PAIR)] = join_pair(
                dot(probs, v3), low
            ).astype(BF)
            lse = top + jnp.log(total)
            old = totals[row]
            old = jnp.where(lanes == 2 * p, lse[:loc], old)
            result.append(jnp.where(lanes == 2 * p + 1, lse[loc:], old))
        return tuple(result)

    zero = jnp.zeros((loc, 128), F32)
    totals = lax.fori_loop(0, HEADS // 2, attend, (zero, zero), unroll=3)
    lse_ref[:loc, :] = totals[0]
    lse_ref[loc:, :] = totals[1]
    context = ctx_ref[...]
    acts_ref[:, ff + width : ff + 2 * width] = context
    copies[0].wait()
    branch = dot(context, wout[...]) + b_out
    normed, inverse = norm_parts(tok_own[...].astype(F32) + branch)
    normed_ref[...] = normed
    inv_ref[...] = inverse
    first = normed * gain1 + shift1
    first_low = first.astype(BF)
    acts_ref[:, ff : ff + width] = first_low
    copies[1].wait()
    copies[2].wait()
    feed = first + b_back
    for c in range(ff // width):
        cols = slice(c * width, (c + 1) * width)
        before = dot(first_low, win[:, cols]) + b_in[:, cols]
        cdf = 0.5 + 0.5 * lax.erf(before * (0.5**0.5))
        hidden = (before * cdf).astype(BF)
        acts_ref[:, cols] = hidden
        bell = jnp.exp(-0.5 * before * before) * (0.3989422804014327)
        slope_ref[:, cols] = (cdf + before * bell).astype(BF)
        feed = feed + dot(hidden, wback[cols, :])
    normed2, inverse2 = norm_parts(feed)
    out_ref[...] = (normed2 * gain2 + shift2).astype(BF)
    copies[3].wait()
    upstream = og_ref[...].astype(F32)
    grad_two = norm_pull(upstream, normed2, inverse2, gain2)
    gtwo_ref[...] = grad_two
    feed_grad = grad_two.astype(BF)
    feed_ref[...] = feed_grad
    small_ref[0:1, :] = col_sum(feed_grad.astype(F32))
    small_ref[1:2, :] = col_sum(upstream * normed2)
    small_ref[2:3, :] = col_sum(upstream)
    base = ff + 2 * width
    block = width // groups
    for s in range(groups):
        rel = s ^ me
        piece = feed_grad[:, s * block : (s + 1) * block]
        for i in range(groups // 2):

            @pl.when(rel == 2 * i)
            def _():
                keep_ref[:, i * block : (i + 1) * block] = piece

            @pl.when(rel == 2 * i + 1)
            def _():
                acts_ref[:, base + i * block : base + (i + 1) * block] = piece


def backward_kernel(
    groups,
    me_ref,
    feed_ref,
    slope_ref,
    gtwo_ref,
    normed_ref,
    inv_ref,
    acts_ref,
    lse_ref,
    vec_ref,
    wout,
    win,
    wback,
    keep_ref,
    send_ref,
    msg_ref,
    gone_ref,
    small_ref,
):
    me = me_ref[0]
    rows, width = feed_ref.shape
    ff = win.shape[1]
    block = ff // groups
    spans = [pl.ds(pl.multiple_of((i ^ me) * block, block), block) for i in range(groups)]
    feed_grad = feed_ref[...]
    first_grad = gtwo_ref[...]
    for i, span in enumerate(spans):
        s = i ^ me
        hidden_grad = dot(feed_grad, wback[span, :], 1, 1)
        before_grad = (hidden_grad * slope_ref[:, span].astype(F32)).astype(BF)
        small_ref[pl.ds(s, 1), :] = col_sum(before_grad.astype(F32))
        target = send_ref if i % 2 else keep_ref
        target[:, (i // 2) * block : (i // 2 + 1) * block] = before_grad
        first_grad = first_grad + dot(before_grad, win[:, span], 1, 1)
    normed = normed_ref[...]
    grad_one = norm_pull(first_grad, normed, inv_ref[...], vec_ref[3 * width :].reshape(1, -1))
    gone_ref[...] = grad_one
    branch_grad = grad_one.astype(BF)
    small_ref[4:5, :] = col_sum(branch_grad.astype(F32))
    small_ref[5:6, :] = col_sum(first_grad * normed)
    small_ref[6:7, :] = col_sum(first_grad)
    context_grad = dot(branch_grad, wout[...], 1, 1).astype(BF)
    msg_ref[:, :width] = context_grad
    product = context_grad.astype(F32) * acts_ref[:, ff + width : ff + 2 * width].astype(F32)
    lanes = lax.broadcasted_iota(jnp.int32, (rows, 128), 1)
    low = lanes < HDIM
    delta = jnp.zeros((rows, 128), F32)
    for p in range(HEADS // 2):
        tile = product[:, p * PAIR : (p + 1) * PAIR]
        both = jnp.sum(tile, axis=-1, keepdims=True)
        even = jnp.sum(jnp.where(low, tile, 0.0), axis=-1, keepdims=True)
        delta = jnp.where(lanes == 2 * p, even, delta)
        delta = jnp.where(lanes == 2 * p + 1, both - even, delta)
    packed = jnp.zeros((rows, 128), F32)
    shift = 0
    for value in (lse_ref[...], delta):
        for _ in range(3):
            term = value.astype(BF).astype(F32)
            packed = packed + (pltpu.roll(term, shift, 1) if shift else term)
            value = value - term
            shift += 16
    msg_ref[:, width:] = packed.astype(BF)
    base = 2 * block
    small = width // groups
    for s in range(groups):
        rel = s ^ me
        piece = branch_grad[:, s * small : (s + 1) * small]
        for i in range(groups // 2):

            @pl.when(rel == 2 * i)
            def _():
                keep_ref[:, base + i * small : base + (i + 1) * small] = piece

            @pl.when(rel == 2 * i + 1)
            def _():
                send_ref[:, base + i * small : base + (i + 1) * small] = piece


def attend_back_kernel(
    groups,
    me_ref,
    mask_ref,
    mask_t_ref,
    near_ref,
    own_ref,
    msg_prev,
    msg_own,
    msg_next,
    small1_ref,
    small2_ref,
    all_ref,
    keep_ref,
    send_ref,
    send2_ref,
    sums_ref,
    info_t_ref,
):
    me = me_ref[0]
    rows = msg_own.shape[0]
    width = own_ref.shape[1] // 3
    loc = rows // 2
    msgs = (msg_prev, msg_own, msg_next)
    blocks = (near_ref.at[0], own_ref, near_ref.at[1])
    own_info = []
    for row in range(2):
        at = slice(row * loc, (row + 1) * loc)
        for b in range(3):
            raw = msgs[b][at, width:].astype(F32)
            info = raw + pltpu.roll(raw, 112, 1) + pltpu.roll(raw, 96, 1)
            if b == 1:
                own_info.append(info)
            info_t_ref[row, b] = info.T
    low = lax.broadcasted_iota(jnp.int32, (loc, PAIR), 1) < HDIM
    lanes = lax.broadcasted_iota(jnp.int32, (loc, 128), 1)
    scale = jnp.asarray(HDIM**-0.5, BF)

    def column(info, lane):
        return jnp.sum(jnp.where(lanes == lane, info, 0.0), axis=-1, keepdims=True)

    def heads(p, carry):
        spans = [pl.ds(pl.multiple_of(p * PAIR + part * width, PAIR), PAIR) for part in range(3)]
        for row in range(2):
            at = slice(row * loc, (row + 1) * loc)
            info = own_info[row]
            lse2 = jnp.concatenate([column(info, 2 * p), column(info, 2 * p + 1)], axis=0)
            delta2 = jnp.concatenate([column(info, 48 + 2 * p), column(info, 49 + 2 * p)], axis=0)
            q3 = jnp.concatenate([b[at, spans[0]] for b in blocks], axis=0)
            k3 = jnp.concatenate([b[at, spans[1]] for b in blocks], axis=0)
            v3 = jnp.concatenate([b[at, spans[2]] for b in blocks], axis=0)
            u3 = jnp.concatenate([m[at, spans[0]] for m in msgs], axis=0)
            mask = mask_ref[row]
            scores = dot(split_pair(q3[loc : 2 * loc], low) * scale, k3, 1, 1)
            probs = jnp.exp(scores + jnp.concatenate([mask, mask], axis=0) - lse2)
            prob_grad = dot(split_pair(u3[loc : 2 * loc], low), v3, 1, 1)
            score_grad = (probs * (prob_grad - delta2)).astype(BF)
            query_grad = join_pair(dot(score_grad, k3), low) * HDIM**-0.5
            all_ref[at, spans[0]] = query_grad.astype(BF)

            def line(which):
                halves = []
                for h in range(2):
                    parts = [info_t_ref[row, b, pl.ds(which + 2 * p + h, 1), :] for b in range(3)]
                    halves.append(
                        jnp.broadcast_to(jnp.concatenate(parts, axis=1), (loc, 3 * loc))
                    )
                return jnp.concatenate(halves, axis=0)

            mask_t = mask_t_ref[row]
            scores_t = dot(split_pair(k3[loc : 2 * loc], low) * scale, q3, 1, 1)
            probs_t = jnp.exp(scores_t + jnp.concatenate([mask_t, mask_t], axis=0) - line(0))
            value_grad = join_pair(dot(probs_t.astype(BF), u3), low)
            prob_grad_t = dot(split_pair(v3[loc : 2 * loc], low), u3, 1, 1)
            score_grad_t = (probs_t * (prob_grad_t - line(48))).astype(BF)
            key_grad = join_pair(dot(score_grad_t, q3), low) * HDIM**-0.5
            all_ref[at, spans[1]] = key_grad.astype(BF)
            all_ref[at, spans[2]] = value_grad.astype(BF)
        return carry

    lax.fori_loop(0, HEADS // 2, heads, 0, unroll=3)
    value_at = 2 * width
    sums_ref[...] = jnp.concatenate(
        [
            small1_ref[...],
            small2_ref[...],
            col_sum(all_ref[:, :width].astype(F32)),
            col_sum(all_ref[:, value_at:].astype(F32)),
            jnp.zeros((SUM_ROWS - 12, width), F32),
        ],
        axis=0,
    )
    send_ref[loc:, :] = jnp.zeros((SUM_ROWS, send_ref.shape[1]), BF)
    pack_sums(sums_ref[...], send_ref, loc)
    block = 3 * width // groups
    for s in range(groups):
        rel = s ^ me
        piece = all_ref[:, s * block : (s + 1) * block]
        for i in range(groups // 2):

            @pl.when(rel == 2 * i)
            def _():
                keep_ref[:, i * block : (i + 1) * block] = piece

            @pl.when(rel == 2 * i + 1)
            def _():
                send_ref[:loc, i * block : (i + 1) * block] = piece[:loc]
                send2_ref[:, i * block : (i + 1) * block] = piece[loc:]


def pack_sums(value, ref, at):
    ref[at : at + SUM_ROWS, : value.shape[1]] = value.astype(BF)


def read_sums(ref, at, width):
    return ref[at : at + SUM_ROWS, :width].astype(F32)


def turn_rows(order, d, tmp_ref, turned_ref, block_rows, part):
    rows = block_rows // 2
    bits = [bit - 2 for bit in order if bit != 1]
    for j in range(1 << len(bits)):
        rel = sum(((j >> (len(bits) - 1 - k)) & 1) << bit for k, bit in enumerate(bits))
        start = pl.multiple_of((rel ^ d) * block_rows + part * rows, rows)
        turned_ref[j * rows : (j + 1) * rows, :] = tmp_ref[pl.ds(start, rows), :]


def orders_of(kind):
    first, second, *rest = HALVING[kind]
    return (first, second, *rest), (second, first, *rest)


def both_left(mine, peer):
    return jnp.concatenate([mine.T, peer.T], axis=1)


def by_halves(pieces, base, width):
    return [
        jnp.concatenate([r[:, base + x * width : base + (x + 1) * width] for r in pieces], axis=0)
        for x in range(2)
    ]


def put(result, order, x, keep, send):
    blocks = 1 << (len(order) - 1)
    rows = result.shape[0] // blocks
    k = order.index(1)
    run = blocks >> k
    for i in range(1 << k):
        at = (2 * i + x) * run
        ref, at = (keep, at) if at < blocks else (send, at - blocks)
        ref[at * rows : (at + run) * rows] = result[i * run * rows : (i + 1) * run * rows]


def in_kernel(dp, d_ref, acts, acts_peer, mine, peer, keep0, send0, keep1, send1, tmp, *turned):
    width = acts.shape[1]
    tmp[...] = both_left(acts[...], acts_peer[...])
    wide = (mine.shape[1] - width // 2) // 2
    rights = by_halves((mine, peer), 0, wide)
    outs = ((keep0, send0), (keep1, send1))
    for part, order in enumerate(orders_of("in")):
        turn_rows(order, d_ref[0], tmp, turned[part], width // dp, part)
        for x in range(2):
            put(dot(turned[part][...], rights[x]).astype(BF), order, x, *outs[part])


def qkv_kernel(
    dp,
    ids_ref,
    tok,
    tok_prev,
    tok_next,
    ctx,
    ctx_peer,
    mine,
    peer,
    peer2,
    out_mine,
    out_peer,
    sums_ref,
    keep0,
    send0,
    keep1,
    send1,
    total_ref,
    tmp,
    tmp2,
    *turned,
):
    rows, width = tok.shape
    d = ids_ref[0]
    other = jnp.where(ids_ref[1] % 2 == 0, tok_next[...], tok_prev[...])
    tmp[...] = both_left(tok[...], other)
    tmp2[...] = both_left(ctx[...], ctx_peer[...])
    half = peer2.shape[0]
    rights = by_halves((mine, peer.at[:half], peer2), 0, mine.shape[1] // 2)
    outs = by_halves((out_mine, out_peer), 0, out_mine.shape[1] // 2)
    refs = ((keep0, send0), (keep1, send1))
    for part, order in enumerate(orders_of("qkv")):
        turn_rows(order, d, tmp, turned[part], width // dp, part)
        turn_rows(order, d, tmp2, turned[2 + part], width // dp, part)
        for x in range(2):
            result = jnp.concatenate(
                [dot(turned[part][...], rights[x]), dot(turned[2 + part][...], outs[x])], axis=1
            ).astype(BF)
            put(result, order, x, *refs[part])
    total = sums_ref[...] + read_sums(peer, half, width)
    total_ref[...] = total
    pack_sums(total, send0, keep0.shape[0])


def back_kernel(dp, d_ref, hid, hid_peer, feed, feed_peer, keep0, send0, keep1, send1):
    d = d_ref[0]
    chunk = hid.shape[1] // dp
    side = feed.shape[1] // 2
    rows = side // 4
    turned = [feed[...].T, feed_peer[...].T]
    orders = orders_of("back")
    for rel in range(dp):
        span = pl.ds(pl.multiple_of((rel ^ d) * chunk, chunk), chunk)
        result = (dot(turned[0], hid[:, span]) + dot(turned[1], hid_peer[:, span])).astype(BF)
        for x in range(2):
            bits = 2 * x + 4 * rel
            for part, refs in enumerate(((keep0, send0), (keep1, send1))):
                at = 0
                for bit in orders[part]:
                    at = 2 * at + ((bits >> bit) & 1)
                ref, at = refs[at // dp], at % dp
                for h in range(2):
                    start = x * side + h * 2 * rows + part * rows
                    ref[at * rows : (at + 1) * rows, h * chunk : (h + 1) * chunk] = result[
                        start : start + rows
                    ]


def total_of(keep, got):
    return keep[...].astype(F32) + got[: keep.shape[0]].astype(F32)


def step_sums(sums_ref, got, at, total_ref, send, send_at):
    total = sums_ref[...] + read_sums(got, at, sums_ref.shape[1])
    total_ref[...] = total
    if send is not None:
        pack_sums(total, send, send_at)


def first_step(keep0, got0, keep1, got1, *refs):
    if len(refs) == 6:
        sums_ref, new0, send0, new1, send1, total_ref = refs
        step_sums(sums_ref, got0, keep0.shape[0], total_ref, send0, keep0.shape[0] // 2)
    else:
        new0, send0, new1, send1 = refs
    half = keep0.shape[0] // 2
    for keep, got, new, send in ((keep0, got0, new0, send0), (keep1, got1, new1, send1)):
        total = total_of(keep, got).astype(BF)
        new[...] = total[:half]
        send[:half] = total[half:]


def second_step(rows, keep0, got0, keep1, got1, *refs):
    if len(refs) == 4:
        sums_ref, new, send, total_ref = refs
        step_sums(sums_ref, got0, keep0.shape[0], total_ref, send, new.shape[0])
    else:
        new, send = refs
    half = keep0.shape[0] // 2
    for part, (keep, got) in enumerate(((keep0, got0), (keep1, got1))):
        total = total_of(keep, got).astype(BF)
        for b in range(half // rows):
            at = (2 * b + part) * rows
            new[at : at + rows] = total[b * rows : (b + 1) * rows]
            send[at : at + rows] = total[half + b * rows : half + (b + 1) * rows]


def third_step(keep, got, *refs):
    if len(refs) == 4:
        sums_ref, new, send, total_ref = refs
        step_sums(sums_ref, got, keep.shape[0], total_ref, send, new.shape[0])
    else:
        new, send = refs
    half = keep.shape[0] // 2
    total = total_of(keep, got).astype(BF)
    new[...] = total[:half]
    send[:half] = total[half:]


def last_step(kind, keep, got, *refs):
    total = total_of(keep, got)
    if kind == "back":
        chunk = total.shape[1] // 2
        refs[0][...] = jnp.concatenate([total[:, :chunk].T, total[:, chunk:].T], axis=1)
    elif kind == "in":
        refs[0][...] = total
    else:
        sums_ref, qkv_ref, out_ref, inner_ref, *vectors = refs
        qkv_ref[...] = total[:, : qkv_ref.shape[1]]
        out_ref[...] = total[:, qkv_ref.shape[1] :]
        width = sums_ref.shape[1]
        sums = sums_ref[...] + read_sums(got, keep.shape[0], width)
        for i in range(4):
            inner_ref[i * width : (i + 1) * width] = sums[3 + i]
        for row, ref in zip((0, 1, 2, 7, 8, 9, 10, 11), vectors):
            ref[...] = sums[row]


HALVING = {"back": (2, 3, 1, 4), "in": (1, 3, 2, 4), "qkv": (1, 3, 2, 4)}


def flip(value, bit):
    count = lax.axis_size("dp") * lax.axis_size("seq")
    return lax.ppermute(value, BOTH, [(i, i ^ (1 << bit)) for i in range(count)])


class Reduction:
    def __init__(self, kind, parts, sums=None):
        self.kind, self.keeps, self.sums = kind, parts[0::2], sums
        self.at, self.result = 0, None
        self.gots = tuple(flip(v, b) for v, b in zip(parts[1::2], HALVING[kind]))

    def step(self, outs):
        extra = 0 if self.sums is None else SUM_ROWS
        total = self.keeps[0].shape[0]
        width = self.keeps[0].shape[1]
        half = total // 2
        operands = [v for pair in zip(self.keeps, self.gots) for v in pair]
        sums = () if self.sums is None else (shape_of(SUM_ROWS, width, dtype=F32),)
        if self.at == 0:
            kernel = first_step
            shapes = (half, half + extra, half, half)
        elif self.at == 1:
            kernel = functools.partial(second_step, outs["rows"])
            shapes = (total, total + extra)
        else:
            kernel, shapes = third_step, (half, half + extra)
        shapes = tuple(shape_of(n, width) for n in shapes) + sums
        last = self.at > 1 and "last" in outs
        if last:
            kernel = functools.partial(last_step, self.kind)
            shapes = tuple(shape_of(*dims, dtype=F32) for dims in outs["last"])
        if self.sums is not None:
            operands.append(self.sums)
        result = pl.pallas_call(
            kernel,
            name=f"add_{self.kind}_{self.at}",
            cost_estimate=cost(1),
            out_shape=shapes,
            in_specs=[VMEM] * len(operands),
            out_specs=(VMEM,) * len(shapes),
            compiler_params=params(12),
        )(*operands)
        self.at += 1
        if last:
            self.result = result
            return
        if self.sums is not None:
            self.sums = result[-1]
        self.keeps = result[0 : len(shapes) - len(sums) : 2]
        sends = result[1 : len(shapes) - len(sums) : 2]
        bits = HALVING[self.kind]
        bits = bits[1::-1] if self.at == 1 else bits[self.at :]
        self.gots = tuple(flip(v, b) for v, b in zip(sends, bits))


def wait_for(unit, done):
    got, *rest = unit.gots
    if done.result is None:
        keep, *others = done.keeps
        got, keep = lax.optimization_barrier((got, keep))
        done.keeps = (keep, *others)
    else:
        first, *others = done.result
        got, first = lax.optimization_barrier((got, first))
        done.result = (first, *others)
    unit.gots = (got, *rest)


def plain_reduce(left, right):
    dp = lax.axis_size("dp")
    part = jnp.einsum("tk,xtw->xkw", left, right, preferred_element_type=F32).astype(BF)
    part = part[0].astype(F32) + flip(part[1], 1).astype(F32)
    part = part.reshape(dp, left.shape[1] // dp, right.shape[2]).astype(BF)
    part = jnp.take(part, jnp.arange(dp) ^ lax.axis_index("dp"), axis=0)
    for bit in reversed(range(dp.bit_length() - 1)):
        half = part.shape[0] // 2
        part = part[:half].astype(F32) + flip(part[half:], 2 + bit).astype(F32)
        part = part.astype(BF) if bit else part
    return part[0]


def plain_sum(value, low):
    count = lax.axis_size("dp") * lax.axis_size("seq")
    for bit in range(low, count.bit_length() - 1):
        value = value + flip(value, bit)
    return value


def shape_of(*dims, dtype=BF):
    return jax.ShapeDtypeStruct(dims, dtype)


def cost(us):
    return pl.CostEstimate(flops=int(us * 1e6), bytes_accessed=int(us * 1e4), transcendentals=0)


def params(mib):
    return pltpu.CompilerParams(vmem_limit_bytes=mib << 20)


def local(
    tokens,
    segment_ids,
    padding,
    w_qkv,
    b_query,
    b_value,
    w_out,
    b_out,
    ln1_gain,
    ln1_bias,
    w_in,
    b_in,
    w_back,
    b_back,
    ln2_gain,
    ln2_bias,
    out_grad,
):
    seqs, loc, width = tokens.shape
    groups, dp = lax.axis_size("seq"), lax.axis_size("dp")
    dp_bits = dp.bit_length() - 1
    ff = w_in.shape[1]
    rows = seqs * loc
    me = lax.axis_index("seq").astype(jnp.int32).reshape(1)
    d = lax.axis_index("dp").astype(jnp.int32).reshape(1)
    up = [(i, i + 1) for i in range(groups - 1)]
    down = [(i + 1, i) for i in range(groups - 1)]

    def around(value):
        return lax.ppermute(value, "seq", up), lax.ppermute(value, "seq", down)

    flat = tokens.reshape(rows, width)
    tok_prev, tok_next = around(flat)
    vec1 = jnp.concatenate([b_query, b_value, b_out, ln1_gain])
    vec2 = jnp.concatenate([ln1_bias, b_back, ln2_gain, ln2_bias])
    ids = jnp.stack([segment_ids, padding])
    own_qkv, mask, mask_t, wqkv = pl.pallas_call(
        functools.partial(own_kernel, groups),
        name="own_projections",
        cost_estimate=cost(4),
        out_shape=(
            shape_of(rows, 3 * width),
            shape_of(seqs, loc, 3 * loc, dtype=F32),
            shape_of(seqs, loc, 3 * loc, dtype=F32),
            shape_of(*w_qkv.shape),
        ),
        in_specs=[SMEM] + [VMEM] * 3 + [HBM],
        out_specs=(VMEM,) * 4,
        scratch_shapes=[pltpu.SemaphoreType.DMA((3,))],
        compiler_params=params(48),
    )(me, ids, flat, vec1, w_qkv)
    extra = width // groups * 2
    acts_width = ff + 2 * width + extra
    near_qkv, acts, feed_grad, slope, lse, normed, inverse, grad_two, result, feed_keep, small1, *weights = (
        pl.pallas_call(
            functools.partial(forward_kernel, groups),
            name="layer_forward",
            cost_estimate=cost(16),
            out_shape=(
                shape_of(2, rows, 3 * width),
                shape_of(rows, acts_width),
                shape_of(rows, width),
                shape_of(rows, ff),
                shape_of(rows, 128, dtype=F32),
                shape_of(rows, width, dtype=F32),
                shape_of(rows, 1, dtype=F32),
                shape_of(rows, width, dtype=F32),
                shape_of(rows, width),
                shape_of(rows, extra),
                shape_of(3, width, dtype=F32),
                *(shape_of(*w.shape) for w in (w_out, w_in, w_back)),
            ),
            in_specs=[SMEM] + [VMEM] * 9 + [HBM] * 4,
            out_specs=(VMEM,) * 14,
            scratch_shapes=[
                pltpu.VMEM((rows, width), BF),
                pltpu.VMEM((rows, width), BF),
                pltpu.SemaphoreType.DMA((4,)),
            ],
            compiler_params=params(24),
        )(
            me,
            tok_prev,
            tok_next,
            flat,
            own_qkv,
            mask,
            vec1,
            vec2,
            b_in,
            wqkv,
            out_grad.reshape(rows, width),
            w_out,
            w_in,
            w_back,
        )
    )
    acts_peer = flip(acts, 0)

    side = 2 * (ff // groups) + extra
    grads_keep, grads_send, msg, grad_one, small2 = pl.pallas_call(
        functools.partial(backward_kernel, groups),
        name="layer_backward",
            cost_estimate=cost(8),
        out_shape=(
            shape_of(rows, side),
            shape_of(rows, side),
            shape_of(rows, width + 128),
            shape_of(rows, width, dtype=F32),
            shape_of(7, width, dtype=F32),
        ),
        in_specs=[SMEM] + [VMEM] * 11,
        out_specs=(VMEM,) * 5,
        compiler_params=params(12),
    )(me, feed_grad, slope, grad_two, normed, inverse, acts, lse, vec1, *weights)
    msg_prev, msg_next = around(msg)
    grads_peer = flip(grads_send, 0)

    kernels = (width // dp) % 32 == 0 and (ff // dp) % 128 == 0 and dp == 8
    small = width // groups
    wide = ff // groups
    qkv_block = 3 * width // groups
    block_rows = width // dp
    part_rows = dp * block_rows // 2
    base = ff + 2 * width

    def acts_block(i):
        return pl.BlockSpec((rows, width), lambda g: (0, i))

    first_at, ctx_at = ff // width, ff // width + 1
    out_at = 2 * wide // extra
    if kernels:
        back = pl.pallas_call(
            functools.partial(back_kernel, dp),
            name="grad_w_back",
            cost_estimate=cost(3),
            grid=(1,),
            out_shape=(shape_of(part_rows, width),) * 4,
            in_specs=[
                SMEM,
                pl.BlockSpec((rows, ff), lambda i: (0, 0)),
                pl.BlockSpec((rows, ff), lambda i: (0, 0)),
                pl.BlockSpec((rows, extra), lambda i: (0, 0)),
                pl.BlockSpec((rows, extra), lambda i: (0, base // extra)),
            ],
            compiler_params=params(16),
        )(d, acts, acts_peer, feed_keep, acts_peer)
        grads_keep, msg_prev, msg_next = lax.optimization_barrier((grads_keep, msg_prev, msg_next))
        whole = pl.BlockSpec((rows, side), lambda g: (0, 0))
        inner = pl.pallas_call(
            functools.partial(in_kernel, dp),
            name="grad_w_in",
            cost_estimate=cost(4),
            grid=(1,),
            out_shape=(shape_of(part_rows, wide),) * 4,
            in_specs=[SMEM, acts_block(first_at), acts_block(first_at), whole, whole],
            scratch_shapes=[pltpu.VMEM((width, 2 * rows), BF)]
            + [pltpu.VMEM((width // 2, 2 * rows), BF)] * 2,
            compiler_params=params(16),
        )(d, acts, acts_peer, grads_keep, grads_peer)
        red_back = Reduction("back", back)
        red_in = Reduction("in", inner)
        msg_prev, msg_next, keep_a, keep_b = lax.optimization_barrier(
            (msg_prev, msg_next, red_back.keeps[0], red_in.keeps[0])
        )
        red_back.keeps = (keep_a, red_back.keeps[1])
        red_in.keeps = (keep_b, red_in.keeps[1])

    qkv_grad, qkv_keep, qkv_send, qkv_send2, sums = pl.pallas_call(
        functools.partial(attend_back_kernel, groups),
        name="attend_backward",
        cost_estimate=cost(11),
        out_shape=(
            shape_of(rows, 3 * width),
            shape_of(rows, 2 * qkv_block),
            shape_of(loc + SUM_ROWS, 2 * qkv_block),
            shape_of(rows - loc, 2 * qkv_block),
            shape_of(SUM_ROWS, width, dtype=F32),
        ),
        in_specs=[SMEM] + [VMEM] * 9,
        out_specs=(VMEM,) * 5,
        scratch_shapes=[pltpu.VMEM((2, 3, 128, loc), F32)],
        compiler_params=params(16),
    )(me, mask, mask_t, near_qkv, own_qkv, msg_prev, msg, msg_next, small1, small2)
    if kernels:
        red_back.step({})
        qkv_send, keep_a = lax.optimization_barrier((qkv_send, red_back.keeps[0]))
        red_back.keeps = (keep_a, red_back.keeps[1])
    qkv_peer, qkv_peer2 = flip(qkv_send, 0), flip(qkv_send2, 0)
    input_grad = grad_one + dot(qkv_grad, w_qkv, 1, 1)
    if kernels:
        red_in.step({})
        *qkv, sums = pl.pallas_call(
            functools.partial(qkv_kernel, dp),
            name="grad_w_qkv_out",
            cost_estimate=cost(3),
            out_shape=(
                shape_of(part_rows, width),
                shape_of(part_rows + SUM_ROWS, width),
                shape_of(part_rows, width),
                shape_of(part_rows, width),
                shape_of(SUM_ROWS, width, dtype=F32),
            ),
            grid=(1,),
            in_specs=[SMEM]
            + [pl.BlockSpec((rows, width), lambda i: (0, 0))] * 3
            + [acts_block(ctx_at)] * 2
            + [pl.BlockSpec((rows, 2 * qkv_block), lambda i: (0, 0))]
            + [pl.BlockSpec((loc + SUM_ROWS, 2 * qkv_block), lambda i: (0, 0))]
            + [pl.BlockSpec((rows - loc, 2 * qkv_block), lambda i: (0, 0))]
            + [pl.BlockSpec((rows, extra), lambda i: (0, out_at))] * 2
            + [pl.BlockSpec((SUM_ROWS, width), lambda i: (0, 0))],
            scratch_shapes=[pltpu.VMEM((width, 2 * rows), BF)] * 2
            + [pltpu.VMEM((width // 2, 2 * rows), BF)] * 4,
            compiler_params=params(20),
        )(
            jnp.concatenate([d, me]),
            flat,
            tok_prev,
            tok_next,
            acts,
            acts_peer,
            qkv_keep,
            qkv_peer,
            qkv_peer2,
            grads_keep,
            grads_peer,
            sums,
        )
        qkv[3], keep_b = lax.optimization_barrier((qkv[3], red_in.keeps[0]))
        red_in.keeps = (keep_b, red_in.keeps[1])
        red_qkv = Reduction("qkv", qkv, sums)
        units = (red_back, red_in, red_qkv)
        last = (
            ((ff // dp, small),),
            ((block_rows, wide),),
            ((block_rows, qkv_block), (block_rows, small), (ff,)) + ((width,),) * 8,
        )
        done = None
        for k in EVENTS if dp_bits == 3 else [0, 1, 2] * (dp_bits + 1):
            if units[k].at > dp_bits:
                continue
            outs = {"rows": block_rows // 2}
            if units[k].at == dp_bits:
                outs["last"] = last[k]
            if done is not None and done is not units[k]:
                wait_for(units[k], done)
            units[k].step(outs)
            done = units[k]
        g_back = red_back.result[0]
        g_in = red_in.result[0]
        g_qkv, g_out, b_in_g, *vectors = red_qkv.result
    else:

        def by_x(v, w):
            return v.reshape(v.shape[0], 2, w).transpose(1, 0, 2)

        def pile(a, b):
            return jnp.concatenate([a, b], axis=0)

        feeds = by_x(pile(feed_keep, acts_peer[:, base:]), small)
        g_back = plain_reduce(pile(acts[:, :ff], acts_peer[:, :ff]), feeds)
        grads = pile(grads_keep, grads_peer)
        lefts = pile(acts, acts_peer)
        g_in = plain_reduce(lefts[:, ff : ff + width], by_x(grads[:, : 2 * wide], wide))
        g_out = plain_reduce(lefts[:, ff + width : base], by_x(grads[:, 2 * wide :], small))
        other = jnp.where(me[0] % 2 == 0, tok_next, tok_prev)
        grads = by_x(pile(qkv_keep, pile(qkv_peer[:loc], qkv_peer2)), qkv_block)
        g_qkv = plain_reduce(pile(flat, other), grads)
        sums = plain_sum(sums, 0)
        b_in_g = sums[3:7].reshape(-1)
        vectors = [sums[i] for i in (0, 1, 2, 7, 8, 9, 10, 11)]
    b_back_g, gain2, shift2, b_out_g, gain1, shift1, b_q_g, b_v_g = vectors
    shape = (seqs, loc, width)
    return (
        result.reshape(shape),
        input_grad.reshape(shape).astype(BF),
        g_qkv,
        b_q_g,
        b_v_g,
        g_out,
        b_out_g,
        gain1,
        shift1,
        g_in,
        b_in_g,
        g_back,
        b_back_g,
        gain2,
        shift2,
    )


EVENTS = [0, 1, 0, 2, 1, 2, 0, 1, 2, 2]


def solution(mesh):
    row = P("dp", "seq", None)
    in_specs = (row, P("dp", None), P("dp", None)) + (P(),) * 13 + (row,)
    block = P("dp", "seq")
    out_specs = (row, row, block, P(), P(), block, P(), P(), P(), block, P(), block, P(), P(), P())
    return jax.shard_map(local, mesh=mesh, in_specs=in_specs, out_specs=out_specs, check_vma=False)
```

```python
import functools

import jax
import jax.numpy as jnp
from jax import lax
from jax.experimental import pallas as pl
from jax.experimental.pallas import tpu as pltpu
from jax.sharding import PartitionSpec as P

HEADS = 12
HDIM = 64
PAIR = 2 * HDIM
LN_EPS = 1e-12
FAR = -1e9
SUM_ROWS = 16
BOTH = ("dp", "seq")
BF = jnp.bfloat16
F32 = jnp.float32
HBM = pl.BlockSpec(memory_space=pltpu.HBM)
VMEM = pl.BlockSpec(memory_space=pltpu.VMEM)
SMEM = pl.BlockSpec(memory_space=pltpu.SMEM)


def dot(a, b, ca=1, cb=0):
    return lax.dot_general(a, b, (((ca,), (cb,)), ((), ())), preferred_element_type=F32)


def mean_of(v):
    return jnp.mean(v, axis=-1, keepdims=True)


def norm_parts(values):
    center = values - mean_of(values)
    inverse = lax.rsqrt(mean_of(center * center) + LN_EPS)
    return center * inverse, inverse


def norm_pull(upstream, normed, inverse, gain):
    scaled = upstream * gain
    return (scaled - mean_of(scaled) - normed * mean_of(scaled * normed)) * inverse


def col_sum(v):
    return jnp.sum(v, axis=0, keepdims=True)


def mask_of(me, groups, ids_ref, row, loc):
    own = pl.ds(pl.multiple_of(me * loc, loc), loc)
    seg_ref, pad_ref = ids_ref.at[0], ids_ref.at[1]
    seg_t = jnp.broadcast_to(seg_ref[row : row + 1, own].astype(F32), (loc, loc)).T
    pad_t = jnp.broadcast_to(pad_ref[row : row + 1, own].astype(F32), (loc, loc)).T
    eye = lax.broadcasted_iota(jnp.int32, (loc, loc), 0) == lax.broadcasted_iota(
        jnp.int32, (loc, loc), 1
    )
    keys, queries = [], []
    for block in range(3):
        at = me + block - 1
        out_of = jnp.where((at < 0) | (at >= groups), FAR, 0.0).astype(F32)
        at = jnp.clip(at, 0, groups - 1)
        span = pl.ds(pl.multiple_of(at * loc, loc), loc)
        seg_b = seg_ref[row : row + 1, span].astype(F32)
        pad_b = pad_ref[row : row + 1, span].astype(F32)
        same = seg_t == seg_b
        seen, seen_t = pad_b == 0.0, pad_t == 0.0
        if block == 1:
            seen, seen_t = seen | eye, seen_t | eye
        keys.append(jnp.where(same & seen, 0.0, FAR) + out_of)
        queries.append(jnp.where(same & seen_t, 0.0, FAR) + out_of)
    return jnp.concatenate(keys, axis=1), jnp.concatenate(queries, axis=1)


def split_pair(v, low):
    zero = jnp.zeros_like(v)
    return jnp.concatenate([jnp.where(low, v, zero), jnp.where(low, zero, v)], axis=0)


def join_pair(v, low):
    half = v.shape[0] // 2
    return jnp.where(low, v[:half], v[half:])


def own_kernel(
    groups, me_ref, ids_ref, tok_ref, vec_ref, wqkv_hbm, qkv_ref, mask_ref, mask_t_ref, wqkv, sems
):
    me = me_ref[0]
    rows, width = tok_ref.shape
    loc = rows // 2
    copies = []
    for part in range(3):
        cols = pl.ds(part * width, width)
        copies.append(pltpu.make_async_copy(wqkv_hbm.at[:, cols], wqkv.at[:, cols], sems.at[part]))
        copies[-1].start()
    for row in range(2):
        mask_ref[row], mask_t_ref[row] = mask_of(me, groups, ids_ref, row, loc)
    vec = vec_ref[...].reshape(1, -1)
    biases = (vec[:, :width], 0.0, vec[:, width : 2 * width])
    for part in range(3):
        copies[part].wait()
        cols = slice(part * width, (part + 1) * width)
        qkv_ref[:, cols] = (dot(tok_ref[...], wqkv[:, cols]) + biases[part]).astype(BF)


def forward_kernel(
    groups,
    me_ref,
    tok_prev,
    tok_next,
    tok_own,
    own_ref,
    mask_ref,
    vec_ref,
    vec2_ref,
    b_in_ref,
    wqkv,
    og_hbm,
    wout_hbm,
    win_hbm,
    wback_hbm,
    qkv_ref,
    acts_ref,
    feed_ref,
    slope_ref,
    lse_ref,
    normed_ref,
    inv_ref,
    gtwo_ref,
    out_ref,
    keep_ref,
    small_ref,
    wout,
    win,
    wback,
    ctx_ref,
    og_ref,
    sems,
):
    me = me_ref[0]
    rows, width = tok_own.shape
    loc = rows // 2
    ff = win.shape[1]
    pairs = ((wout_hbm, wout), (win_hbm, win), (wback_hbm, wback), (og_hbm, og_ref))
    copies = [pltpu.make_async_copy(a, b, sems.at[i]) for i, (a, b) in enumerate(pairs)]
    for copy in copies:
        copy.start()
    vec, vec2 = vec_ref[...].reshape(1, -1), vec2_ref[...].reshape(1, -1)
    b_query, b_value, b_out, gain1 = (vec[:, i * width : (i + 1) * width] for i in range(4))
    shift1, b_back, gain2, shift2 = (vec2[:, i * width : (i + 1) * width] for i in range(4))
    b_in = b_in_ref[...].reshape(1, -1)
    b_qkv = (b_query, 0.0, b_value)
    for part in range(3):
        cols = slice(part * width, (part + 1) * width)
        for block, tok in enumerate((tok_prev, tok_next)):
            qkv_ref[block, :, cols] = (dot(tok[...], wqkv[:, cols]) + b_qkv[part]).astype(BF)
    blocks = (qkv_ref.at[0], own_ref, qkv_ref.at[1])
    low = lax.broadcasted_iota(jnp.int32, (loc, PAIR), 1) < HDIM
    lanes = lax.broadcasted_iota(jnp.int32, (loc, 128), 1)

    def attend(p, totals):
        spans = [pl.ds(pl.multiple_of(p * PAIR + part * width, PAIR), PAIR) for part in range(3)]
        result = []
        for row in range(2):
            at = slice(row * loc, (row + 1) * loc)
            q2 = split_pair(own_ref[at, spans[0]], low) * jnp.asarray(HDIM**-0.5, BF)
            k3 = jnp.concatenate([b[at, spans[1]] for b in blocks], axis=0)
            v3 = jnp.concatenate([b[at, spans[2]] for b in blocks], axis=0)
            mask = mask_ref[row]
            scores = dot(q2, k3, 1, 1) + jnp.concatenate([mask, mask], axis=0)
            top = jnp.max(scores, axis=-1, keepdims=True)
            powers = jnp.exp(scores - top)
            total = jnp.sum(powers, axis=-1, keepdims=True)
            probs = (powers * (1.0 / total)).astype(BF)
            ctx_ref[at, pl.ds(pl.multiple_of(p * PAIR, PAIR), PAIR)] = join_pair(
                dot(probs, v3), low
            ).astype(BF)
            lse = top + jnp.log(total)
            old = totals[row]
            old = jnp.where(lanes == 2 * p, lse[:loc], old)
            result.append(jnp.where(lanes == 2 * p + 1, lse[loc:], old))
        return tuple(result)

    zero = jnp.zeros((loc, 128), F32)
    totals = lax.fori_loop(0, HEADS // 2, attend, (zero, zero), unroll=6)
    lse_ref[:loc, :] = totals[0]
    lse_ref[loc:, :] = totals[1]
    context = ctx_ref[...]
    acts_ref[:, ff + width : ff + 2 * width] = context
    copies[0].wait()
    branch = dot(context, wout[...]) + b_out
    normed, inverse = norm_parts(tok_own[...].astype(F32) + branch)
    normed_ref[...] = normed
    inv_ref[...] = inverse
    first = normed * gain1 + shift1
    first_low = first.astype(BF)
    acts_ref[:, ff : ff + width] = first_low
    copies[1].wait()
    copies[2].wait()
    feed = first + b_back
    for c in range(ff // width):
        cols = slice(c * width, (c + 1) * width)
        before = dot(first_low, win[:, cols]) + b_in[:, cols]
        cdf = 0.5 + 0.5 * lax.erf(before * (0.5**0.5))
        hidden = (before * cdf).astype(BF)
        acts_ref[:, cols] = hidden
        bell = jnp.exp(-0.5 * before * before) * (0.3989422804014327)
        slope_ref[:, cols] = (cdf + before * bell).astype(BF)
        feed = feed + dot(hidden, wback[cols, :])
    normed2, inverse2 = norm_parts(feed)
    out_ref[...] = (normed2 * gain2 + shift2).astype(BF)
    copies[3].wait()
    upstream = og_ref[...].astype(F32)
    grad_two = norm_pull(upstream, normed2, inverse2, gain2)
    gtwo_ref[...] = grad_two
    feed_grad = grad_two.astype(BF)
    feed_ref[...] = feed_grad
    small_ref[0:1, :] = col_sum(feed_grad.astype(F32))
    small_ref[1:2, :] = col_sum(upstream * normed2)
    small_ref[2:3, :] = col_sum(upstream)
    base = ff + 2 * width
    block = width // groups
    for s in range(groups):
        rel = s ^ me
        piece = feed_grad[:, s * block : (s + 1) * block]
        for i in range(groups // 2):

            @pl.when(rel == 2 * i)
            def _():
                keep_ref[:, i * block : (i + 1) * block] = piece

            @pl.when(rel == 2 * i + 1)
            def _():
                acts_ref[:, base + i * block : base + (i + 1) * block] = piece


def backward_kernel(
    groups,
    me_ref,
    feed_ref,
    slope_ref,
    gtwo_ref,
    normed_ref,
    inv_ref,
    acts_ref,
    lse_ref,
    vec_ref,
    wout,
    win,
    wback,
    keep_ref,
    send_ref,
    msg_ref,
    gone_ref,
    small_ref,
):
    me = me_ref[0]
    rows, width = feed_ref.shape
    ff = win.shape[1]
    block = ff // groups
    spans = [pl.ds(pl.multiple_of((i ^ me) * block, block), block) for i in range(groups)]
    feed_grad = feed_ref[...]
    first_grad = gtwo_ref[...]
    for i, span in enumerate(spans):
        s = i ^ me
        hidden_grad = dot(feed_grad, wback[span, :], 1, 1)
        before_grad = (hidden_grad * slope_ref[:, span].astype(F32)).astype(BF)
        small_ref[pl.ds(s, 1), :] = col_sum(before_grad.astype(F32))
        target = send_ref if i % 2 else keep_ref
        target[:, (i // 2) * block : (i // 2 + 1) * block] = before_grad
        first_grad = first_grad + dot(before_grad, win[:, span], 1, 1)
    normed = normed_ref[...]
    grad_one = norm_pull(first_grad, normed, inv_ref[...], vec_ref[3 * width :].reshape(1, -1))
    gone_ref[...] = grad_one
    branch_grad = grad_one.astype(BF)
    small_ref[4:5, :] = col_sum(branch_grad.astype(F32))
    small_ref[5:6, :] = col_sum(first_grad * normed)
    small_ref[6:7, :] = col_sum(first_grad)
    context_grad = dot(branch_grad, wout[...], 1, 1).astype(BF)
    msg_ref[:, :width] = context_grad
    product = context_grad.astype(F32) * acts_ref[:, ff + width : ff + 2 * width].astype(F32)
    lanes = lax.broadcasted_iota(jnp.int32, (rows, 128), 1)
    low = lanes < HDIM
    delta = jnp.zeros((rows, 128), F32)
    for p in range(HEADS // 2):
        tile = product[:, p * PAIR : (p + 1) * PAIR]
        both = jnp.sum(tile, axis=-1, keepdims=True)
        even = jnp.sum(jnp.where(low, tile, 0.0), axis=-1, keepdims=True)
        delta = jnp.where(lanes == 2 * p, even, delta)
        delta = jnp.where(lanes == 2 * p + 1, both - even, delta)
    packed = jnp.zeros((rows, 128), F32)
    shift = 0
    for value in (lse_ref[...], delta):
        for _ in range(3):
            term = value.astype(BF).astype(F32)
            packed = packed + (pltpu.roll(term, shift, 1) if shift else term)
            value = value - term
            shift += 16
    msg_ref[:, width:] = packed.astype(BF)
    base = 2 * block
    small = width // groups
    for s in range(groups):
        rel = s ^ me
        piece = branch_grad[:, s * small : (s + 1) * small]
        for i in range(groups // 2):

            @pl.when(rel == 2 * i)
            def _():
                keep_ref[:, base + i * small : base + (i + 1) * small] = piece

            @pl.when(rel == 2 * i + 1)
            def _():
                send_ref[:, base + i * small : base + (i + 1) * small] = piece


def attend_back_kernel(
    groups,
    me_ref,
    mask_ref,
    mask_t_ref,
    near_ref,
    own_ref,
    msg_prev,
    msg_own,
    msg_next,
    small1_ref,
    small2_ref,
    all_ref,
    keep_ref,
    send_ref,
    send2_ref,
    sums_ref,
    info_t_ref,
):
    me = me_ref[0]
    rows = msg_own.shape[0]
    width = own_ref.shape[1] // 3
    loc = rows // 2
    msgs = (msg_prev, msg_own, msg_next)
    blocks = (near_ref.at[0], own_ref, near_ref.at[1])
    own_info = []
    for row in range(2):
        at = slice(row * loc, (row + 1) * loc)
        for b in range(3):
            raw = msgs[b][at, width:].astype(F32)
            info = raw + pltpu.roll(raw, 112, 1) + pltpu.roll(raw, 96, 1)
            if b == 1:
                own_info.append(info)
            info_t_ref[row, b] = info.T
    low = lax.broadcasted_iota(jnp.int32, (loc, PAIR), 1) < HDIM
    lanes = lax.broadcasted_iota(jnp.int32, (loc, 128), 1)
    scale = jnp.asarray(HDIM**-0.5, BF)

    def column(info, lane):
        return jnp.sum(jnp.where(lanes == lane, info, 0.0), axis=-1, keepdims=True)

    def heads(p, carry):
        spans = [pl.ds(pl.multiple_of(p * PAIR + part * width, PAIR), PAIR) for part in range(3)]
        for row in range(2):
            at = slice(row * loc, (row + 1) * loc)
            info = own_info[row]
            lse2 = jnp.concatenate([column(info, 2 * p), column(info, 2 * p + 1)], axis=0)
            delta2 = jnp.concatenate([column(info, 48 + 2 * p), column(info, 49 + 2 * p)], axis=0)
            q3 = jnp.concatenate([b[at, spans[0]] for b in blocks], axis=0)
            k3 = jnp.concatenate([b[at, spans[1]] for b in blocks], axis=0)
            v3 = jnp.concatenate([b[at, spans[2]] for b in blocks], axis=0)
            u3 = jnp.concatenate([m[at, spans[0]] for m in msgs], axis=0)
            mask = mask_ref[row]
            scores = dot(split_pair(q3[loc : 2 * loc], low) * scale, k3, 1, 1)
            probs = jnp.exp(scores + jnp.concatenate([mask, mask], axis=0) - lse2)
            prob_grad = dot(split_pair(u3[loc : 2 * loc], low), v3, 1, 1)
            score_grad = (probs * (prob_grad - delta2)).astype(BF)
            query_grad = join_pair(dot(score_grad, k3), low) * HDIM**-0.5
            all_ref[at, spans[0]] = query_grad.astype(BF)

            def line(which):
                halves = []
                for h in range(2):
                    parts = [info_t_ref[row, b, pl.ds(which + 2 * p + h, 1), :] for b in range(3)]
                    halves.append(
                        jnp.broadcast_to(jnp.concatenate(parts, axis=1), (loc, 3 * loc))
                    )
                return jnp.concatenate(halves, axis=0)

            mask_t = mask_t_ref[row]
            scores_t = dot(split_pair(k3[loc : 2 * loc], low) * scale, q3, 1, 1)
            probs_t = jnp.exp(scores_t + jnp.concatenate([mask_t, mask_t], axis=0) - line(0))
            value_grad = join_pair(dot(probs_t.astype(BF), u3), low)
            prob_grad_t = dot(split_pair(v3[loc : 2 * loc], low), u3, 1, 1)
            score_grad_t = (probs_t * (prob_grad_t - line(48))).astype(BF)
            key_grad = join_pair(dot(score_grad_t, q3), low) * HDIM**-0.5
            all_ref[at, spans[1]] = key_grad.astype(BF)
            all_ref[at, spans[2]] = value_grad.astype(BF)
        return carry

    lax.fori_loop(0, HEADS // 2, heads, 0, unroll=6)
    value_at = 2 * width
    sums_ref[...] = jnp.concatenate(
        [
            small1_ref[...],
            small2_ref[...],
            col_sum(all_ref[:, :width].astype(F32)),
            col_sum(all_ref[:, value_at:].astype(F32)),
            jnp.zeros((SUM_ROWS - 12, width), F32),
        ],
        axis=0,
    )
    send_ref[loc:, :] = jnp.zeros((SUM_ROWS, send_ref.shape[1]), BF)
    pack_sums(sums_ref[...], send_ref, loc)
    block = 3 * width // groups
    for s in range(groups):
        rel = s ^ me
        piece = all_ref[:, s * block : (s + 1) * block]
        for i in range(groups // 2):

            @pl.when(rel == 2 * i)
            def _():
                keep_ref[:, i * block : (i + 1) * block] = piece

            @pl.when(rel == 2 * i + 1)
            def _():
                send_ref[:loc, i * block : (i + 1) * block] = piece[:loc]
                send2_ref[:, i * block : (i + 1) * block] = piece[loc:]


def pack_sums(value, ref, at):
    ref[at : at + SUM_ROWS, : value.shape[1]] = value.astype(BF)


def read_sums(ref, at, width):
    return ref[at : at + SUM_ROWS, :width].astype(F32)


def turn_rows(order, d, tmp_ref, turned_ref, block_rows, part):
    rows = block_rows // 2
    bits = [bit - 2 for bit in order if bit != 1]
    for j in range(1 << len(bits)):
        rel = sum(((j >> (len(bits) - 1 - k)) & 1) << bit for k, bit in enumerate(bits))
        start = pl.multiple_of((rel ^ d) * block_rows + part * rows, rows)
        turned_ref[j * rows : (j + 1) * rows, :] = tmp_ref[pl.ds(start, rows), :]


def orders_of(kind):
    first, second, *rest = HALVING[kind]
    return (first, second, *rest), (second, first, *rest)


def both_left(mine, peer):
    return jnp.concatenate([mine.T, peer.T], axis=1)


def by_halves(pieces, base, width):
    return [
        jnp.concatenate([r[:, base + x * width : base + (x + 1) * width] for r in pieces], axis=0)
        for x in range(2)
    ]


def put(result, order, x, keep, send):
    blocks = 1 << (len(order) - 1)
    rows = result.shape[0] // blocks
    k = order.index(1)
    run = blocks >> k
    for i in range(1 << k):
        at = (2 * i + x) * run
        ref, at = (keep, at) if at < blocks else (send, at - blocks)
        ref[at * rows : (at + run) * rows] = result[i * run * rows : (i + 1) * run * rows]


def in_kernel(dp, d_ref, acts, acts_peer, mine, peer, keep0, send0, keep1, send1, tmp, *turned):
    width = acts.shape[1]
    tmp[...] = both_left(acts[...], acts_peer[...])
    wide = (mine.shape[1] - width // 2) // 2
    rights = by_halves((mine, peer), 0, wide)
    outs = ((keep0, send0), (keep1, send1))
    for part, order in enumerate(orders_of("in")):
        turn_rows(order, d_ref[0], tmp, turned[part], width // dp, part)
        for x in range(2):
            put(dot(turned[part][...], rights[x]).astype(BF), order, x, *outs[part])


def qkv_kernel(
    dp,
    ids_ref,
    tok,
    tok_prev,
    tok_next,
    ctx,
    ctx_peer,
    mine,
    peer,
    peer2,
    out_mine,
    out_peer,
    sums_ref,
    keep0,
    send0,
    keep1,
    send1,
    total_ref,
    tmp,
    tmp2,
    *turned,
):
    rows, width = tok.shape
    d = ids_ref[0]
    other = jnp.where(ids_ref[1] % 2 == 0, tok_next[...], tok_prev[...])
    tmp[...] = both_left(tok[...], other)
    tmp2[...] = both_left(ctx[...], ctx_peer[...])
    half = peer2.shape[0]
    rights = by_halves((mine, peer.at[:half], peer2), 0, mine.shape[1] // 2)
    outs = by_halves((out_mine, out_peer), 0, out_mine.shape[1] // 2)
    refs = ((keep0, send0), (keep1, send1))
    for part, order in enumerate(orders_of("qkv")):
        turn_rows(order, d, tmp, turned[part], width // dp, part)
        turn_rows(order, d, tmp2, turned[2 + part], width // dp, part)
        for x in range(2):
            result = jnp.concatenate(
                [dot(turned[part][...], rights[x]), dot(turned[2 + part][...], outs[x])], axis=1
            ).astype(BF)
            put(result, order, x, *refs[part])
    total = sums_ref[...] + read_sums(peer, half, width)
    total_ref[...] = total
    pack_sums(total, send0, keep0.shape[0])


def back_kernel(dp, d_ref, hid, hid_peer, feed, feed_peer, keep0, send0, keep1, send1):
    d = d_ref[0]
    chunk = hid.shape[1] // dp
    side = feed.shape[1] // 2
    rows = side // 4
    turned = [feed[...].T, feed_peer[...].T]
    orders = orders_of("back")
    for rel in range(dp):
        span = pl.ds(pl.multiple_of((rel ^ d) * chunk, chunk), chunk)
        result = (dot(turned[0], hid[:, span]) + dot(turned[1], hid_peer[:, span])).astype(BF)
        for x in range(2):
            bits = 2 * x + 4 * rel
            for part, refs in enumerate(((keep0, send0), (keep1, send1))):
                at = 0
                for bit in orders[part]:
                    at = 2 * at + ((bits >> bit) & 1)
                ref, at = refs[at // dp], at % dp
                for h in range(2):
                    start = x * side + h * 2 * rows + part * rows
                    ref[at * rows : (at + 1) * rows, h * chunk : (h + 1) * chunk] = result[
                        start : start + rows
                    ]


def total_of(keep, got):
    return keep[...].astype(F32) + got[: keep.shape[0]].astype(F32)


def step_sums(sums_ref, got, at, total_ref, send, send_at):
    total = sums_ref[...] + read_sums(got, at, sums_ref.shape[1])
    total_ref[...] = total
    if send is not None:
        pack_sums(total, send, send_at)


def first_step(keep0, got0, keep1, got1, *refs):
    if len(refs) == 6:
        sums_ref, new0, send0, new1, send1, total_ref = refs
        step_sums(sums_ref, got0, keep0.shape[0], total_ref, send0, keep0.shape[0] // 2)
    else:
        new0, send0, new1, send1 = refs
    half = keep0.shape[0] // 2
    for keep, got, new, send in ((keep0, got0, new0, send0), (keep1, got1, new1, send1)):
        total = total_of(keep, got).astype(BF)
        new[...] = total[:half]
        send[:half] = total[half:]


def second_step(rows, keep0, got0, keep1, got1, *refs):
    if len(refs) == 4:
        sums_ref, new, send, total_ref = refs
        step_sums(sums_ref, got0, keep0.shape[0], total_ref, send, new.shape[0])
    else:
        new, send = refs
    half = keep0.shape[0] // 2
    for part, (keep, got) in enumerate(((keep0, got0), (keep1, got1))):
        total = total_of(keep, got).astype(BF)
        for b in range(half // rows):
            at = (2 * b + part) * rows
            new[at : at + rows] = total[b * rows : (b + 1) * rows]
            send[at : at + rows] = total[half + b * rows : half + (b + 1) * rows]


def third_step(keep, got, *refs):
    if len(refs) == 4:
        sums_ref, new, send, total_ref = refs
        step_sums(sums_ref, got, keep.shape[0], total_ref, send, new.shape[0])
    else:
        new, send = refs
    half = keep.shape[0] // 2
    total = total_of(keep, got).astype(BF)
    new[...] = total[:half]
    send[:half] = total[half:]


def last_step(kind, keep, got, *refs):
    total = total_of(keep, got)
    if kind == "back":
        chunk = total.shape[1] // 2
        refs[0][...] = jnp.concatenate([total[:, :chunk].T, total[:, chunk:].T], axis=1)
    elif kind == "in":
        refs[0][...] = total
    else:
        sums_ref, qkv_ref, out_ref, inner_ref, *vectors = refs
        qkv_ref[...] = total[:, : qkv_ref.shape[1]]
        out_ref[...] = total[:, qkv_ref.shape[1] :]
        width = sums_ref.shape[1]
        sums = sums_ref[...] + read_sums(got, keep.shape[0], width)
        for i in range(4):
            inner_ref[i * width : (i + 1) * width] = sums[3 + i]
        for row, ref in zip((0, 1, 2, 7, 8, 9, 10, 11), vectors):
            ref[...] = sums[row]


HALVING = {"back": (2, 3, 1, 4), "in": (1, 3, 2, 4), "qkv": (1, 3, 2, 4)}


def flip(value, bit):
    count = lax.axis_size("dp") * lax.axis_size("seq")
    return lax.ppermute(value, BOTH, [(i, i ^ (1 << bit)) for i in range(count)])


class Reduction:
    def __init__(self, kind, parts, sums=None):
        self.kind, self.keeps, self.sums = kind, parts[0::2], sums
        self.at, self.result = 0, None
        self.gots = tuple(flip(v, b) for v, b in zip(parts[1::2], HALVING[kind]))

    def step(self, outs):
        extra = 0 if self.sums is None else SUM_ROWS
        total = self.keeps[0].shape[0]
        width = self.keeps[0].shape[1]
        half = total // 2
        operands = [v for pair in zip(self.keeps, self.gots) for v in pair]
        sums = () if self.sums is None else (shape_of(SUM_ROWS, width, dtype=F32),)
        if self.at == 0:
            kernel = first_step
            shapes = (half, half + extra, half, half)
        elif self.at == 1:
            kernel = functools.partial(second_step, outs["rows"])
            shapes = (total, total + extra)
        else:
            kernel, shapes = third_step, (half, half + extra)
        shapes = tuple(shape_of(n, width) for n in shapes) + sums
        last = self.at > 1 and "last" in outs
        if last:
            kernel = functools.partial(last_step, self.kind)
            shapes = tuple(shape_of(*dims, dtype=F32) for dims in outs["last"])
        if self.sums is not None:
            operands.append(self.sums)
        result = pl.pallas_call(
            kernel,
            name=f"add_{self.kind}_{self.at}",
            cost_estimate=cost(1),
            out_shape=shapes,
            in_specs=[VMEM] * len(operands),
            out_specs=(VMEM,) * len(shapes),
            compiler_params=params(12),
        )(*operands)
        self.at += 1
        if last:
            self.result = result
            return
        if self.sums is not None:
            self.sums = result[-1]
        self.keeps = result[0 : len(shapes) - len(sums) : 2]
        sends = result[1 : len(shapes) - len(sums) : 2]
        bits = HALVING[self.kind]
        bits = bits[1::-1] if self.at == 1 else bits[self.at :]
        self.gots = tuple(flip(v, b) for v, b in zip(sends, bits))


def wait_for(unit, done):
    got, *rest = unit.gots
    if done.result is None:
        keep, *others = done.keeps
        got, keep = lax.optimization_barrier((got, keep))
        done.keeps = (keep, *others)
    else:
        first, *others = done.result
        got, first = lax.optimization_barrier((got, first))
        done.result = (first, *others)
    unit.gots = (got, *rest)


def plain_reduce(left, right):
    dp = lax.axis_size("dp")
    part = jnp.einsum("tk,xtw->xkw", left, right, preferred_element_type=F32).astype(BF)
    part = part[0].astype(F32) + flip(part[1], 1).astype(F32)
    part = part.reshape(dp, left.shape[1] // dp, right.shape[2]).astype(BF)
    part = jnp.take(part, jnp.arange(dp) ^ lax.axis_index("dp"), axis=0)
    for bit in reversed(range(dp.bit_length() - 1)):
        half = part.shape[0] // 2
        part = part[:half].astype(F32) + flip(part[half:], 2 + bit).astype(F32)
        part = part.astype(BF) if bit else part
    return part[0]


def plain_sum(value, low):
    count = lax.axis_size("dp") * lax.axis_size("seq")
    for bit in range(low, count.bit_length() - 1):
        value = value + flip(value, bit)
    return value


def shape_of(*dims, dtype=BF):
    return jax.ShapeDtypeStruct(dims, dtype)


def cost(us):
    return pl.CostEstimate(flops=int(us * 1e6), bytes_accessed=int(us * 1e4), transcendentals=0)


def params(mib):
    return pltpu.CompilerParams(vmem_limit_bytes=mib << 20)


def local(
    tokens,
    segment_ids,
    padding,
    w_qkv,
    b_query,
    b_value,
    w_out,
    b_out,
    ln1_gain,
    ln1_bias,
    w_in,
    b_in,
    w_back,
    b_back,
    ln2_gain,
    ln2_bias,
    out_grad,
):
    seqs, loc, width = tokens.shape
    groups, dp = lax.axis_size("seq"), lax.axis_size("dp")
    dp_bits = dp.bit_length() - 1
    ff = w_in.shape[1]
    rows = seqs * loc
    me = lax.axis_index("seq").astype(jnp.int32).reshape(1)
    d = lax.axis_index("dp").astype(jnp.int32).reshape(1)
    up = [(i, i + 1) for i in range(groups - 1)]
    down = [(i + 1, i) for i in range(groups - 1)]

    def around(value):
        return lax.ppermute(value, "seq", up), lax.ppermute(value, "seq", down)

    flat = tokens.reshape(rows, width)
    tok_prev, tok_next = around(flat)
    vec1 = jnp.concatenate([b_query, b_value, b_out, ln1_gain])
    vec2 = jnp.concatenate([ln1_bias, b_back, ln2_gain, ln2_bias])
    ids = jnp.stack([segment_ids, padding])
    own_qkv, mask, mask_t, wqkv = pl.pallas_call(
        functools.partial(own_kernel, groups),
        name="own_projections",
        cost_estimate=cost(4),
        out_shape=(
            shape_of(rows, 3 * width),
            shape_of(seqs, loc, 3 * loc, dtype=F32),
            shape_of(seqs, loc, 3 * loc, dtype=F32),
            shape_of(*w_qkv.shape),
        ),
        in_specs=[SMEM] + [VMEM] * 3 + [HBM],
        out_specs=(VMEM,) * 4,
        scratch_shapes=[pltpu.SemaphoreType.DMA((3,))],
        compiler_params=params(48),
    )(me, ids, flat, vec1, w_qkv)
    extra = width // groups * 2
    acts_width = ff + 2 * width + extra
    near_qkv, acts, feed_grad, slope, lse, normed, inverse, grad_two, result, feed_keep, small1, *weights = (
        pl.pallas_call(
            functools.partial(forward_kernel, groups),
            name="layer_forward",
            cost_estimate=cost(16),
            out_shape=(
                shape_of(2, rows, 3 * width),
                shape_of(rows, acts_width),
                shape_of(rows, width),
                shape_of(rows, ff),
                shape_of(rows, 128, dtype=F32),
                shape_of(rows, width, dtype=F32),
                shape_of(rows, 1, dtype=F32),
                shape_of(rows, width, dtype=F32),
                shape_of(rows, width),
                shape_of(rows, extra),
                shape_of(3, width, dtype=F32),
                *(shape_of(*w.shape) for w in (w_out, w_in, w_back)),
            ),
            in_specs=[SMEM] + [VMEM] * 9 + [HBM] * 4,
            out_specs=(VMEM,) * 14,
            scratch_shapes=[
                pltpu.VMEM((rows, width), BF),
                pltpu.VMEM((rows, width), BF),
                pltpu.SemaphoreType.DMA((4,)),
            ],
            compiler_params=params(24),
        )(
            me,
            tok_prev,
            tok_next,
            flat,
            own_qkv,
            mask,
            vec1,
            vec2,
            b_in,
            wqkv,
            out_grad.reshape(rows, width),
            w_out,
            w_in,
            w_back,
        )
    )
    acts_peer = flip(acts, 0)

    side = 2 * (ff // groups) + extra
    grads_keep, grads_send, msg, grad_one, small2 = pl.pallas_call(
        functools.partial(backward_kernel, groups),
        name="layer_backward",
            cost_estimate=cost(8),
        out_shape=(
            shape_of(rows, side),
            shape_of(rows, side),
            shape_of(rows, width + 128),
            shape_of(rows, width, dtype=F32),
            shape_of(7, width, dtype=F32),
        ),
        in_specs=[SMEM] + [VMEM] * 11,
        out_specs=(VMEM,) * 5,
        compiler_params=params(12),
    )(me, feed_grad, slope, grad_two, normed, inverse, acts, lse, vec1, *weights)
    msg_prev, msg_next = around(msg)
    grads_peer = flip(grads_send, 0)

    kernels = (width // dp) % 32 == 0 and (ff // dp) % 128 == 0 and dp == 8
    small = width // groups
    wide = ff // groups
    qkv_block = 3 * width // groups
    block_rows = width // dp
    part_rows = dp * block_rows // 2
    base = ff + 2 * width

    def acts_block(i):
        return pl.BlockSpec((rows, width), lambda g: (0, i))

    first_at, ctx_at = ff // width, ff // width + 1
    out_at = 2 * wide // extra
    if kernels:
        back = pl.pallas_call(
            functools.partial(back_kernel, dp),
            name="grad_w_back",
            cost_estimate=cost(3),
            grid=(1,),
            out_shape=(shape_of(part_rows, width),) * 4,
            in_specs=[
                SMEM,
                pl.BlockSpec((rows, ff), lambda i: (0, 0)),
                pl.BlockSpec((rows, ff), lambda i: (0, 0)),
                pl.BlockSpec((rows, extra), lambda i: (0, 0)),
                pl.BlockSpec((rows, extra), lambda i: (0, base // extra)),
            ],
            compiler_params=params(16),
        )(d, acts, acts_peer, feed_keep, acts_peer)
        grads_keep, msg_prev, msg_next = lax.optimization_barrier((grads_keep, msg_prev, msg_next))
        whole = pl.BlockSpec((rows, side), lambda g: (0, 0))
        inner = pl.pallas_call(
            functools.partial(in_kernel, dp),
            name="grad_w_in",
            cost_estimate=cost(4),
            grid=(1,),
            out_shape=(shape_of(part_rows, wide),) * 4,
            in_specs=[SMEM, acts_block(first_at), acts_block(first_at), whole, whole],
            scratch_shapes=[pltpu.VMEM((width, 2 * rows), BF)]
            + [pltpu.VMEM((width // 2, 2 * rows), BF)] * 2,
            compiler_params=params(16),
        )(d, acts, acts_peer, grads_keep, grads_peer)
        red_back = Reduction("back", back)
        red_in = Reduction("in", inner)
        msg_prev, msg_next, keep_a, keep_b = lax.optimization_barrier(
            (msg_prev, msg_next, red_back.keeps[0], red_in.keeps[0])
        )
        red_back.keeps = (keep_a, red_back.keeps[1])
        red_in.keeps = (keep_b, red_in.keeps[1])

    qkv_grad, qkv_keep, qkv_send, qkv_send2, sums = pl.pallas_call(
        functools.partial(attend_back_kernel, groups),
        name="attend_backward",
        cost_estimate=cost(11),
        out_shape=(
            shape_of(rows, 3 * width),
            shape_of(rows, 2 * qkv_block),
            shape_of(loc + SUM_ROWS, 2 * qkv_block),
            shape_of(rows - loc, 2 * qkv_block),
            shape_of(SUM_ROWS, width, dtype=F32),
        ),
        in_specs=[SMEM] + [VMEM] * 9,
        out_specs=(VMEM,) * 5,
        scratch_shapes=[pltpu.VMEM((2, 3, 128, loc), F32)],
        compiler_params=params(16),
    )(me, mask, mask_t, near_qkv, own_qkv, msg_prev, msg, msg_next, small1, small2)
    if kernels:
        red_back.step({})
        qkv_send, keep_a = lax.optimization_barrier((qkv_send, red_back.keeps[0]))
        red_back.keeps = (keep_a, red_back.keeps[1])
    qkv_peer, qkv_peer2 = flip(qkv_send, 0), flip(qkv_send2, 0)
    input_grad = grad_one + dot(qkv_grad, w_qkv, 1, 1)
    if kernels:
        red_in.step({})
        *qkv, sums = pl.pallas_call(
            functools.partial(qkv_kernel, dp),
            name="grad_w_qkv_out",
            cost_estimate=cost(3),
            out_shape=(
                shape_of(part_rows, width),
                shape_of(part_rows + SUM_ROWS, width),
                shape_of(part_rows, width),
                shape_of(part_rows, width),
                shape_of(SUM_ROWS, width, dtype=F32),
            ),
            grid=(1,),
            in_specs=[SMEM]
            + [pl.BlockSpec((rows, width), lambda i: (0, 0))] * 3
            + [acts_block(ctx_at)] * 2
            + [pl.BlockSpec((rows, 2 * qkv_block), lambda i: (0, 0))]
            + [pl.BlockSpec((loc + SUM_ROWS, 2 * qkv_block), lambda i: (0, 0))]
            + [pl.BlockSpec((rows - loc, 2 * qkv_block), lambda i: (0, 0))]
            + [pl.BlockSpec((rows, extra), lambda i: (0, out_at))] * 2
            + [pl.BlockSpec((SUM_ROWS, width), lambda i: (0, 0))],
            scratch_shapes=[pltpu.VMEM((width, 2 * rows), BF)] * 2
            + [pltpu.VMEM((width // 2, 2 * rows), BF)] * 4,
            compiler_params=params(20),
        )(
            jnp.concatenate([d, me]),
            flat,
            tok_prev,
            tok_next,
            acts,
            acts_peer,
            qkv_keep,
            qkv_peer,
            qkv_peer2,
            grads_keep,
            grads_peer,
            sums,
        )
        qkv[3], keep_b = lax.optimization_barrier((qkv[3], red_in.keeps[0]))
        red_in.keeps = (keep_b, red_in.keeps[1])
        red_qkv = Reduction("qkv", qkv, sums)
        units = (red_back, red_in, red_qkv)
        last = (
            ((ff // dp, small),),
            ((block_rows, wide),),
            ((block_rows, qkv_block), (block_rows, small), (ff,)) + ((width,),) * 8,
        )
        done = None
        for k in EVENTS if dp_bits == 3 else [0, 1, 2] * (dp_bits + 1):
            if units[k].at > dp_bits:
                continue
            outs = {"rows": block_rows // 2}
            if units[k].at == dp_bits:
                outs["last"] = last[k]
            if done is not None and done is not units[k]:
                wait_for(units[k], done)
            units[k].step(outs)
            done = units[k]
        g_back = red_back.result[0]
        g_in = red_in.result[0]
        g_qkv, g_out, b_in_g, *vectors = red_qkv.result
    else:

        def by_x(v, w):
            return v.reshape(v.shape[0], 2, w).transpose(1, 0, 2)

        def pile(a, b):
            return jnp.concatenate([a, b], axis=0)

        feeds = by_x(pile(feed_keep, acts_peer[:, base:]), small)
        g_back = plain_reduce(pile(acts[:, :ff], acts_peer[:, :ff]), feeds)
        grads = pile(grads_keep, grads_peer)
        lefts = pile(acts, acts_peer)
        g_in = plain_reduce(lefts[:, ff : ff + width], by_x(grads[:, : 2 * wide], wide))
        g_out = plain_reduce(lefts[:, ff + width : base], by_x(grads[:, 2 * wide :], small))
        other = jnp.where(me[0] % 2 == 0, tok_next, tok_prev)
        grads = by_x(pile(qkv_keep, pile(qkv_peer[:loc], qkv_peer2)), qkv_block)
        g_qkv = plain_reduce(pile(flat, other), grads)
        sums = plain_sum(sums, 0)
        b_in_g = sums[3:7].reshape(-1)
        vectors = [sums[i] for i in (0, 1, 2, 7, 8, 9, 10, 11)]
    b_back_g, gain2, shift2, b_out_g, gain1, shift1, b_q_g, b_v_g = vectors
    shape = (seqs, loc, width)
    return (
        result.reshape(shape),
        input_grad.reshape(shape).astype(BF),
        g_qkv,
        b_q_g,
        b_v_g,
        g_out,
        b_out_g,
        gain1,
        shift1,
        g_in,
        b_in_g,
        g_back,
        b_back_g,
        gain2,
        shift2,
    )


EVENTS = [0, 1, 0, 2, 1, 2, 0, 1, 2, 2]


def solution(mesh):
    row = P("dp", "seq", None)
    in_specs = (row, P("dp", None), P("dp", None)) + (P(),) * 13 + (row,)
    block = P("dp", "seq")
    out_specs = (row, row, block, P(), P(), block, P(), P(), P(), block, P(), block, P(), P(), P())
    return jax.shard_map(local, mesh=mesh, in_specs=in_specs, out_specs=out_specs, check_vma=False)
```

```python
import functools

import jax
import jax.numpy as jnp
from jax import lax
from jax.experimental import pallas as pl
from jax.experimental.pallas import tpu as pltpu
from jax.sharding import PartitionSpec as P

HEADS = 12
HDIM = 64
PAIR = 2 * HDIM
LN_EPS = 1e-12
FAR = -1e9
SUM_ROWS = 16
BOTH = ("dp", "seq")
BF = jnp.bfloat16
F32 = jnp.float32
HBM = pl.BlockSpec(memory_space=pltpu.HBM)
VMEM = pl.BlockSpec(memory_space=pltpu.VMEM)
SMEM = pl.BlockSpec(memory_space=pltpu.SMEM)


def dot(a, b, ca=1, cb=0):
    return lax.dot_general(a, b, (((ca,), (cb,)), ((), ())), preferred_element_type=F32)


def mean_of(v):
    return jnp.mean(v, axis=-1, keepdims=True)


def norm_parts(values):
    center = values - mean_of(values)
    inverse = lax.rsqrt(mean_of(center * center) + LN_EPS)
    return center * inverse, inverse


def norm_pull(upstream, normed, inverse, gain):
    scaled = upstream * gain
    return (scaled - mean_of(scaled) - normed * mean_of(scaled * normed)) * inverse


def col_sum(v):
    return jnp.sum(v, axis=0, keepdims=True)


def mask_of(me, groups, ids_ref, row, loc):
    own = pl.ds(pl.multiple_of(me * loc, loc), loc)
    seg_ref, pad_ref = ids_ref.at[0], ids_ref.at[1]
    seg_t = jnp.broadcast_to(seg_ref[row : row + 1, own].astype(F32), (loc, loc)).T
    pad_t = jnp.broadcast_to(pad_ref[row : row + 1, own].astype(F32), (loc, loc)).T
    eye = lax.broadcasted_iota(jnp.int32, (loc, loc), 0) == lax.broadcasted_iota(
        jnp.int32, (loc, loc), 1
    )
    keys, queries = [], []
    for block in range(3):
        at = me + block - 1
        out_of = jnp.where((at < 0) | (at >= groups), FAR, 0.0).astype(F32)
        at = jnp.clip(at, 0, groups - 1)
        span = pl.ds(pl.multiple_of(at * loc, loc), loc)
        seg_b = seg_ref[row : row + 1, span].astype(F32)
        pad_b = pad_ref[row : row + 1, span].astype(F32)
        same = seg_t == seg_b
        seen, seen_t = pad_b == 0.0, pad_t == 0.0
        if block == 1:
            seen, seen_t = seen | eye, seen_t | eye
        keys.append(jnp.where(same & seen, 0.0, FAR) + out_of)
        queries.append(jnp.where(same & seen_t, 0.0, FAR) + out_of)
    return jnp.concatenate(keys, axis=1), jnp.concatenate(queries, axis=1)


def split_pair(v, low):
    zero = jnp.zeros_like(v)
    return jnp.concatenate([jnp.where(low, v, zero), jnp.where(low, zero, v)], axis=0)


def join_pair(v, low):
    half = v.shape[0] // 2
    return jnp.where(low, v[:half], v[half:])


def own_kernel(
    groups, me_ref, ids_ref, tok_ref, vec_ref, wqkv_hbm, qkv_ref, mask_ref, mask_t_ref, wqkv, sems
):
    me = me_ref[0]
    rows, width = tok_ref.shape
    loc = rows // 2
    copies = []
    for part in range(3):
        cols = pl.ds(part * width, width)
        copies.append(pltpu.make_async_copy(wqkv_hbm.at[:, cols], wqkv.at[:, cols], sems.at[part]))
        copies[-1].start()
    for row in range(2):
        mask_ref[row], mask_t_ref[row] = mask_of(me, groups, ids_ref, row, loc)
    vec = vec_ref[...].reshape(1, -1)
    biases = (vec[:, :width], 0.0, vec[:, width : 2 * width])
    for part in range(3):
        copies[part].wait()
        cols = slice(part * width, (part + 1) * width)
        qkv_ref[:, cols] = (dot(tok_ref[...], wqkv[:, cols]) + biases[part]).astype(BF)


def forward_kernel(
    groups,
    me_ref,
    tok_prev,
    tok_next,
    tok_own,
    own_ref,
    mask_ref,
    vec_ref,
    vec2_ref,
    b_in_ref,
    wqkv,
    og_hbm,
    wout_hbm,
    win_hbm,
    wback_hbm,
    qkv_ref,
    acts_ref,
    feed_ref,
    slope_ref,
    lse_ref,
    normed_ref,
    inv_ref,
    gtwo_ref,
    out_ref,
    keep_ref,
    small_ref,
    wout,
    win,
    wback,
    ctx_ref,
    og_ref,
    sems,
):
    me = me_ref[0]
    rows, width = tok_own.shape
    loc = rows // 2
    ff = win.shape[1]
    pairs = ((wout_hbm, wout), (win_hbm, win), (wback_hbm, wback), (og_hbm, og_ref))
    copies = [pltpu.make_async_copy(a, b, sems.at[i]) for i, (a, b) in enumerate(pairs)]
    for copy in copies:
        copy.start()
    vec, vec2 = vec_ref[...].reshape(1, -1), vec2_ref[...].reshape(1, -1)
    b_query, b_value, b_out, gain1 = (vec[:, i * width : (i + 1) * width] for i in range(4))
    shift1, b_back, gain2, shift2 = (vec2[:, i * width : (i + 1) * width] for i in range(4))
    b_in = b_in_ref[...].reshape(1, -1)
    b_qkv = (b_query, 0.0, b_value)
    for part in range(3):
        cols = slice(part * width, (part + 1) * width)
        for block, tok in enumerate((tok_prev, tok_next)):
            qkv_ref[block, :, cols] = (dot(tok[...], wqkv[:, cols]) + b_qkv[part]).astype(BF)
    blocks = (qkv_ref.at[0], own_ref, qkv_ref.at[1])
    low = lax.broadcasted_iota(jnp.int32, (loc, PAIR), 1) < HDIM
    lanes = lax.broadcasted_iota(jnp.int32, (loc, 128), 1)

    def attend(p, totals):
        spans = [pl.ds(pl.multiple_of(p * PAIR + part * width, PAIR), PAIR) for part in range(3)]
        result = []
        for row in range(2):
            at = slice(row * loc, (row + 1) * loc)
            q2 = split_pair(own_ref[at, spans[0]], low) * jnp.asarray(HDIM**-0.5, BF)
            k3 = jnp.concatenate([b[at, spans[1]] for b in blocks], axis=0)
            v3 = jnp.concatenate([b[at, spans[2]] for b in blocks], axis=0)
            mask = mask_ref[row]
            scores = dot(q2, k3, 1, 1) + jnp.concatenate([mask, mask], axis=0)
            top = jnp.max(scores, axis=-1, keepdims=True)
            powers = jnp.exp(scores - top)
            total = jnp.sum(powers, axis=-1, keepdims=True)
            probs = (powers * (1.0 / total)).astype(BF)
            ctx_ref[at, pl.ds(pl.multiple_of(p * PAIR, PAIR), PAIR)] = join_pair(
                dot(probs, v3), low
            ).astype(BF)
            lse = top + jnp.log(total)
            old = totals[row]
            old = jnp.where(lanes == 2 * p, lse[:loc], old)
            result.append(jnp.where(lanes == 2 * p + 1, lse[loc:], old))
        return tuple(result)

    zero = jnp.zeros((loc, 128), F32)
    totals = lax.fori_loop(0, HEADS // 2, attend, (zero, zero), unroll=3)
    lse_ref[:loc, :] = totals[0]
    lse_ref[loc:, :] = totals[1]
    context = ctx_ref[...]
    acts_ref[:, ff + width : ff + 2 * width] = context
    copies[0].wait()
    branch = dot(context, wout[...]) + b_out
    normed, inverse = norm_parts(tok_own[...].astype(F32) + branch)
    normed_ref[...] = normed
    inv_ref[...] = inverse
    first = normed * gain1 + shift1
    first_low = first.astype(BF)
    acts_ref[:, ff : ff + width] = first_low
    copies[1].wait()
    copies[2].wait()
    feed = first + b_back
    for c in range(ff // width):
        cols = slice(c * width, (c + 1) * width)
        before = dot(first_low, win[:, cols]) + b_in[:, cols]
        cdf = 0.5 + 0.5 * lax.erf(before * (0.5**0.5))
        hidden = (before * cdf).astype(BF)
        acts_ref[:, cols] = hidden
        bell = jnp.exp(-0.5 * before * before) * (0.3989422804014327)
        slope_ref[:, cols] = (cdf + before * bell).astype(BF)
        feed = feed + dot(hidden, wback[cols, :])
    normed2, inverse2 = norm_parts(feed)
    out_ref[...] = (normed2 * gain2 + shift2).astype(BF)
    copies[3].wait()
    upstream = og_ref[...].astype(F32)
    grad_two = norm_pull(upstream, normed2, inverse2, gain2)
    gtwo_ref[...] = grad_two
    feed_grad = grad_two.astype(BF)
    feed_ref[...] = feed_grad
    small_ref[0:1, :] = col_sum(feed_grad.astype(F32))
    small_ref[1:2, :] = col_sum(upstream * normed2)
    small_ref[2:3, :] = col_sum(upstream)
    base = ff + 2 * width
    block = width // groups
    for s in range(groups):
        rel = s ^ me
        piece = feed_grad[:, s * block : (s + 1) * block]
        for i in range(groups // 2):

            @pl.when(rel == 2 * i)
            def _():
                keep_ref[:, i * block : (i + 1) * block] = piece

            @pl.when(rel == 2 * i + 1)
            def _():
                acts_ref[:, base + i * block : base + (i + 1) * block] = piece


def backward_kernel(
    groups,
    me_ref,
    feed_ref,
    slope_ref,
    gtwo_ref,
    normed_ref,
    inv_ref,
    acts_ref,
    lse_ref,
    vec_ref,
    wout,
    win,
    wback,
    keep_ref,
    send_ref,
    msg_ref,
    gone_ref,
    small_ref,
):
    me = me_ref[0]
    rows, width = feed_ref.shape
    ff = win.shape[1]
    block = ff // groups
    spans = [pl.ds(pl.multiple_of((i ^ me) * block, block), block) for i in range(groups)]
    feed_grad = feed_ref[...]
    first_grad = gtwo_ref[...]
    for i, span in enumerate(spans):
        s = i ^ me
        hidden_grad = dot(feed_grad, wback[span, :], 1, 1)
        before_grad = (hidden_grad * slope_ref[:, span].astype(F32)).astype(BF)
        small_ref[pl.ds(s, 1), :] = col_sum(before_grad.astype(F32))
        target = send_ref if i % 2 else keep_ref
        target[:, (i // 2) * block : (i // 2 + 1) * block] = before_grad
        first_grad = first_grad + dot(before_grad, win[:, span], 1, 1)
    normed = normed_ref[...]
    grad_one = norm_pull(first_grad, normed, inv_ref[...], vec_ref[3 * width :].reshape(1, -1))
    gone_ref[...] = grad_one
    branch_grad = grad_one.astype(BF)
    small_ref[4:5, :] = col_sum(branch_grad.astype(F32))
    small_ref[5:6, :] = col_sum(first_grad * normed)
    small_ref[6:7, :] = col_sum(first_grad)
    context_grad = dot(branch_grad, wout[...], 1, 1).astype(BF)
    msg_ref[:, :width] = context_grad
    product = context_grad.astype(F32) * acts_ref[:, ff + width : ff + 2 * width].astype(F32)
    lanes = lax.broadcasted_iota(jnp.int32, (rows, 128), 1)
    low = lanes < HDIM
    delta = jnp.zeros((rows, 128), F32)
    for p in range(HEADS // 2):
        tile = product[:, p * PAIR : (p + 1) * PAIR]
        both = jnp.sum(tile, axis=-1, keepdims=True)
        even = jnp.sum(jnp.where(low, tile, 0.0), axis=-1, keepdims=True)
        delta = jnp.where(lanes == 2 * p, even, delta)
        delta = jnp.where(lanes == 2 * p + 1, both - even, delta)
    packed = jnp.zeros((rows, 128), F32)
    shift = 0
    for value in (lse_ref[...], delta):
        for _ in range(3):
            term = value.astype(BF).astype(F32)
            packed = packed + (pltpu.roll(term, shift, 1) if shift else term)
            value = value - term
            shift += 16
    msg_ref[:, width:] = packed.astype(BF)
    base = 2 * block
    small = width // groups
    for s in range(groups):
        rel = s ^ me
        piece = branch_grad[:, s * small : (s + 1) * small]
        for i in range(groups // 2):

            @pl.when(rel == 2 * i)
            def _():
                keep_ref[:, base + i * small : base + (i + 1) * small] = piece

            @pl.when(rel == 2 * i + 1)
            def _():
                send_ref[:, base + i * small : base + (i + 1) * small] = piece


def attend_back_kernel(
    groups,
    me_ref,
    mask_ref,
    mask_t_ref,
    near_ref,
    own_ref,
    msg_prev,
    msg_own,
    msg_next,
    small1_ref,
    small2_ref,
    all_ref,
    keep_ref,
    send_ref,
    send2_ref,
    sums_ref,
    info_t_ref,
):
    me = me_ref[0]
    rows = msg_own.shape[0]
    width = own_ref.shape[1] // 3
    loc = rows // 2
    msgs = (msg_prev, msg_own, msg_next)
    blocks = (near_ref.at[0], own_ref, near_ref.at[1])
    own_info = []
    for row in range(2):
        at = slice(row * loc, (row + 1) * loc)
        for b in range(3):
            raw = msgs[b][at, width:].astype(F32)
            info = raw + pltpu.roll(raw, 112, 1) + pltpu.roll(raw, 96, 1)
            if b == 1:
                own_info.append(info)
            info_t_ref[row, b] = info.T
    low = lax.broadcasted_iota(jnp.int32, (loc, PAIR), 1) < HDIM
    lanes = lax.broadcasted_iota(jnp.int32, (loc, 128), 1)
    scale = jnp.asarray(HDIM**-0.5, BF)

    def column(info, lane):
        return jnp.sum(jnp.where(lanes == lane, info, 0.0), axis=-1, keepdims=True)

    def heads(p, carry):
        spans = [pl.ds(pl.multiple_of(p * PAIR + part * width, PAIR), PAIR) for part in range(3)]
        for row in range(2):
            at = slice(row * loc, (row + 1) * loc)
            info = own_info[row]
            lse2 = jnp.concatenate([column(info, 2 * p), column(info, 2 * p + 1)], axis=0)
            delta2 = jnp.concatenate([column(info, 48 + 2 * p), column(info, 49 + 2 * p)], axis=0)
            q3 = jnp.concatenate([b[at, spans[0]] for b in blocks], axis=0)
            k3 = jnp.concatenate([b[at, spans[1]] for b in blocks], axis=0)
            v3 = jnp.concatenate([b[at, spans[2]] for b in blocks], axis=0)
            u3 = jnp.concatenate([m[at, spans[0]] for m in msgs], axis=0)
            mask = mask_ref[row]
            scores = dot(split_pair(q3[loc : 2 * loc], low) * scale, k3, 1, 1)
            probs = jnp.exp(scores + jnp.concatenate([mask, mask], axis=0) - lse2)
            prob_grad = dot(split_pair(u3[loc : 2 * loc], low), v3, 1, 1)
            score_grad = (probs * (prob_grad - delta2)).astype(BF)
            query_grad = join_pair(dot(score_grad, k3), low) * HDIM**-0.5
            all_ref[at, spans[0]] = query_grad.astype(BF)

            def line(which):
                halves = []
                for h in range(2):
                    parts = [info_t_ref[row, b, pl.ds(which + 2 * p + h, 1), :] for b in range(3)]
                    halves.append(
                        jnp.broadcast_to(jnp.concatenate(parts, axis=1), (loc, 3 * loc))
                    )
                return jnp.concatenate(halves, axis=0)

            mask_t = mask_t_ref[row]
            scores_t = dot(split_pair(k3[loc : 2 * loc], low) * scale, q3, 1, 1)
            probs_t = jnp.exp(scores_t + jnp.concatenate([mask_t, mask_t], axis=0) - line(0))
            value_grad = join_pair(dot(probs_t.astype(BF), u3), low)
            prob_grad_t = dot(split_pair(v3[loc : 2 * loc], low), u3, 1, 1)
            score_grad_t = (probs_t * (prob_grad_t - line(48))).astype(BF)
            key_grad = join_pair(dot(score_grad_t, q3), low) * HDIM**-0.5
            all_ref[at, spans[1]] = key_grad.astype(BF)
            all_ref[at, spans[2]] = value_grad.astype(BF)
        return carry

    lax.fori_loop(0, HEADS // 2, heads, 0, unroll=3)
    value_at = 2 * width
    sums_ref[...] = jnp.concatenate(
        [
            small1_ref[...],
            small2_ref[...],
            col_sum(all_ref[:, :width].astype(F32)),
            col_sum(all_ref[:, value_at:].astype(F32)),
            jnp.zeros((SUM_ROWS - 12, width), F32),
        ],
        axis=0,
    )
    send_ref[loc:, :] = jnp.zeros((SUM_ROWS, send_ref.shape[1]), BF)
    pack_sums(sums_ref[...], send_ref, loc)
    block = 3 * width // groups
    for s in range(groups):
        rel = s ^ me
        piece = all_ref[:, s * block : (s + 1) * block]
        for i in range(groups // 2):

            @pl.when(rel == 2 * i)
            def _():
                keep_ref[:, i * block : (i + 1) * block] = piece

            @pl.when(rel == 2 * i + 1)
            def _():
                send_ref[:loc, i * block : (i + 1) * block] = piece[:loc]
                send2_ref[:, i * block : (i + 1) * block] = piece[loc:]


def pack_sums(value, ref, at):
    ref[at : at + SUM_ROWS, : value.shape[1]] = value.astype(BF)


def read_sums(ref, at, width):
    return ref[at : at + SUM_ROWS, :width].astype(F32)


def turn_rows(order, d, tmp_ref, turned_ref, block_rows, part):
    rows = block_rows // 2
    bits = [bit - 2 for bit in order if bit != 1]
    for j in range(1 << len(bits)):
        rel = sum(((j >> (len(bits) - 1 - k)) & 1) << bit for k, bit in enumerate(bits))
        start = pl.multiple_of((rel ^ d) * block_rows + part * rows, rows)
        turned_ref[j * rows : (j + 1) * rows, :] = tmp_ref[pl.ds(start, rows), :]


def orders_of(kind):
    first, second, *rest = HALVING[kind]
    return (first, second, *rest), (second, first, *rest)


def both_left(mine, peer):
    return jnp.concatenate([mine.T, peer.T], axis=1)


def by_halves(pieces, base, width):
    return [
        jnp.concatenate([r[:, base + x * width : base + (x + 1) * width] for r in pieces], axis=0)
        for x in range(2)
    ]


def put(result, order, x, keep, send):
    blocks = 1 << (len(order) - 1)
    rows = result.shape[0] // blocks
    k = order.index(1)
    run = blocks >> k
    for i in range(1 << k):
        at = (2 * i + x) * run
        ref, at = (keep, at) if at < blocks else (send, at - blocks)
        ref[at * rows : (at + run) * rows] = result[i * run * rows : (i + 1) * run * rows]


def in_kernel(dp, d_ref, acts, acts_peer, mine, peer, keep0, send0, keep1, send1, tmp, *turned):
    width = acts.shape[1]
    tmp[...] = both_left(acts[...], acts_peer[...])
    wide = (mine.shape[1] - width // 2) // 2
    rights = by_halves((mine, peer), 0, wide)
    outs = ((keep0, send0), (keep1, send1))
    for part, order in enumerate(orders_of("in")):
        turn_rows(order, d_ref[0], tmp, turned[part], width // dp, part)
        for x in range(2):
            put(dot(turned[part][...], rights[x]).astype(BF), order, x, *outs[part])


def qkv_kernel(
    dp,
    ids_ref,
    tok,
    tok_prev,
    tok_next,
    ctx,
    ctx_peer,
    mine,
    peer,
    peer2,
    out_mine,
    out_peer,
    sums_ref,
    keep0,
    send0,
    keep1,
    send1,
    total_ref,
    tmp,
    tmp2,
    *turned,
):
    rows, width = tok.shape
    d = ids_ref[0]
    other = jnp.where(ids_ref[1] % 2 == 0, tok_next[...], tok_prev[...])
    tmp[...] = both_left(tok[...], other)
    tmp2[...] = both_left(ctx[...], ctx_peer[...])
    half = peer2.shape[0]
    rights = by_halves((mine, peer.at[:half], peer2), 0, mine.shape[1] // 2)
    outs = by_halves((out_mine, out_peer), 0, out_mine.shape[1] // 2)
    refs = ((keep0, send0), (keep1, send1))
    for part, order in enumerate(orders_of("qkv")):
        turn_rows(order, d, tmp, turned[part], width // dp, part)
        turn_rows(order, d, tmp2, turned[2 + part], width // dp, part)
        for x in range(2):
            result = jnp.concatenate(
                [dot(turned[part][...], rights[x]), dot(turned[2 + part][...], outs[x])], axis=1
            ).astype(BF)
            put(result, order, x, *refs[part])
    total = sums_ref[...] + read_sums(peer, half, width)
    total_ref[...] = total
    pack_sums(total, send0, keep0.shape[0])


def back_kernel(dp, d_ref, hid, hid_peer, feed, feed_peer, keep0, send0, keep1, send1):
    d = d_ref[0]
    chunk = hid.shape[1] // dp
    side = feed.shape[1] // 2
    rows = side // 4
    turned = [feed[...].T, feed_peer[...].T]
    orders = orders_of("back")
    for rel in range(dp):
        span = pl.ds(pl.multiple_of((rel ^ d) * chunk, chunk), chunk)
        result = (dot(turned[0], hid[:, span]) + dot(turned[1], hid_peer[:, span])).astype(BF)
        for x in range(2):
            bits = 2 * x + 4 * rel
            for part, refs in enumerate(((keep0, send0), (keep1, send1))):
                at = 0
                for bit in orders[part]:
                    at = 2 * at + ((bits >> bit) & 1)
                ref, at = refs[at // dp], at % dp
                for h in range(2):
                    start = x * side + h * 2 * rows + part * rows
                    ref[at * rows : (at + 1) * rows, h * chunk : (h + 1) * chunk] = result[
                        start : start + rows
                    ]


def total_of(keep, got):
    return keep[...].astype(F32) + got[: keep.shape[0]].astype(F32)


def step_sums(sums_ref, got, at, total_ref, send, send_at):
    total = sums_ref[...] + read_sums(got, at, sums_ref.shape[1])
    total_ref[...] = total
    if send is not None:
        pack_sums(total, send, send_at)


def first_step(keep0, got0, keep1, got1, *refs):
    if len(refs) == 6:
        sums_ref, new0, send0, new1, send1, total_ref = refs
        step_sums(sums_ref, got0, keep0.shape[0], total_ref, send0, keep0.shape[0] // 2)
    else:
        new0, send0, new1, send1 = refs
    half = keep0.shape[0] // 2
    for keep, got, new, send in ((keep0, got0, new0, send0), (keep1, got1, new1, send1)):
        total = total_of(keep, got).astype(BF)
        new[...] = total[:half]
        send[:half] = total[half:]


def second_step(rows, keep0, got0, keep1, got1, *refs):
    if len(refs) == 4:
        sums_ref, new, send, total_ref = refs
        step_sums(sums_ref, got0, keep0.shape[0], total_ref, send, new.shape[0])
    else:
        new, send = refs
    half = keep0.shape[0] // 2
    for part, (keep, got) in enumerate(((keep0, got0), (keep1, got1))):
        total = total_of(keep, got).astype(BF)
        for b in range(half // rows):
            at = (2 * b + part) * rows
            new[at : at + rows] = total[b * rows : (b + 1) * rows]
            send[at : at + rows] = total[half + b * rows : half + (b + 1) * rows]


def third_step(keep, got, *refs):
    if len(refs) == 4:
        sums_ref, new, send, total_ref = refs
        step_sums(sums_ref, got, keep.shape[0], total_ref, send, new.shape[0])
    else:
        new, send = refs
    half = keep.shape[0] // 2
    total = total_of(keep, got).astype(BF)
    new[...] = total[:half]
    send[:half] = total[half:]


def last_step(kind, keep, got, *refs):
    total = total_of(keep, got)
    if kind == "back":
        chunk = total.shape[1] // 2
        refs[0][...] = jnp.concatenate([total[:, :chunk].T, total[:, chunk:].T], axis=1)
    elif kind == "in":
        refs[0][...] = total
    else:
        sums_ref, qkv_ref, out_ref, inner_ref, *vectors = refs
        qkv_ref[...] = total[:, : qkv_ref.shape[1]]
        out_ref[...] = total[:, qkv_ref.shape[1] :]
        width = sums_ref.shape[1]
        sums = sums_ref[...] + read_sums(got, keep.shape[0], width)
        for i in range(4):
            inner_ref[i * width : (i + 1) * width] = sums[3 + i]
        for row, ref in zip((0, 1, 2, 7, 8, 9, 10, 11), vectors):
            ref[...] = sums[row]


HALVING = {"back": (2, 3, 1, 4), "in": (1, 3, 2, 4), "qkv": (1, 3, 2, 4)}


def flip(value, bit):
    count = lax.axis_size("dp") * lax.axis_size("seq")
    return lax.ppermute(value, BOTH, [(i, i ^ (1 << bit)) for i in range(count)])


class Reduction:
    def __init__(self, kind, parts, sums=None):
        self.kind, self.keeps, self.sums = kind, parts[0::2], sums
        self.at, self.result = 0, None
        self.gots = tuple(flip(v, b) for v, b in zip(parts[1::2], HALVING[kind]))

    def step(self, outs):
        extra = 0 if self.sums is None else SUM_ROWS
        total = self.keeps[0].shape[0]
        width = self.keeps[0].shape[1]
        half = total // 2
        operands = [v for pair in zip(self.keeps, self.gots) for v in pair]
        sums = () if self.sums is None else (shape_of(SUM_ROWS, width, dtype=F32),)
        if self.at == 0:
            kernel = first_step
            shapes = (half, half + extra, half, half)
        elif self.at == 1:
            kernel = functools.partial(second_step, outs["rows"])
            shapes = (total, total + extra)
        else:
            kernel, shapes = third_step, (half, half + extra)
        shapes = tuple(shape_of(n, width) for n in shapes) + sums
        last = self.at > 1 and "last" in outs
        if last:
            kernel = functools.partial(last_step, self.kind)
            shapes = tuple(shape_of(*dims, dtype=F32) for dims in outs["last"])
        if self.sums is not None:
            operands.append(self.sums)
        result = pl.pallas_call(
            kernel,
            name=f"add_{self.kind}_{self.at}",
            cost_estimate=cost(1),
            out_shape=shapes,
            in_specs=[VMEM] * len(operands),
            out_specs=(VMEM,) * len(shapes),
            compiler_params=params(12),
        )(*operands)
        self.at += 1
        if last:
            self.result = result
            return
        if self.sums is not None:
            self.sums = result[-1]
        self.keeps = result[0 : len(shapes) - len(sums) : 2]
        sends = result[1 : len(shapes) - len(sums) : 2]
        bits = HALVING[self.kind]
        bits = bits[1::-1] if self.at == 1 else bits[self.at :]
        self.gots = tuple(flip(v, b) for v, b in zip(sends, bits))


def wait_for(unit, done):
    got, *rest = unit.gots
    if done.result is None:
        keep, *others = done.keeps
        got, keep = lax.optimization_barrier((got, keep))
        done.keeps = (keep, *others)
    else:
        first, *others = done.result
        got, first = lax.optimization_barrier((got, first))
        done.result = (first, *others)
    unit.gots = (got, *rest)


def plain_reduce(left, right):
    dp = lax.axis_size("dp")
    part = jnp.einsum("tk,xtw->xkw", left, right, preferred_element_type=F32).astype(BF)
    part = part[0].astype(F32) + flip(part[1], 1).astype(F32)
    part = part.reshape(dp, left.shape[1] // dp, right.shape[2]).astype(BF)
    part = jnp.take(part, jnp.arange(dp) ^ lax.axis_index("dp"), axis=0)
    for bit in reversed(range(dp.bit_length() - 1)):
        half = part.shape[0] // 2
        part = part[:half].astype(F32) + flip(part[half:], 2 + bit).astype(F32)
        part = part.astype(BF) if bit else part
    return part[0]


def plain_sum(value, low):
    count = lax.axis_size("dp") * lax.axis_size("seq")
    for bit in range(low, count.bit_length() - 1):
        value = value + flip(value, bit)
    return value


def shape_of(*dims, dtype=BF):
    return jax.ShapeDtypeStruct(dims, dtype)


def cost(us):
    return pl.CostEstimate(flops=int(us * 1e6), bytes_accessed=int(us * 1e4), transcendentals=0)


def params(mib):
    return pltpu.CompilerParams(vmem_limit_bytes=mib << 20)


def local(
    tokens,
    segment_ids,
    padding,
    w_qkv,
    b_query,
    b_value,
    w_out,
    b_out,
    ln1_gain,
    ln1_bias,
    w_in,
    b_in,
    w_back,
    b_back,
    ln2_gain,
    ln2_bias,
    out_grad,
):
    seqs, loc, width = tokens.shape
    groups, dp = lax.axis_size("seq"), lax.axis_size("dp")
    dp_bits = dp.bit_length() - 1
    ff = w_in.shape[1]
    rows = seqs * loc
    me = lax.axis_index("seq").astype(jnp.int32).reshape(1)
    d = lax.axis_index("dp").astype(jnp.int32).reshape(1)
    up = [(i, i + 1) for i in range(groups - 1)]
    down = [(i + 1, i) for i in range(groups - 1)]

    def around(value):
        return lax.ppermute(value, "seq", up), lax.ppermute(value, "seq", down)

    flat = tokens.reshape(rows, width)
    tok_prev, tok_next = around(flat)
    vec1 = jnp.concatenate([b_query, b_value, b_out, ln1_gain])
    vec2 = jnp.concatenate([ln1_bias, b_back, ln2_gain, ln2_bias])
    ids = jnp.stack([segment_ids, padding])
    own_qkv, mask, mask_t, wqkv = pl.pallas_call(
        functools.partial(own_kernel, groups),
        name="own_projections",
        cost_estimate=cost(4),
        out_shape=(
            shape_of(rows, 3 * width),
            shape_of(seqs, loc, 3 * loc, dtype=F32),
            shape_of(seqs, loc, 3 * loc, dtype=F32),
            shape_of(*w_qkv.shape),
        ),
        in_specs=[SMEM] + [VMEM] * 3 + [HBM],
        out_specs=(VMEM,) * 4,
        scratch_shapes=[pltpu.SemaphoreType.DMA((3,))],
        compiler_params=params(48),
    )(me, ids, flat, vec1, w_qkv)
    extra = width // groups * 2
    acts_width = ff + 2 * width + extra
    near_qkv, acts, feed_grad, slope, lse, normed, inverse, grad_two, result, feed_keep, small1, *weights = (
        pl.pallas_call(
            functools.partial(forward_kernel, groups),
            name="layer_forward",
            cost_estimate=cost(16),
            out_shape=(
                shape_of(2, rows, 3 * width),
                shape_of(rows, acts_width),
                shape_of(rows, width),
                shape_of(rows, ff),
                shape_of(rows, 128, dtype=F32),
                shape_of(rows, width, dtype=F32),
                shape_of(rows, 1, dtype=F32),
                shape_of(rows, width, dtype=F32),
                shape_of(rows, width),
                shape_of(rows, extra),
                shape_of(3, width, dtype=F32),
                *(shape_of(*w.shape) for w in (w_out, w_in, w_back)),
            ),
            in_specs=[SMEM] + [VMEM] * 9 + [HBM] * 4,
            out_specs=(VMEM,) * 14,
            scratch_shapes=[
                pltpu.VMEM((rows, width), BF),
                pltpu.VMEM((rows, width), BF),
                pltpu.SemaphoreType.DMA((4,)),
            ],
            compiler_params=params(24),
        )(
            me,
            tok_prev,
            tok_next,
            flat,
            own_qkv,
            mask,
            vec1,
            vec2,
            b_in,
            wqkv,
            out_grad.reshape(rows, width),
            w_out,
            w_in,
            w_back,
        )
    )
    acts_peer = flip(acts, 0)

    side = 2 * (ff // groups) + extra
    grads_keep, grads_send, msg, grad_one, small2 = pl.pallas_call(
        functools.partial(backward_kernel, groups),
        name="layer_backward",
            cost_estimate=cost(8),
        out_shape=(
            shape_of(rows, side),
            shape_of(rows, side),
            shape_of(rows, width + 128),
            shape_of(rows, width, dtype=F32),
            shape_of(7, width, dtype=F32),
        ),
        in_specs=[SMEM] + [VMEM] * 11,
        out_specs=(VMEM,) * 5,
        compiler_params=params(12),
    )(me, feed_grad, slope, grad_two, normed, inverse, acts, lse, vec1, *weights)
    msg_prev, msg_next = around(msg)
    grads_peer = flip(grads_send, 0)

    kernels = (width // dp) % 32 == 0 and (ff // dp) % 128 == 0 and dp == 8
    small = width // groups
    wide = ff // groups
    qkv_block = 3 * width // groups
    block_rows = width // dp
    part_rows = dp * block_rows // 2
    base = ff + 2 * width

    def acts_block(i):
        return pl.BlockSpec((rows, width), lambda g: (0, i))

    first_at, ctx_at = ff // width, ff // width + 1
    out_at = 2 * wide // extra
    if kernels:
        back = pl.pallas_call(
            functools.partial(back_kernel, dp),
            name="grad_w_back",
            cost_estimate=cost(3),
            grid=(1,),
            out_shape=(shape_of(part_rows, width),) * 4,
            in_specs=[
                SMEM,
                pl.BlockSpec((rows, ff), lambda i: (0, 0)),
                pl.BlockSpec((rows, ff), lambda i: (0, 0)),
                pl.BlockSpec((rows, extra), lambda i: (0, 0)),
                pl.BlockSpec((rows, extra), lambda i: (0, base // extra)),
            ],
            compiler_params=params(16),
        )(d, acts, acts_peer, feed_keep, acts_peer)
        grads_keep, msg_prev, msg_next = lax.optimization_barrier((grads_keep, msg_prev, msg_next))
        whole = pl.BlockSpec((rows, side), lambda g: (0, 0))
        inner = pl.pallas_call(
            functools.partial(in_kernel, dp),
            name="grad_w_in",
            cost_estimate=cost(4),
            grid=(1,),
            out_shape=(shape_of(part_rows, wide),) * 4,
            in_specs=[SMEM, acts_block(first_at), acts_block(first_at), whole, whole],
            scratch_shapes=[pltpu.VMEM((width, 2 * rows), BF)]
            + [pltpu.VMEM((width // 2, 2 * rows), BF)] * 2,
            compiler_params=params(16),
        )(d, acts, acts_peer, grads_keep, grads_peer)
        red_back = Reduction("back", back)
        red_in = Reduction("in", inner)
        msg_prev, msg_next, keep_a, keep_b = lax.optimization_barrier(
            (msg_prev, msg_next, red_back.keeps[0], red_in.keeps[0])
        )
        red_back.keeps = (keep_a, red_back.keeps[1])
        red_in.keeps = (keep_b, red_in.keeps[1])

    qkv_grad, qkv_keep, qkv_send, qkv_send2, sums = pl.pallas_call(
        functools.partial(attend_back_kernel, groups),
        name="attend_backward",
        cost_estimate=cost(11),
        out_shape=(
            shape_of(rows, 3 * width),
            shape_of(rows, 2 * qkv_block),
            shape_of(loc + SUM_ROWS, 2 * qkv_block),
            shape_of(rows - loc, 2 * qkv_block),
            shape_of(SUM_ROWS, width, dtype=F32),
        ),
        in_specs=[SMEM] + [VMEM] * 9,
        out_specs=(VMEM,) * 5,
        scratch_shapes=[pltpu.VMEM((2, 3, 128, loc), F32)],
        compiler_params=params(16),
    )(me, mask, mask_t, near_qkv, own_qkv, msg_prev, msg, msg_next, small1, small2)
    if kernels:
        red_back.step({})
        qkv_send, keep_a = lax.optimization_barrier((qkv_send, red_back.keeps[0]))
        red_back.keeps = (keep_a, red_back.keeps[1])
    qkv_peer, qkv_peer2 = flip(qkv_send, 0), flip(qkv_send2, 0)
    input_grad = grad_one + dot(qkv_grad, w_qkv, 1, 1)
    if kernels:
        red_in.step({})
        *qkv, sums = pl.pallas_call(
            functools.partial(qkv_kernel, dp),
            name="grad_w_qkv_out",
            cost_estimate=cost(3),
            out_shape=(
                shape_of(part_rows, width),
                shape_of(part_rows + SUM_ROWS, width),
                shape_of(part_rows, width),
                shape_of(part_rows, width),
                shape_of(SUM_ROWS, width, dtype=F32),
            ),
            grid=(1,),
            in_specs=[SMEM]
            + [pl.BlockSpec((rows, width), lambda i: (0, 0))] * 3
            + [acts_block(ctx_at)] * 2
            + [pl.BlockSpec((rows, 2 * qkv_block), lambda i: (0, 0))]
            + [pl.BlockSpec((loc + SUM_ROWS, 2 * qkv_block), lambda i: (0, 0))]
            + [pl.BlockSpec((rows - loc, 2 * qkv_block), lambda i: (0, 0))]
            + [pl.BlockSpec((rows, extra), lambda i: (0, out_at))] * 2
            + [pl.BlockSpec((SUM_ROWS, width), lambda i: (0, 0))],
            scratch_shapes=[pltpu.VMEM((width, 2 * rows), BF)] * 2
            + [pltpu.VMEM((width // 2, 2 * rows), BF)] * 4,
            compiler_params=params(20),
        )(
            jnp.concatenate([d, me]),
            flat,
            tok_prev,
            tok_next,
            acts,
            acts_peer,
            qkv_keep,
            qkv_peer,
            qkv_peer2,
            grads_keep,
            grads_peer,
            sums,
        )
        qkv[3], keep_b = lax.optimization_barrier((qkv[3], red_in.keeps[0]))
        red_in.keeps = (keep_b, red_in.keeps[1])
        red_qkv = Reduction("qkv", qkv, sums)
        units = (red_back, red_in, red_qkv)
        last = (
            ((ff // dp, small),),
            ((block_rows, wide),),
            ((block_rows, qkv_block), (block_rows, small), (ff,)) + ((width,),) * 8,
        )
        done = None
        for k in EVENTS if dp_bits == 3 else [0, 1, 2] * (dp_bits + 1):
            if units[k].at > dp_bits:
                continue
            outs = {"rows": block_rows // 2}
            if units[k].at == dp_bits:
                outs["last"] = last[k]
            if done is not None and done is not units[k]:
                wait_for(units[k], done)
            units[k].step(outs)
            done = units[k]
        g_back = red_back.result[0]
        g_in = red_in.result[0]
        g_qkv, g_out, b_in_g, *vectors = red_qkv.result
    else:

        def by_x(v, w):
            return v.reshape(v.shape[0], 2, w).transpose(1, 0, 2)

        def pile(a, b):
            return jnp.concatenate([a, b], axis=0)

        feeds = by_x(pile(feed_keep, acts_peer[:, base:]), small)
        g_back = plain_reduce(pile(acts[:, :ff], acts_peer[:, :ff]), feeds)
        grads = pile(grads_keep, grads_peer)
        lefts = pile(acts, acts_peer)
        g_in = plain_reduce(lefts[:, ff : ff + width], by_x(grads[:, : 2 * wide], wide))
        g_out = plain_reduce(lefts[:, ff + width : base], by_x(grads[:, 2 * wide :], small))
        other = jnp.where(me[0] % 2 == 0, tok_next, tok_prev)
        grads = by_x(pile(qkv_keep, pile(qkv_peer[:loc], qkv_peer2)), qkv_block)
        g_qkv = plain_reduce(pile(flat, other), grads)
        sums = plain_sum(sums, 0)
        b_in_g = sums[3:7].reshape(-1)
        vectors = [sums[i] for i in (0, 1, 2, 7, 8, 9, 10, 11)]
    b_back_g, gain2, shift2, b_out_g, gain1, shift1, b_q_g, b_v_g = vectors
    shape = (seqs, loc, width)
    return (
        result.reshape(shape),
        input_grad.reshape(shape).astype(BF),
        g_qkv,
        b_q_g,
        b_v_g,
        g_out,
        b_out_g,
        gain1,
        shift1,
        g_in,
        b_in_g,
        g_back,
        b_back_g,
        gain2,
        shift2,
    )


EVENTS = [0, 1, 0, 2, 1, 2, 0, 2, 1, 2]


def solution(mesh):
    row = P("dp", "seq", None)
    in_specs = (row, P("dp", None), P("dp", None)) + (P(),) * 13 + (row,)
    block = P("dp", "seq")
    out_specs = (row, row, block, P(), P(), block, P(), P(), P(), block, P(), block, P(), P(), P())
    return jax.shard_map(local, mesh=mesh, in_specs=in_specs, out_specs=out_specs, check_vma=False)
```
